512 devices in a mesh: dp: 2 (over y_hi), chan: 16 (over z), ctx: 16 (over x, y_lo, core).
Axes of the slice: x: 4, y: 4 (y_hi: 2, y_lo: 2; y = y_hi * 2 + y_lo), z: 16, core: 2. Of those that a mesh axis runs over, the one named last changes fastest.
Arguments:
- values: bfloat16 [2, 8192, 4096], P('dp', 'ctx', 'chan'), may hold values from -6 to 6
- gate_first: bfloat16 [2, 8192, 4096], P('dp', 'ctx', 'chan'), may hold values from -6 to 6
- gate_second: bfloat16 [2, 8192, 4096], P('dp', 'ctx', 'chan'), may hold values from -6 to 6
- filter_features: bfloat16 [64, 8192], P(None, 'ctx'), may hold values from -4 to 4
- filter_weight: bfloat16 [64, 4096], P(None, 'chan'), may hold values from -0.75 to 0.75
- decay_rate: float32 [4096], P('chan'), may hold values from 0.5 to 8
- skip_bias: float32 [4096], P('chan'), may hold values from -4 to 4
- output_grad: bfloat16 [2, 8192, 4096], P('dp', 'ctx', 'chan'), may hold values from -6 to 6
Outputs:
- output: bfloat16 [2, 8192, 4096], P('dp', 'ctx', 'chan')
- values_grad: bfloat16 [2, 8192, 4096], P('dp', 'ctx', 'chan')
- first_grad: bfloat16 [2, 8192, 4096], P('dp', 'ctx', 'chan')
- second_grad: bfloat16 [2, 8192, 4096], P('dp', 'ctx', 'chan')
- weight_grad: float32 [64, 4096], P(None, 'chan')
- feature_grad: float32 [64, 8192], P(None, 'ctx')
The draws below stay inside these ranges and needn't reach their ends.
All inputs are finite; a program needn't handle non-finite values.
Results may differ from the reference program's by a relative error of at most 0.03.
Values may be sent and summed in bfloat16 or wider, within the bound.
No kernel may reach another device: no remote copies, remote signals or barrier semaphores. Data moves between devices by JAX's collectives and lax.ppermute only.
A program may use at most 64 MiB of HBM per device.

```python
import math
from functools import partial
import jax
import jax.numpy as jnp
from jax import lax

CH_DEV = 256
ORDER = 64
R2 = 256
CHAN = 4096
SEQS = 2
LEN = 8192
NFFT = 16384
R1 = 64


def level_of(rng, extent, pieces, low, high):
    def one(position, blocks):
        draws = jax.random.uniform(jax.random.fold_in(jax.random.fold_in(rng, 6), position), (blocks,), jnp.float32, low / len(pieces), high / len(pieces))
        return jnp.repeat(jnp.exp(draws), extent[position] // blocks).reshape((-1,) + (1,) * (len(extent) - position - 1))

    factor_of = one(*pieces[0])
    for cut in pieces[1:]:
        factor_of = factor_of * one(*cut)
    return factor_of


def normal_values(own_key, extent, spread, limit, pieces=(), kind=jnp.bfloat16):
    values = jax.random.normal(own_key, extent, jnp.float32) * spread
    if len(pieces) > 0:
        values = level_of(own_key, extent, pieces, -0.22, 0.18) * values
    return jnp.clip(values, min=-limit, max=limit).astype(kind)


def setup_inputs(seed: int = 0) -> dict:
    key_list = jax.random.split(jax.random.key(seed), 9)
    values = normal_values(key_list[0], (SEQS, LEN, CHAN), 1.0, 6.0, ((0, 2), (1, 16), (2, 16)))
    gate_first = normal_values(key_list[1], (SEQS, LEN, CHAN), 1.0, 6.0, ((0, 2), (1, 16), (2, 16)))
    gate_second = normal_values(key_list[2], (SEQS, LEN, CHAN), 1.0, 6.0, ((0, 2), (1, 16), (2, 16)))
    filter_features = normal_values(key_list[3], (ORDER, LEN), 1.0, 4.0, ((1, 16),))
    filter_weight = normal_values(key_list[4], (ORDER, CHAN), ORDER ** -0.5, 0.75, ((1, 16),))
    decay_rate = jnp.clip(jnp.exp(math.log(8.0) - 2.7725887 * jax.random.uniform(key_list[5], (CHAN,), jnp.float32) ** level_of(key_list[5], (CHAN,), ((0, 16),), -0.2, 0.2)), 0.5, 8.0)
    skip_bias = normal_values(key_list[6], (CHAN,), 1.0, 4.0, ((0, 16),), jnp.float32)
    output_grad = normal_values(key_list[7], (SEQS, LEN, CHAN), 1.0, 6.0, ((0, 2), (1, 16), (2, 16)))
    return dict(values=values, gate_first=gate_first, gate_second=gate_second, filter_features=filter_features, filter_weight=filter_weight, decay_rate=decay_rate, skip_bias=skip_bias, output_grad=output_grad)


def to_wide(source_array):
    return lax.optimization_barrier(source_array).astype(jnp.float32)

def phases(left_index, right_index, period):
    product = left_index[:, None] * right_index[None, :] % period
    return 2.0 * math.pi / period * product.astype(jnp.float32)

def forward_spectra(signal):
    item_count = signal.shape[0]
    channels = signal.shape[-1]
    half_rows = R1 // 2
    grid_values = to_wide(signal).reshape(item_count, half_rows, R2, channels)
    freq_one = jnp.arange(R1, dtype=jnp.int32)
    angles_one = phases(freq_one, jnp.arange(half_rows, dtype=jnp.int32), R1)
    matrix_one = to_wide(jnp.concatenate([jnp.cos(angles_one), -jnp.sin(angles_one)], axis=0).astype(jnp.bfloat16))
    section_one = jnp.einsum('kn,snjc->skjc', matrix_one, grid_values, precision=lax.Precision.HIGHEST)
    real_part = section_one[:, :R1]
    imag_part = section_one[:, R1:]
    freq_two = jnp.arange(R2, dtype=jnp.int32)
    twiddle = phases(freq_one, freq_two, NFFT)[None, :, :, None]
    cosines = jnp.cos(twiddle)
    sines = jnp.sin(twiddle)
    section_out = jnp.stack([real_part * cosines + imag_part * sines, imag_part * cosines - real_part * sines], axis=1)
    section_out = to_wide(section_out.astype(jnp.bfloat16))
    angles_two = phases(freq_two, freq_two, R2)
    basis_two = to_wide(jnp.stack([jnp.cos(angles_two), jnp.sin(angles_two)]).astype(jnp.bfloat16))
    products_two = jnp.einsum('tmj,srkjc->strkmc', basis_two, section_out, precision=lax.Precision.HIGHEST)
    spectra = jnp.stack([products_two[:, 0, 0] + products_two[:, 1, 1], products_two[:, 0, 1] - products_two[:, 1, 0]], axis=1)
    return spectra.astype(jnp.bfloat16)

def inverse_signal(spectrum, factor):
    item_count = spectrum.shape[0]
    channels = spectrum.shape[-1]
    half_rows = R1 // 2
    freq_two = jnp.arange(R2, dtype=jnp.int32)
    angles_two = phases(freq_two, freq_two, R2)
    basis_two = to_wide(jnp.stack([jnp.cos(angles_two), jnp.sin(angles_two)]).astype(jnp.bfloat16))
    products_two = jnp.einsum('tmj,srkjc->strkmc', basis_two, to_wide(spectrum), precision=lax.Precision.HIGHEST)
    back_real = products_two[:, 0, 0] - products_two[:, 1, 1]
    back_imag = products_two[:, 0, 1] + products_two[:, 1, 0]
    freq_one = jnp.arange(R1, dtype=jnp.int32)
    twiddle = phases(freq_one, freq_two, NFFT)[None, :, :, None]
    cosines = jnp.cos(twiddle)
    sines = jnp.sin(twiddle)
    section_out = jnp.stack([back_real * cosines - back_imag * sines, back_imag * cosines + back_real * sines], axis=1)
    section_out = to_wide(section_out.astype(jnp.bfloat16)).reshape(item_count, 2 * R1, R2, channels)
    angles_one = phases(jnp.arange(half_rows, dtype=jnp.int32), freq_one, R1)
    matrix_one = to_wide(jnp.concatenate([jnp.cos(angles_one), -jnp.sin(angles_one)], axis=1).astype(jnp.bfloat16))
    signal = jnp.einsum('nk,skjc->snjc', matrix_one, section_out, precision=lax.Precision.HIGHEST) * factor
    return signal.astype(jnp.bfloat16).reshape(item_count, LEN, channels)

def complex_product(left_spec, right_spec, conjugate):
    left_real = to_wide(left_spec[:, 0])
    left_imag = to_wide(left_spec[:, 1])
    right_real = to_wide(right_spec[:, 0])
    right_imag = to_wide(right_spec[:, 1])
    if conjugate:
        real_out = left_real * right_real + left_imag * right_imag
        imag_out = left_imag * right_real - left_real * right_imag
    else:
        real_out = left_real * right_real - left_imag * right_imag
        imag_out = left_real * right_imag + left_imag * right_real
    return jnp.stack([real_out, imag_out], axis=1).astype(jnp.bfloat16)

def one_block(filter_features, block):
    values, gate_first, gate_second, output_grad, filter_weight, decay_rate, skip_bias = block
    batch_size = values.shape[0]
    positions = jnp.arange(LEN, dtype=jnp.int32).astype(jnp.float32) / LEN
    window = jnp.exp(-decay_rate[None, :] * positions[:, None])
    raw_kernel = jnp.dot(filter_features.T, filter_weight, preferred_element_type=jnp.float32)
    kernel = (raw_kernel * window).astype(jnp.bfloat16)
    mixed_in = (values.astype(jnp.float32) * gate_first.astype(jnp.float32)).astype(jnp.bfloat16)
    scaled_grad = (output_grad.astype(jnp.float32) * gate_second.astype(jnp.float32)).astype(jnp.bfloat16)
    spectra = forward_spectra(jnp.concatenate([mixed_in, kernel[None], scaled_grad], axis=0))
    mixed_spec = spectra[:batch_size]
    kernel_spec = jnp.broadcast_to(spectra[batch_size:batch_size + 1], mixed_spec.shape)
    grad_spec = spectra[batch_size + 1:]
    products = jnp.concatenate([complex_product(mixed_spec, kernel_spec, False), complex_product(grad_spec, kernel_spec, True), complex_product(grad_spec, mixed_spec, True)], axis=0)
    signals = inverse_signal(products, 1.0 / (NFFT * math.sqrt(LEN)))
    conv = to_wide(signals[:batch_size])
    grad_conv = to_wide(signals[batch_size:2 * batch_size])
    filter_conv = to_wide(signals[2 * batch_size:])
    total = conv + skip_bias * to_wide(mixed_in)
    output = (gate_second.astype(jnp.float32) * total).astype(jnp.bfloat16)
    second_grad = (output_grad.astype(jnp.float32) * total).astype(jnp.bfloat16)
    delta = grad_conv + skip_bias * to_wide(scaled_grad)
    values_grad = (delta * gate_first.astype(jnp.float32)).astype(jnp.bfloat16)
    first_grad = (delta * values.astype(jnp.float32)).astype(jnp.bfloat16)
    kernel_grad = to_wide((filter_conv * window).astype(jnp.bfloat16))
    weight_grad = jnp.einsum('ot,btc->oc', filter_features.astype(jnp.float32), kernel_grad, precision=lax.Precision.HIGHEST)
    feature_part = jnp.einsum('oc,btc->ot', filter_weight.astype(jnp.float32), kernel_grad, precision=lax.Precision.HIGHEST)
    return (output, values_grad, first_grad, second_grad, weight_grad, feature_part)

def reference(values, gate_first, gate_second, filter_features, filter_weight, decay_rate, skip_bias, output_grad):
    block_count = values.shape[2] // CH_DEV

    def split_channels(source_array):
        shaped = source_array.reshape(source_array.shape[:-1] + (block_count, CH_DEV))
        return jnp.moveaxis(shaped, -2, 0)

    def join_channels(source_array):
        moved = jnp.moveaxis(source_array, 0, -2)
        return moved.reshape(moved.shape[:-2] + (block_count * CH_DEV,))
    blocks = (split_channels(values), split_channels(gate_first), split_channels(gate_second), split_channels(output_grad), split_channels(filter_weight), decay_rate.reshape(block_count, CH_DEV), skip_bias.reshape(block_count, CH_DEV))
    results = lax.map(partial(one_block, filter_features), blocks)
    output = join_channels(results[0])
    values_grad = join_channels(results[1])
    first_grad = join_channels(results[2])
    second_grad = join_channels(results[3])
    weight_grad = join_channels(results[4])
    feature_grad = lax.optimization_barrier(jnp.sum(results[5], axis=0))
    return (output, values_grad, first_grad, second_grad, weight_grad, feature_grad)
```

```python
import functools
import math

import jax
import jax.numpy as jnp
import numpy as np
from jax import lax
from jax.experimental import pallas as pl
from jax.experimental.pallas import tpu as pltpu
from jax.sharding import PartitionSpec as P

LENGTH = 8192
PERIOD = 2 * LENGTH
TOK = 512
RADIX = PERIOD // TOK
BLOCKS = RADIX // 2
HALF = RADIX // 2 + 1
CH = 256
OWN = 8
GROUP = 32
ORDER = 64
PAIRS = (HALF + 1) // 2
ROWS = 2 * HALF + PAIRS
VMEM_LIMIT = 56 * 1024 * 1024


def tables():
    grid = np.arange(TOK)
    angle = 2.0 * np.pi / TOK * (np.outer(grid, grid) % TOK)
    basis = np.concatenate([np.cos(angle), np.sin(angle)], axis=0).astype(jnp.bfloat16)
    turn = 2.0 * np.pi / PERIOD * np.outer(np.arange(HALF), grid)
    forward = np.stack([np.cos(turn), np.sin(turn)]).astype(np.float32)
    factor = 1.0 / (PERIOD * math.sqrt(LENGTH))
    inverse = (np.stack([np.cos(turn), np.sin(turn)]) * factor).astype(np.float32)
    return basis, forward, inverse


def add(a, b):
    if a is None:
        return b
    return a if b is None else a + b


def sub(a, b):
    if b is None:
        return a
    return -b if a is None else a - b


def neg(a):
    return None if a is None else -a


def rotate(value, index, period):
    real, imag = value
    if index == 0:
        return value
    if 4 * index == period:
        return imag, neg(real)
    c = math.cos(2 * math.pi * index / period)
    s = math.sin(2 * math.pi * index / period)
    if imag is None:
        return real * c, real * (-s)
    if 8 * index == period:
        return (real + imag) * c, (imag - real) * c
    return real * c + imag * s, imag * c - real * s


def rotate_back(value, index, period):
    real, imag = value
    if index == 0:
        return value
    if 4 * index == period:
        return neg(imag), real
    c = math.cos(2 * math.pi * index / period)
    s = math.sin(2 * math.pi * index / period)
    if 8 * index == period:
        return (real - imag) * c, (imag + real) * c
    return real * c - imag * s, imag * c + real * s


def real_dft(xs, n):
    if n == 2:
        return [(xs[0], None), (xs[0], None)]
    if n == 4:
        return [(xs[0] + xs[1], None), (xs[0], -xs[1]), (xs[0] - xs[1], None)]
    even = real_dft(xs[0::2], n // 2)
    odd = real_dft(xs[1::2], n // 2)
    out = [None] * (n // 2 + 1)
    for k in range(n // 4 + 1):
        t = rotate(odd[k], k, n)
        e = even[k]
        out[k] = (add(e[0], t[0]), add(e[1], t[1]))
        if 4 * k != n:
            out[n // 2 - k] = (sub(e[0], t[0]), sub(t[1], e[1]))
    return out


def real_inverse(spec, n):
    if n == 4:
        total = spec[0][0] + spec[2][0]
        diff = spec[0][0] - spec[2][0]
        return [total + 2.0 * spec[1][0], diff - 2.0 * spec[1][1]]
    even, odd = [], []
    for k in range(n // 4 + 1):
        a, b = spec[k], spec[n // 2 - k]
        if 4 * k == n:
            even.append((2.0 * a[0], None))
            odd.append((-2.0 * a[1], None))
            continue
        even.append((add(a[0], b[0]), sub(a[1], b[1])))
        odd.append(rotate_back((sub(a[0], b[0]), add(a[1], b[1])), k, n))
    first = real_inverse(even, n // 2)
    second = real_inverse(odd, n // 2)
    return [first[i // 2] if i % 2 == 0 else second[i // 2] for i in range(n // 2)]


def spread_kernel(place, values, gate_first, gate_second, grad, features, weight, decay, out):
    f32 = jnp.float32
    mixed = (values[...].astype(f32) * gate_first[...].astype(f32)).T
    scaled = (grad[...].astype(f32) * gate_second[...].astype(f32)).T
    both = jnp.concatenate(
        [mixed.reshape(GROUP, OWN, TOK), scaled.reshape(GROUP, OWN, TOK)], axis=1
    )
    out[:, :, :TOK] = both.astype(jnp.bfloat16)
    dp = place[0]
    ctx = place[1]
    half = TOK // 2
    mine = jnp.where(dp == 0, features[:, :half].astype(f32), features[:, half:].astype(f32))
    raw = lax.dot_general(
        weight[...],
        mine.astype(jnp.bfloat16),
        (((0,), (0,)), ((), ())),
        preferred_element_type=f32,
    )
    first = ctx * TOK + dp * half
    positions = (first + lax.broadcasted_iota(jnp.int32, (1, half), 1)).astype(f32) / LENGTH
    kernel = (raw * jnp.exp(-decay[...] * positions)).reshape(GROUP, OWN, half)
    folded = jnp.concatenate([kernel[:, :, : half // 2], kernel[:, :, half // 2 :]], axis=1)
    out[:, :, TOK:] = folded.astype(jnp.bfloat16)


def spread(place, values, gate_first, gate_second, grad, features, weight, decay, **kw):
    return pl.pallas_call(
        spread_kernel,
        out_shape=jax.ShapeDtypeStruct((GROUP, 2 * OWN, TOK + 128), jnp.bfloat16),
        in_specs=[pl.BlockSpec(memory_space=pltpu.SMEM)] + [pl.BlockSpec(memory_space=pltpu.VMEM)] * 7,
        out_specs=pl.BlockSpec(memory_space=pltpu.VMEM),
        compiler_params=pltpu.CompilerParams(vmem_limit_bytes=VMEM_LIMIT),
        name="spread",
        **kw,
    )(place, values, gate_first, gate_second, grad, features, weight, decay)


def spectral_kernel(
    got, basis, forward, inverse, features, decay, out, lhs_re, lhs_im, res_re, res_im, filt_re, filt_im, kernel_grad
):
    f32, bf16 = jnp.float32, jnp.bfloat16

    def lanes_of(chunk):
        return pl.ds(pl.multiple_of(chunk * 128, 128), 128)

    def transformed(xs, lanes):
        spec = real_dft(xs, RADIX)
        turned = []
        for k, (real, imag) in enumerate(spec):
            if k == 0:
                turned.append((real, jnp.zeros_like(real)))
                continue
            c = forward[0, k : k + 1, lanes]
            s = forward[1, k : k + 1, lanes]
            if imag is None:
                turned.append((real * c, -(real * s)))
            else:
                turned.append((real * c + imag * s, imag * c - real * s))
        return turned

    def signals_in(step, carry):
        s = step // 4
        lanes = lanes_of(step % 4)
        xs = [got[s * BLOCKS + j, :, lanes].astype(f32) for j in range(BLOCKS)]
        low = transformed([x[:OWN] for x in xs], lanes)
        high = transformed([x[OWN:] for x in xs], lanes)
        for k in range(HALF):
            lhs_re[2 * k + s, :, lanes] = jnp.concatenate([low[k][0], high[k][0]], axis=0).astype(bf16)
            lhs_im[2 * k + s, :, lanes] = jnp.concatenate([low[k][1], high[k][1]], axis=0).astype(bf16)
        return carry

    lax.fori_loop(0, 8, signals_in, 0)

    def kernel_in(s, carry):
        xs = [got[s * BLOCKS + j, :, TOK:].astype(f32) for j in range(BLOCKS)]
        for q in range(2):
            lanes = lanes_of(2 * s + q)
            spec = transformed([x[q * OWN : (q + 1) * OWN] for x in xs], lanes)
            spec.append((jnp.zeros_like(spec[0][0]),) * 2)
            for p in range(PAIRS):
                a, b = spec[2 * p], spec[2 * p + 1]
                lhs_re[2 * HALF + p, :, lanes] = jnp.concatenate([a[0], b[0]], axis=0).astype(bf16)
                lhs_im[2 * HALF + p, :, lanes] = jnp.concatenate([a[1], b[1]], axis=0).astype(bf16)
        return carry

    lax.fori_loop(0, 2, kernel_in, 0)

    def product(first, second):
        lhs = jnp.concatenate([first, second], axis=1)
        res = jnp.dot(lhs, basis[...], preferred_element_type=f32)
        return res.reshape(ROWS, 2 * OWN, TOK)

    real = lhs_re[...].reshape(ROWS * 2 * OWN, TOK)
    imag = lhs_im[...].reshape(ROWS * 2 * OWN, TOK)
    res_re[...] = product(real, imag)
    res_im[...] = product(imag, -real)

    filt_re[...] = jnp.zeros_like(filt_re)
    filt_im[...] = jnp.zeros_like(filt_im)

    def multiply(k, carry):
        pair = k // 2
        rows = pl.ds(pl.multiple_of(k % 2 * OWN, OWN), OWN)
        hr = res_re[2 * HALF + pair, rows, :]
        hi = res_im[2 * HALF + pair, rows, :]
        total_re, total_im = None, None
        for s in range(2):
            zr = res_re[2 * k + s, :OWN, :]
            zi = res_im[2 * k + s, :OWN, :]
            gr = res_re[2 * k + s, OWN:, :]
            gi = res_im[2 * k + s, OWN:, :]
            lhs_re[2 * k + s] = jnp.concatenate(
                [zr * hr - zi * hi, gr * hr + gi * hi], axis=0
            ).astype(bf16)
            lhs_im[2 * k + s] = jnp.concatenate(
                [zr * hi + zi * hr, gi * hr - gr * hi], axis=0
            ).astype(bf16)
            total_re = add(total_re, gr * zr + gi * zi)
            total_im = add(total_im, gi * zr - gr * zi)
        filt_re[pair, rows, :] = total_re
        filt_im[pair, rows, :] = total_im
        return carry

    lax.fori_loop(0, HALF, multiply, 0)
    lhs_re[2 * HALF :] = filt_re[...].astype(bf16)
    lhs_im[2 * HALF :] = filt_im[...].astype(bf16)

    real = lhs_re[...].reshape(ROWS * 2 * OWN, TOK)
    imag = lhs_im[...].reshape(ROWS * 2 * OWN, TOK)
    res_re[...] = product(real, -imag)
    res_im[...] = product(imag, real)

    def returned(spec, lanes):
        turned = []
        for k, (real, imag) in enumerate(spec):
            c = inverse[0, k : k + 1, lanes]
            s = inverse[1, k : k + 1, lanes]
            if k in (0, HALF - 1):
                turned.append((real * c - imag * s, None))
            else:
                turned.append((real * c - imag * s, imag * c + real * s))
        return real_inverse(turned, RADIX)

    def filter_out(chunk, carry):
        rate = decay[...]
        parts = []
        for q in range(2):
            lanes = lanes_of(chunk + 2 * q)
            spec = []
            for k in range(HALF):
                rows = slice(k % 2 * OWN, k % 2 * OWN + OWN)
                block = 2 * HALF + k // 2
                spec.append((res_re[block, rows, lanes], res_im[block, rows, lanes]))
            parts.append(returned(spec, lanes))
        ahead = lax.broadcasted_iota(jnp.int32, (OWN, 128), 1) + chunk * 128
        for j in range(BLOCKS):
            pieces = []
            for q in range(2):
                positions = (ahead + (TOK * j + 256 * q)).astype(f32) / LENGTH
                pieces.append(parts[q][j] * jnp.exp(-rate * positions))
            both = jnp.concatenate(pieces, axis=0).astype(bf16)
            kernel_grad[:, lanes_of(2 * j + chunk)] = both
            out[j, :, lanes_of(4 + chunk)] = both
            out[BLOCKS + j, :, lanes_of(4 + chunk)] = both
        return carry

    lax.fori_loop(0, 2, filter_out, 0)

    def signals_out(step, carry):
        s = step // 4
        lanes = lanes_of(step % 4)
        halves = []
        for rows in (slice(0, OWN), slice(OWN, 2 * OWN)):
            spec = [(res_re[2 * k + s, rows, lanes], res_im[2 * k + s, rows, lanes]) for k in range(HALF)]
            halves.append(returned(spec, lanes))
        for j in range(BLOCKS):
            out[s * BLOCKS + j, :, lanes] = jnp.concatenate([halves[0][j], halves[1][j]], axis=0).astype(bf16)
        return carry

    lax.fori_loop(0, 8, signals_out, 0)

    sums = []
    for q in range(2):
        along = jnp.concatenate(
            [features[j, :, 256 * q : 256 * (q + 1)] for j in range(BLOCKS)], axis=1
        )
        sums.append(
            lax.dot_general(
                kernel_grad[...], along, (((1,), (1,)), ((), ())), preferred_element_type=f32
            )
        )
    own_weight = sums[0][:OWN] + sums[1][OWN:]
    padded = jnp.concatenate([own_weight, jnp.zeros((OWN, 128 - ORDER), f32)], axis=1)
    padded = jnp.concatenate([padded, jnp.zeros((OWN, 128), f32)], axis=0).astype(bf16)
    out[:, :, TOK + 256 :] = jnp.broadcast_to(padded[None], (GROUP, 2 * OWN, 128))


def spectral(got, features, decay, **kw):
    basis, forward, inverse = tables()
    wide = pltpu.VMEM((ROWS, 2 * OWN, TOK), jnp.bfloat16)
    result = pltpu.VMEM((ROWS, 2 * OWN, TOK), jnp.float32)
    filt = pltpu.VMEM((PAIRS, 2 * OWN, TOK), jnp.float32)
    return pl.pallas_call(
        spectral_kernel,
        out_shape=jax.ShapeDtypeStruct((GROUP, 2 * OWN, TOK + 256 + 128), jnp.bfloat16),
        in_specs=[pl.BlockSpec(memory_space=pltpu.VMEM)] * 6,
        out_specs=pl.BlockSpec(memory_space=pltpu.VMEM),
        scratch_shapes=[
            wide, wide, result, result, filt, filt,
            pltpu.VMEM((2 * OWN, BLOCKS * 256), jnp.bfloat16),
        ],
        compiler_params=pltpu.CompilerParams(vmem_limit_bytes=VMEM_LIMIT),
        name="spectral",
        **kw,
    )(got, jnp.asarray(basis), jnp.asarray(forward), jnp.asarray(inverse), features, decay)


def feature_kernel(back, weight, part, weight_grad):
    f32, bf16 = jnp.float32, jnp.bfloat16
    for q in range(2):
        kernel_grad = back[:, :, TOK : TOK + 256].astype(f32)[:, q * OWN : (q + 1) * OWN]
        kernel_grad = kernel_grad.reshape(CH, 256).astype(bf16)
        part[:, 256 * q : 256 * (q + 1)] = jnp.dot(
            weight[...], kernel_grad, preferred_element_type=f32
        ).astype(bf16)
    own = back[:, :, TOK + 256 :].astype(f32)[:, :OWN].reshape(CH, 128)
    weight_grad[...] = own.T[:ORDER]


def feature_part(back, weight, **kw):
    return pl.pallas_call(
        feature_kernel,
        out_shape=(
            jax.ShapeDtypeStruct((ORDER, TOK), jnp.bfloat16),
            jax.ShapeDtypeStruct((ORDER, CH), jnp.float32),
        ),
        in_specs=[pl.BlockSpec(memory_space=pltpu.VMEM)] * 2,
        out_specs=(pl.BlockSpec(memory_space=pltpu.VMEM),) * 2,
        compiler_params=pltpu.CompilerParams(vmem_limit_bytes=VMEM_LIMIT),
        name="feature_part",
        **kw,
    )(back, weight)


def final_kernel(
    back, values, gate_first, gate_second, grad, skip, output, values_grad, first_grad, second_grad
):
    f32, bf16 = jnp.float32, jnp.bfloat16
    both = back[:, :, :TOK].astype(f32)
    conv = both[:, :OWN].reshape(CH, TOK).T
    grad_conv = both[:, OWN:].reshape(CH, TOK).T
    x = values[...].astype(f32)
    g1 = gate_first[...].astype(f32)
    g2 = gate_second[...].astype(f32)
    dy = grad[...].astype(f32)
    bias = skip[...]
    total = conv + bias * (x * g1).astype(bf16).astype(f32)
    output[...] = (g2 * total).astype(bf16)
    second_grad[...] = (dy * total).astype(bf16)
    delta = grad_conv + bias * (dy * g2).astype(bf16).astype(f32)
    values_grad[...] = (delta * g1).astype(bf16)
    first_grad[...] = (delta * x).astype(bf16)


def final(back, values, gate_first, gate_second, grad, skip, **kw):
    shape = jax.ShapeDtypeStruct((TOK, CH), jnp.bfloat16)
    return pl.pallas_call(
        final_kernel,
        out_shape=(shape,) * 4,
        in_specs=[pl.BlockSpec(memory_space=pltpu.VMEM)] * 6,
        out_specs=(pl.BlockSpec(memory_space=pltpu.VMEM),) * 4,
        compiler_params=pltpu.CompilerParams(vmem_limit_bytes=VMEM_LIMIT),
        name="final",
        **kw,
    )(back, values, gate_first, gate_second, grad, skip)


def local(
    values,
    gate_first,
    gate_second,
    filter_features,
    filter_weight,
    decay_rate,
    skip_bias,
    output_grad,
):
    values, gate_first, gate_second, output_grad = (
        a[0] for a in (values, gate_first, gate_second, output_grad)
    )
    dp = lax.axis_index("dp")
    ctx = lax.axis_index("ctx")
    group = ("dp", "ctx")
    place = jnp.stack([dp, ctx]).astype(jnp.int32)
    all_features = lax.all_gather(filter_features, "ctx")
    sent = spread(
        place, values, gate_first, gate_second, output_grad, filter_features, filter_weight, decay_rate[:, None]
    )
    got = lax.all_to_all(sent, group, 0, 0, tiled=True)
    own_decay = lax.dynamic_slice(decay_rate, ((dp * BLOCKS + ctx) * OWN,), (OWN,))
    own_decay = jnp.broadcast_to(own_decay[:, None], (OWN, 128))
    back = lax.all_to_all(spectral(got, all_features, own_decay), group, 0, 0, tiled=True)
    part, weight_grad = feature_part(back, filter_weight)
    pieces = part.reshape(16, 4, TOK)
    pieces = lax.all_to_all(pieces, "chan", 0, 0, tiled=True)
    summed = jnp.sum(pieces.astype(jnp.float32), axis=0).astype(jnp.bfloat16)
    copies = jnp.broadcast_to(summed[None], (16, 4, TOK))
    copies = lax.all_to_all(copies, "chan", 0, 0, tiled=True)
    feature_grad = copies.reshape(ORDER, TOK).astype(jnp.float32)
    outs = final(back, values, gate_first, gate_second, output_grad, skip_bias[None, :])
    output, values_grad, first_grad, second_grad = (a[None] for a in outs)
    return (output, values_grad, first_grad, second_grad, weight_grad, feature_grad)


def solution(mesh):
    in_specs = (
        P("dp", "ctx", "chan"),
        P("dp", "ctx", "chan"),
        P("dp", "ctx", "chan"),
        P(None, "ctx"),
        P(None, "chan"),
        P("chan"),
        P("chan"),
        P("dp", "ctx", "chan"),
    )
    out_specs = (
        P("dp", "ctx", "chan"),
        P("dp", "ctx", "chan"),
        P("dp", "ctx", "chan"),
        P("dp", "ctx", "chan"),
        P(None, "chan"),
        P(None, "ctx"),
    )
    return jax.shard_map(local, mesh=mesh, in_specs=in_specs, out_specs=out_specs, check_vma=False)
```

```python
import functools
import math

import jax
import jax.numpy as jnp
import numpy as np
from jax import lax
from jax.experimental import pallas as pl
from jax.experimental.pallas import tpu as pltpu
from jax.sharding import PartitionSpec as P

LENGTH = 8192
PERIOD = 2 * LENGTH
TOK = 512
RADIX = PERIOD // TOK
BLOCKS = RADIX // 2
HALF = RADIX // 2 + 1
CH = 256
OWN = 8
GROUP = 32
ORDER = 64
PAIRS = (HALF + 1) // 2
ROWS = 2 * HALF + PAIRS
VMEM_LIMIT = 56 * 1024 * 1024


def tables():
    grid = np.arange(TOK)
    angle = 2.0 * np.pi / TOK * (np.outer(grid, grid) % TOK)
    basis = np.concatenate([np.cos(angle), np.sin(angle)], axis=0).astype(jnp.bfloat16)
    turn = 2.0 * np.pi / PERIOD * np.outer(np.arange(HALF), grid)
    forward = np.stack([np.cos(turn), np.sin(turn)]).astype(np.float32)
    factor = 1.0 / (PERIOD * math.sqrt(LENGTH))
    inverse = (np.stack([np.cos(turn), np.sin(turn)]) * factor).astype(np.float32)
    return basis, forward, inverse


def add(a, b):
    if a is None:
        return b
    return a if b is None else a + b


def sub(a, b):
    if b is None:
        return a
    return -b if a is None else a - b


def neg(a):
    return None if a is None else -a


def rotate(value, index, period):
    real, imag = value
    if index == 0:
        return value
    if 4 * index == period:
        return imag, neg(real)
    c = math.cos(2 * math.pi * index / period)
    s = math.sin(2 * math.pi * index / period)
    if imag is None:
        return real * c, real * (-s)
    if 8 * index == period:
        return (real + imag) * c, (imag - real) * c
    return real * c + imag * s, imag * c - real * s


def rotate_back(value, index, period):
    real, imag = value
    if index == 0:
        return value
    if 4 * index == period:
        return neg(imag), real
    c = math.cos(2 * math.pi * index / period)
    s = math.sin(2 * math.pi * index / period)
    if 8 * index == period:
        return (real - imag) * c, (imag + real) * c
    return real * c - imag * s, imag * c + real * s


def real_dft(xs, n):
    if n == 2:
        return [(xs[0], None), (xs[0], None)]
    if n == 4:
        return [(xs[0] + xs[1], None), (xs[0], -xs[1]), (xs[0] - xs[1], None)]
    even = real_dft(xs[0::2], n // 2)
    odd = real_dft(xs[1::2], n // 2)
    out = [None] * (n // 2 + 1)
    for k in range(n // 4 + 1):
        t = rotate(odd[k], k, n)
        e = even[k]
        out[k] = (add(e[0], t[0]), add(e[1], t[1]))
        if 4 * k != n:
            out[n // 2 - k] = (sub(e[0], t[0]), sub(t[1], e[1]))
    return out


def real_inverse(spec, n):
    if n == 4:
        total = spec[0][0] + spec[2][0]
        diff = spec[0][0] - spec[2][0]
        return [total + 2.0 * spec[1][0], diff - 2.0 * spec[1][1]]
    even, odd = [], []
    for k in range(n // 4 + 1):
        a, b = spec[k], spec[n // 2 - k]
        if 4 * k == n:
            even.append((2.0 * a[0], None))
            odd.append((-2.0 * a[1], None))
            continue
        even.append((add(a[0], b[0]), sub(a[1], b[1])))
        odd.append(rotate_back((sub(a[0], b[0]), add(a[1], b[1])), k, n))
    first = real_inverse(even, n // 2)
    second = real_inverse(odd, n // 2)
    return [first[i // 2] if i % 2 == 0 else second[i // 2] for i in range(n // 2)]


def spread_kernel(values, gate_first, gate_second, grad, features, weight, decay, out):
    f32 = jnp.float32
    mixed = (values[...].astype(f32) * gate_first[...].astype(f32)).T
    scaled = (grad[...].astype(f32) * gate_second[...].astype(f32)).T
    both = jnp.concatenate(
        [mixed.reshape(GROUP, OWN, TOK), scaled.reshape(GROUP, OWN, TOK)], axis=1
    )
    out[:, :, :TOK] = both.astype(jnp.bfloat16)
    dp = lax.axis_index("dp")
    ctx = lax.axis_index("ctx")
    half = TOK // 2
    mine = jnp.where(dp == 0, features[:, :half].astype(f32), features[:, half:].astype(f32))
    raw = lax.dot_general(
        mine.astype(jnp.bfloat16),
        weight[...],
        (((0,), (0,)), ((), ())),
        preferred_element_type=f32,
    )
    first = ctx * TOK + dp * half
    positions = (first + lax.broadcasted_iota(jnp.int32, (half, 1), 0)).astype(f32) / LENGTH
    kernel = (raw * jnp.exp(-decay[...] * positions)).T.reshape(GROUP, OWN, half)
    folded = jnp.concatenate([kernel[:, :, : half // 2], kernel[:, :, half // 2 :]], axis=1)
    out[:, :, TOK:] = folded.astype(jnp.bfloat16)


def spread(values, gate_first, gate_second, grad, features, weight, decay, **kw):
    return pl.pallas_call(
        spread_kernel,
        out_shape=jax.ShapeDtypeStruct((GROUP, 2 * OWN, TOK + 128), jnp.bfloat16),
        in_specs=[pl.BlockSpec(memory_space=pltpu.VMEM)] * 7,
        out_specs=pl.BlockSpec(memory_space=pltpu.VMEM),
        compiler_params=pltpu.CompilerParams(vmem_limit_bytes=VMEM_LIMIT),
        name="spread",
        **kw,
    )(values, gate_first, gate_second, grad, features, weight, decay)


def spectral_kernel(
    got, basis, forward, inverse, decay, out, lhs_re, lhs_im, res_re, res_im, filt_re, filt_im, rates
):
    f32, bf16 = jnp.float32, jnp.bfloat16
    rates[...] = jnp.broadcast_to(decay[...], (128, CH)).T
    first = (lax.axis_index("dp") * BLOCKS + lax.axis_index("ctx")) * OWN

    def lanes_of(chunk):
        return pl.ds(pl.multiple_of(chunk * 128, 128), 128)

    def transformed(xs, lanes):
        spec = real_dft(xs, RADIX)
        turned = []
        for k, (real, imag) in enumerate(spec):
            if k == 0:
                turned.append((real, jnp.zeros_like(real)))
                continue
            c = forward[0, k : k + 1, lanes]
            s = forward[1, k : k + 1, lanes]
            if imag is None:
                turned.append((real * c, -(real * s)))
            else:
                turned.append((real * c + imag * s, imag * c - real * s))
        return turned

    def signals_in(step, carry):
        s = step // 4
        lanes = lanes_of(step % 4)
        xs = [got[s * BLOCKS + j, :, lanes].astype(f32) for j in range(BLOCKS)]
        low = transformed([x[:OWN] for x in xs], lanes)
        high = transformed([x[OWN:] for x in xs], lanes)
        for k in range(HALF):
            lhs_re[2 * k + s, :, lanes] = jnp.concatenate([low[k][0], high[k][0]], axis=0).astype(bf16)
            lhs_im[2 * k + s, :, lanes] = jnp.concatenate([low[k][1], high[k][1]], axis=0).astype(bf16)
        return carry

    lax.fori_loop(0, 8, signals_in, 0)

    def kernel_in(s, carry):
        xs = [got[s * BLOCKS + j, :, TOK:].astype(f32) for j in range(BLOCKS)]
        for q in range(2):
            lanes = lanes_of(2 * s + q)
            spec = transformed([x[q * OWN : (q + 1) * OWN] for x in xs], lanes)
            spec.append((jnp.zeros_like(spec[0][0]),) * 2)
            for p in range(PAIRS):
                a, b = spec[2 * p], spec[2 * p + 1]
                lhs_re[2 * HALF + p, :, lanes] = jnp.concatenate([a[0], b[0]], axis=0).astype(bf16)
                lhs_im[2 * HALF + p, :, lanes] = jnp.concatenate([a[1], b[1]], axis=0).astype(bf16)
        return carry

    lax.fori_loop(0, 2, kernel_in, 0)

    def product(first, second):
        lhs = jnp.concatenate([first, second], axis=1)
        res = jnp.dot(lhs, basis[...], preferred_element_type=f32)
        return res.reshape(ROWS, 2 * OWN, TOK)

    real = lhs_re[...].reshape(ROWS * 2 * OWN, TOK)
    imag = lhs_im[...].reshape(ROWS * 2 * OWN, TOK)
    res_re[...] = product(real, imag)
    res_im[...] = product(imag, -real)

    filt_re[...] = jnp.zeros_like(filt_re)
    filt_im[...] = jnp.zeros_like(filt_im)

    def multiply(k, carry):
        pair = k // 2
        rows = pl.ds(pl.multiple_of(k % 2 * OWN, OWN), OWN)
        hr = res_re[2 * HALF + pair, rows, :]
        hi = res_im[2 * HALF + pair, rows, :]
        total_re, total_im = None, None
        for s in range(2):
            zr = res_re[2 * k + s, :OWN, :]
            zi = res_im[2 * k + s, :OWN, :]
            gr = res_re[2 * k + s, OWN:, :]
            gi = res_im[2 * k + s, OWN:, :]
            lhs_re[2 * k + s] = jnp.concatenate(
                [zr * hr - zi * hi, gr * hr + gi * hi], axis=0
            ).astype(bf16)
            lhs_im[2 * k + s] = jnp.concatenate(
                [zr * hi + zi * hr, gi * hr - gr * hi], axis=0
            ).astype(bf16)
            total_re = add(total_re, gr * zr + gi * zi)
            total_im = add(total_im, gi * zr - gr * zi)
        filt_re[pair, rows, :] = total_re
        filt_im[pair, rows, :] = total_im
        return carry

    lax.fori_loop(0, HALF, multiply, 0)
    lhs_re[2 * HALF :] = filt_re[...].astype(bf16)
    lhs_im[2 * HALF :] = filt_im[...].astype(bf16)

    real = lhs_re[...].reshape(ROWS * 2 * OWN, TOK)
    imag = lhs_im[...].reshape(ROWS * 2 * OWN, TOK)
    res_re[...] = product(real, -imag)
    res_im[...] = product(imag, real)

    def returned(spec, lanes):
        turned = []
        for k, (real, imag) in enumerate(spec):
            c = inverse[0, k : k + 1, lanes]
            s = inverse[1, k : k + 1, lanes]
            if k in (0, HALF - 1):
                turned.append((real * c - imag * s, None))
            else:
                turned.append((real * c - imag * s, imag * c + real * s))
        return real_inverse(turned, RADIX)

    def filter_out(chunk, carry):
        rate = rates[pl.ds(pl.multiple_of(first, OWN), OWN), :]
        parts = []
        for q in range(2):
            lanes = lanes_of(chunk + 2 * q)
            spec = []
            for k in range(HALF):
                rows = slice(k % 2 * OWN, k % 2 * OWN + OWN)
                block = 2 * HALF + k // 2
                spec.append((res_re[block, rows, lanes], res_im[block, rows, lanes]))
            parts.append(returned(spec, lanes))
        ahead = lax.broadcasted_iota(jnp.int32, (OWN, 128), 1) + chunk * 128
        for j in range(BLOCKS):
            pieces = []
            for q in range(2):
                positions = (ahead + (TOK * j + 256 * q)).astype(f32) / LENGTH
                pieces.append(parts[q][j] * jnp.exp(-rate * positions))
            both = jnp.concatenate(pieces, axis=0).astype(bf16)
            out[j, :, lanes_of(4 + chunk)] = both
            out[BLOCKS + j, :, lanes_of(4 + chunk)] = both
        return carry

    lax.fori_loop(0, 2, filter_out, 0)

    def signals_out(step, carry):
        s = step // 4
        lanes = lanes_of(step % 4)
        halves = []
        for rows in (slice(0, OWN), slice(OWN, 2 * OWN)):
            spec = [(res_re[2 * k + s, rows, lanes], res_im[2 * k + s, rows, lanes]) for k in range(HALF)]
            halves.append(returned(spec, lanes))
        for j in range(BLOCKS):
            out[s * BLOCKS + j, :, lanes] = jnp.concatenate([halves[0][j], halves[1][j]], axis=0).astype(bf16)
        return carry

    lax.fori_loop(0, 8, signals_out, 0)


def spectral(got, decay, **kw):
    basis, forward, inverse = tables()
    wide = pltpu.VMEM((ROWS, 2 * OWN, TOK), jnp.bfloat16)
    result = pltpu.VMEM((ROWS, 2 * OWN, TOK), jnp.float32)
    filt = pltpu.VMEM((PAIRS, 2 * OWN, TOK), jnp.float32)
    return pl.pallas_call(
        spectral_kernel,
        out_shape=jax.ShapeDtypeStruct((GROUP, 2 * OWN, TOK + 256), jnp.bfloat16),
        in_specs=[pl.BlockSpec(memory_space=pltpu.VMEM)] * 5,
        out_specs=pl.BlockSpec(memory_space=pltpu.VMEM),
        scratch_shapes=[
            wide, wide, result, result, filt, filt,
            pltpu.VMEM((CH, 128), jnp.float32),
        ],
        compiler_params=pltpu.CompilerParams(vmem_limit_bytes=VMEM_LIMIT),
        name="spectral",
        **kw,
    )(got, jnp.asarray(basis), jnp.asarray(forward), jnp.asarray(inverse), decay)


def parts_kernel(back, features, weight, feature_part, weight_part):
    f32, bf16 = jnp.float32, jnp.bfloat16
    half = TOK // 2
    own = back[:, :, TOK:].astype(f32)
    weight_sum = None
    for q in range(2):
        kernel_grad = own[:, q * OWN : (q + 1) * OWN].reshape(CH, half).astype(bf16)
        along = jnp.dot(weight[...], kernel_grad, preferred_element_type=f32).astype(bf16)
        for p in range(2):
            for r in range(4):
                feature_part[4 * r + 2 * q + p] = along[16 * r : 16 * (r + 1), 128 * p : 128 * (p + 1)]
        weight_sum = add(
            weight_sum,
            lax.dot_general(
                features[:, half * q : half * (q + 1)],
                kernel_grad,
                (((1,), (1,)), ((), ())),
                preferred_element_type=f32,
            ),
        )
    weight_part[...] = weight_sum.astype(bf16)


def parts(back, features, weight, **kw):
    return pl.pallas_call(
        parts_kernel,
        out_shape=(
            jax.ShapeDtypeStruct((16, 16, 128), jnp.bfloat16),
            jax.ShapeDtypeStruct((ORDER, CH), jnp.bfloat16),
        ),
        in_specs=[pl.BlockSpec(memory_space=pltpu.VMEM)] * 3,
        out_specs=(pl.BlockSpec(memory_space=pltpu.VMEM),) * 2,
        compiler_params=pltpu.CompilerParams(vmem_limit_bytes=VMEM_LIMIT),
        name="parts",
        **kw,
    )(back, features, weight)


def final_kernel(
    back, values, gate_first, gate_second, grad, skip, output, values_grad, first_grad, second_grad
):
    f32, bf16 = jnp.float32, jnp.bfloat16
    both = back[:, :, :TOK].astype(f32)
    conv = both[:, :OWN].reshape(CH, TOK).T
    grad_conv = both[:, OWN:].reshape(CH, TOK).T
    x = values[...].astype(f32)
    g1 = gate_first[...].astype(f32)
    g2 = gate_second[...].astype(f32)
    dy = grad[...].astype(f32)
    bias = skip[...]
    total = conv + bias * (x * g1).astype(bf16).astype(f32)
    output[...] = (g2 * total).astype(bf16)
    second_grad[...] = (dy * total).astype(bf16)
    delta = grad_conv + bias * (dy * g2).astype(bf16).astype(f32)
    values_grad[...] = (delta * g1).astype(bf16)
    first_grad[...] = (delta * x).astype(bf16)


def final(back, values, gate_first, gate_second, grad, skip, **kw):
    shape = jax.ShapeDtypeStruct((TOK, CH), jnp.bfloat16)
    return pl.pallas_call(
        final_kernel,
        out_shape=(shape,) * 4,
        in_specs=[pl.BlockSpec(memory_space=pltpu.VMEM)] * 6,
        out_specs=(pl.BlockSpec(memory_space=pltpu.VMEM),) * 4,
        compiler_params=pltpu.CompilerParams(vmem_limit_bytes=VMEM_LIMIT),
        name="final",
        **kw,
    )(back, values, gate_first, gate_second, grad, skip)


def local(
    values,
    gate_first,
    gate_second,
    filter_features,
    filter_weight,
    decay_rate,
    skip_bias,
    output_grad,
):
    values, gate_first, gate_second, output_grad = (
        a[0] for a in (values, gate_first, gate_second, output_grad)
    )
    group = ("dp", "ctx")
    decay = decay_rate[None, :]
    sent = spread(values, gate_first, gate_second, output_grad, filter_features, filter_weight, decay)
    got = lax.all_to_all(sent, group, 0, 0, tiled=True)
    back = lax.all_to_all(spectral(got, decay), group, 0, 0, tiled=True)
    feature_part, weight_part = parts(back, filter_features, filter_weight)
    pieces = lax.all_to_all(feature_part, "chan", 0, 0, tiled=True)
    summed = jnp.sum(pieces.astype(jnp.float32), axis=0).astype(jnp.bfloat16)
    copies = lax.all_to_all(jnp.broadcast_to(summed[None], (16, 16, 128)), "chan", 0, 0, tiled=True)
    feature_grad = copies.reshape(4, 4, 16, 128).transpose(0, 2, 1, 3).reshape(ORDER, TOK)
    feature_grad = feature_grad.astype(jnp.float32)
    for distance in (1, 2, 4, 8):
        other = lax.ppermute(weight_part, "ctx", [(i, i ^ distance) for i in range(BLOCKS)])
        weight_sum = weight_part.astype(jnp.float32) + other.astype(jnp.float32)
        weight_part = weight_sum.astype(jnp.bfloat16)
    weight_grad = weight_sum
    outs = final(back, values, gate_first, gate_second, output_grad, skip_bias[None, :])
    output, values_grad, first_grad, second_grad = (a[None] for a in outs)
    return (output, values_grad, first_grad, second_grad, weight_grad, feature_grad)


def solution(mesh):
    in_specs = (
        P("dp", "ctx", "chan"),
        P("dp", "ctx", "chan"),
        P("dp", "ctx", "chan"),
        P(None, "ctx"),
        P(None, "chan"),
        P("chan"),
        P("chan"),
        P("dp", "ctx", "chan"),
    )
    out_specs = (
        P("dp", "ctx", "chan"),
        P("dp", "ctx", "chan"),
        P("dp", "ctx", "chan"),
        P("dp", "ctx", "chan"),
        P(None, "chan"),
        P(None, "ctx"),
    )
    return jax.shard_map(local, mesh=mesh, in_specs=in_specs, out_specs=out_specs, check_vma=False)
```

```python
import functools
import math

import jax
import jax.numpy as jnp
import numpy as np
from jax import lax
from jax.experimental import pallas as pl
from jax.experimental.pallas import tpu as pltpu
from jax.sharding import PartitionSpec as P

LENGTH = 8192
PERIOD = 2 * LENGTH
TOK = 512
RADIX = PERIOD // TOK
BLOCKS = RADIX // 2
HALF = RADIX // 2 + 1
CH = 256
OWN = 8
GROUP = 32
ORDER = 64
PAIRS = (HALF + 1) // 2
ROWS = 2 * HALF + PAIRS
VMEM_LIMIT = 56 * 1024 * 1024


def tables():
    grid = np.arange(TOK)
    angle = 2.0 * np.pi / TOK * (np.outer(grid, grid) % TOK)
    basis = np.concatenate([np.cos(angle), np.sin(angle)], axis=0).astype(jnp.bfloat16)
    turn = 2.0 * np.pi / PERIOD * np.outer(np.arange(HALF), grid)
    forward = np.stack([np.cos(turn), np.sin(turn)]).astype(np.float32)
    factor = 1.0 / (PERIOD * math.sqrt(LENGTH))
    inverse = (np.stack([np.cos(turn), np.sin(turn)]) * factor).astype(np.float32)
    return basis, forward, inverse


def add(a, b):
    if a is None:
        return b
    return a if b is None else a + b


def sub(a, b):
    if b is None:
        return a
    return -b if a is None else a - b


def neg(a):
    return None if a is None else -a


def rotate(value, index, period):
    real, imag = value
    if index == 0:
        return value
    if 4 * index == period:
        return imag, neg(real)
    c = math.cos(2 * math.pi * index / period)
    s = math.sin(2 * math.pi * index / period)
    if imag is None:
        return real * c, real * (-s)
    if 8 * index == period:
        return (real + imag) * c, (imag - real) * c
    return real * c + imag * s, imag * c - real * s


def rotate_back(value, index, period):
    real, imag = value
    if index == 0:
        return value
    if 4 * index == period:
        return neg(imag), real
    c = math.cos(2 * math.pi * index / period)
    s = math.sin(2 * math.pi * index / period)
    if 8 * index == period:
        return (real - imag) * c, (imag + real) * c
    return real * c - imag * s, imag * c + real * s


def real_dft(xs, n):
    if n == 2:
        return [(xs[0], None), (xs[0], None)]
    if n == 4:
        return [(xs[0] + xs[1], None), (xs[0], -xs[1]), (xs[0] - xs[1], None)]
    even = real_dft(xs[0::2], n // 2)
    odd = real_dft(xs[1::2], n // 2)
    out = [None] * (n // 2 + 1)
    for k in range(n // 4 + 1):
        t = rotate(odd[k], k, n)
        e = even[k]
        out[k] = (add(e[0], t[0]), add(e[1], t[1]))
        if 4 * k != n:
            out[n // 2 - k] = (sub(e[0], t[0]), sub(t[1], e[1]))
    return out


def real_inverse(spec, n):
    if n == 4:
        total = spec[0][0] + spec[2][0]
        diff = spec[0][0] - spec[2][0]
        return [total + 2.0 * spec[1][0], diff - 2.0 * spec[1][1]]
    even, odd = [], []
    for k in range(n // 4 + 1):
        a, b = spec[k], spec[n // 2 - k]
        if 4 * k == n:
            even.append((2.0 * a[0], None))
            odd.append((-2.0 * a[1], None))
            continue
        even.append((add(a[0], b[0]), sub(a[1], b[1])))
        odd.append(rotate_back((sub(a[0], b[0]), add(a[1], b[1])), k, n))
    first = real_inverse(even, n // 2)
    second = real_inverse(odd, n // 2)
    return [first[i // 2] if i % 2 == 0 else second[i // 2] for i in range(n // 2)]


def spread_kernel(
    values, gate_first, gate_second, grad, features, weight, decay, out, held, ready, arrived, left
):
    f32 = jnp.float32
    half = TOK // 2
    wide = CH // 2
    loads = []
    for part in range(2):
        lanes = pl.ds(part * wide, wide)
        for slot, source in enumerate((values, gate_first, grad, gate_second)):
            copy = pltpu.make_async_copy(
                source.at[:, lanes], held.at[part, slot], arrived.at[part, slot]
            )
            copy.start()
            loads.append(copy)
    dp = lax.axis_index("dp")
    ctx = lax.axis_index("ctx")
    mine = jnp.where(dp == 0, features[:, :half].astype(f32), features[:, half:].astype(f32))
    raw = lax.dot_general(
        mine.astype(jnp.bfloat16),
        weight[...],
        (((0,), (0,)), ((), ())),
        preferred_element_type=f32,
    )
    first = ctx * TOK + dp * half
    positions = (first + lax.broadcasted_iota(jnp.int32, (half, 1), 0)).astype(f32) / LENGTH
    kernel = (raw * jnp.exp(-decay[...] * positions)).T.reshape(GROUP, OWN, half)
    folded = jnp.concatenate([kernel[:, :, : half // 2], kernel[:, :, half // 2 :]], axis=1)
    ready[:, :, TOK:] = folded.astype(jnp.bfloat16)
    stores = []
    owners = GROUP // 2
    for part in range(2):
        for copy in loads[4 * part : 4 * part + 4]:
            copy.wait()
        mixed = (held[part, 0].astype(f32) * held[part, 1].astype(f32)).T
        scaled = (held[part, 2].astype(f32) * held[part, 3].astype(f32)).T
        both = jnp.concatenate(
            [mixed.reshape(owners, OWN, TOK), scaled.reshape(owners, OWN, TOK)], axis=1
        )
        rows = pl.ds(part * owners, owners)
        ready[part * owners : (part + 1) * owners, :, :TOK] = both.astype(jnp.bfloat16)
        copy = pltpu.make_async_copy(ready.at[rows], out.at[rows], left.at[part])
        copy.start()
        stores.append(copy)
    for copy in stores:
        copy.wait()


def spread(values, gate_first, gate_second, grad, features, weight, decay, **kw):
    shape = (GROUP, 2 * OWN, TOK + 128)
    anywhere = pl.BlockSpec(memory_space=pl.ANY)
    return pl.pallas_call(
        spread_kernel,
        out_shape=jax.ShapeDtypeStruct(shape, jnp.bfloat16),
        in_specs=[anywhere] * 4 + [pl.BlockSpec(memory_space=pltpu.VMEM)] * 3,
        out_specs=anywhere,
        scratch_shapes=[
            pltpu.VMEM((2, 4, TOK, CH // 2), jnp.bfloat16),
            pltpu.VMEM(shape, jnp.bfloat16),
            pltpu.SemaphoreType.DMA((2, 4)),
            pltpu.SemaphoreType.DMA((2,)),
        ],
        compiler_params=pltpu.CompilerParams(vmem_limit_bytes=VMEM_LIMIT),
        name="spread",
        **kw,
    )(values, gate_first, gate_second, grad, features, weight, decay)


def spectral_kernel(
    source, table, forward, inverse, decay, target,
    got, basis, out, lhs_re, lhs_im, res_re, res_im, rates, arrived, left,
):
    f32, bf16 = jnp.float32, jnp.bfloat16

    def load(s):
        rows = pl.ds(s * BLOCKS, BLOCKS)
        return pltpu.make_async_copy(source.at[rows], got.at[rows], arrived.at[s])

    def store(s):
        rows = pl.ds(s * BLOCKS, BLOCKS)
        return pltpu.make_async_copy(out.at[rows], target.at[rows], left.at[s])

    table_load = pltpu.make_async_copy(table, basis, arrived.at[2])
    load(0).start()
    load(1).start()
    table_load.start()
    rates[...] = jnp.broadcast_to(decay[...], (128, CH)).T
    first = (lax.axis_index("dp") * BLOCKS + lax.axis_index("ctx")) * OWN

    def lanes_of(chunk):
        return pl.ds(pl.multiple_of(chunk * 128, 128), 128)

    def transformed(xs, lanes):
        spec = real_dft(xs, RADIX)
        turned = []
        for k, (real, imag) in enumerate(spec):
            if k == 0:
                turned.append((real, jnp.zeros_like(real)))
                continue
            c = forward[0, k : k + 1, lanes]
            s = forward[1, k : k + 1, lanes]
            if imag is None:
                turned.append((real * c, -(real * s)))
            else:
                turned.append((real * c + imag * s, imag * c - real * s))
        return turned

    def signals_in(s, chunk):
        lanes = lanes_of(chunk)
        xs = [got[s * BLOCKS + j, :, lanes].astype(f32) for j in range(BLOCKS)]
        low = transformed([x[:OWN] for x in xs], lanes)
        high = transformed([x[OWN:] for x in xs], lanes)
        for k in range(HALF):
            lhs_re[2 * k + s, :, lanes] = jnp.concatenate([low[k][0], high[k][0]], axis=0).astype(bf16)
            lhs_im[2 * k + s, :, lanes] = jnp.concatenate([low[k][1], high[k][1]], axis=0).astype(bf16)

    def kernel_in(s):
        xs = [got[s * BLOCKS + j, :, TOK:].astype(f32) for j in range(BLOCKS)]
        for q in range(2):
            lanes = lanes_of(2 * s + q)
            spec = transformed([x[q * OWN : (q + 1) * OWN] for x in xs], lanes)
            spec.append((jnp.zeros_like(spec[0][0]),) * 2)
            for p in range(PAIRS):
                a, b = spec[2 * p], spec[2 * p + 1]
                lhs_re[2 * HALF + p, :, lanes] = jnp.concatenate([a[0], b[0]], axis=0).astype(bf16)
                lhs_im[2 * HALF + p, :, lanes] = jnp.concatenate([a[1], b[1]], axis=0).astype(bf16)

    def sequence_in(s, carry):
        load(s).wait()

        def chunk_in(chunk, inner):
            signals_in(s, chunk)
            return inner

        lax.fori_loop(0, 4, chunk_in, 0)
        kernel_in(s)
        return carry

    lax.fori_loop(0, 2, sequence_in, 0)
    table_load.wait()

    def product(first, second):
        lhs = jnp.concatenate([first, second], axis=1)
        res = jnp.dot(lhs, basis[...], preferred_element_type=f32)
        return res.reshape(ROWS, 2 * OWN, TOK)

    real = lhs_re[...].reshape(ROWS * 2 * OWN, TOK)
    imag = lhs_im[...].reshape(ROWS * 2 * OWN, TOK)
    res_re[...] = product(real, imag)
    res_im[...] = product(imag, -real)

    def multiply(k, pair, rows):
        hr = res_re[2 * HALF + pair, rows, :]
        hi = res_im[2 * HALF + pair, rows, :]
        total_re, total_im = None, None
        for s in range(2):
            zr = res_re[2 * k + s, :OWN, :]
            zi = res_im[2 * k + s, :OWN, :]
            gr = res_re[2 * k + s, OWN:, :]
            gi = res_im[2 * k + s, OWN:, :]
            lhs_re[2 * k + s] = jnp.concatenate(
                [zr * hr - zi * hi, gr * hr + gi * hi], axis=0
            ).astype(bf16)
            lhs_im[2 * k + s] = jnp.concatenate(
                [zr * hi + zi * hr, gi * hr - gr * hi], axis=0
            ).astype(bf16)
            total_re = add(total_re, gr * zr + gi * zi)
            total_im = add(total_im, gi * zr - gr * zi)
        return total_re, total_im

    def multiply_pair(pair, carry):
        a = multiply(2 * pair, pair, slice(0, OWN))
        b = multiply(2 * pair + 1, pair, slice(OWN, 2 * OWN))
        lhs_re[2 * HALF + pair] = jnp.concatenate([a[0], b[0]], axis=0).astype(bf16)
        lhs_im[2 * HALF + pair] = jnp.concatenate([a[1], b[1]], axis=0).astype(bf16)
        return carry

    lax.fori_loop(0, PAIRS - 1, multiply_pair, 0, unroll=2)
    last = PAIRS - 1
    a = multiply(2 * last, last, slice(0, OWN))
    blank = jnp.zeros_like(a[0])
    lhs_re[2 * HALF + last] = jnp.concatenate([a[0], blank], axis=0).astype(bf16)
    lhs_im[2 * HALF + last] = jnp.concatenate([a[1], blank], axis=0).astype(bf16)

    real = lhs_re[...].reshape(ROWS * 2 * OWN, TOK)
    imag = lhs_im[...].reshape(ROWS * 2 * OWN, TOK)
    res_re[...] = product(real, -imag)
    res_im[...] = product(imag, real)

    def returned(spec, lanes):
        turned = []
        for k, (real, imag) in enumerate(spec):
            c = inverse[0, k : k + 1, lanes]
            s = inverse[1, k : k + 1, lanes]
            if k in (0, HALF - 1):
                turned.append((real * c - imag * s, None))
            else:
                turned.append((real * c - imag * s, imag * c + real * s))
        return real_inverse(turned, RADIX)

    rate = rates[pl.ds(pl.multiple_of(first, OWN), OWN), :]
    steps = [jnp.exp(-rate * (TOK * j / LENGTH)) for j in range(BLOCKS)]

    def filter_out(chunk, carry):
        pieces = []
        for q in range(2):
            lanes = lanes_of(chunk + 2 * q)
            spec = []
            for k in range(HALF):
                rows = slice(k % 2 * OWN, k % 2 * OWN + OWN)
                block = 2 * HALF + k // 2
                spec.append((res_re[block, rows, lanes], res_im[block, rows, lanes]))
            ahead = lax.broadcasted_iota(jnp.int32, (OWN, 128), 1) + (chunk * 128 + 256 * q)
            fine = jnp.exp(-rate * (ahead.astype(f32) / LENGTH))
            pieces.append([y * (fine * steps[j]) for j, y in enumerate(returned(spec, lanes))])
        for j in range(BLOCKS):
            both = jnp.concatenate([pieces[0][j], pieces[1][j]], axis=0).astype(bf16)
            out[j, :, lanes_of(4 + chunk)] = both
            out[BLOCKS + j, :, lanes_of(4 + chunk)] = both
        return carry

    lax.fori_loop(0, 2, filter_out, 0)

    def sequence_out(s, carry):
        def chunk_out(chunk, inner):
            lanes = lanes_of(chunk)
            halves = []
            for rows in (slice(0, OWN), slice(OWN, 2 * OWN)):
                spec = [
                    (res_re[2 * k + s, rows, lanes], res_im[2 * k + s, rows, lanes]) for k in range(HALF)
                ]
                halves.append(returned(spec, lanes))
            for j in range(BLOCKS):
                both = jnp.concatenate([halves[0][j], halves[1][j]], axis=0).astype(bf16)
                out[s * BLOCKS + j, :, lanes] = both
            return inner

        lax.fori_loop(0, 4, chunk_out, 0)
        store(s).start()
        return carry

    lax.fori_loop(0, 2, sequence_out, 0)
    store(0).wait()
    store(1).wait()


def spectral(got, decay, **kw):
    basis, forward, inverse = tables()
    wide = pltpu.VMEM((ROWS, 2 * OWN, TOK), jnp.bfloat16)
    result = pltpu.VMEM((ROWS, 2 * OWN, TOK), jnp.float32)
    shape = (GROUP, 2 * OWN, TOK + 256)
    anywhere = pl.BlockSpec(memory_space=pl.ANY)
    return pl.pallas_call(
        spectral_kernel,
        out_shape=jax.ShapeDtypeStruct(shape, jnp.bfloat16),
        in_specs=[anywhere] * 2 + [pl.BlockSpec(memory_space=pltpu.VMEM)] * 3,
        out_specs=anywhere,
        scratch_shapes=[
            pltpu.VMEM(got.shape, jnp.bfloat16),
            pltpu.VMEM(basis.shape, jnp.bfloat16),
            pltpu.VMEM(shape, jnp.bfloat16),
            wide, wide, result, result,
            pltpu.VMEM((CH, 128), jnp.float32),
            pltpu.SemaphoreType.DMA((3,)),
            pltpu.SemaphoreType.DMA((2,)),
        ],
        compiler_params=pltpu.CompilerParams(vmem_limit_bytes=VMEM_LIMIT),
        name="spectral",
        **kw,
    )(got, jnp.asarray(basis), jnp.asarray(forward), jnp.asarray(inverse), decay)


def parts_kernel(back, features, weight, sums, own, arrived):
    f32, bf16 = jnp.float32, jnp.bfloat16
    half = TOK // 2
    copy = pltpu.make_async_copy(back.at[:, :, pl.ds(TOK, half)], own, arrived)
    copy.start()
    copy.wait()
    is_feature = lax.axis_index("dp") == 0
    alongs, weight_sum = [], None
    for q in range(2):
        kernel_grad = own[...].astype(f32)[:, q * OWN : (q + 1) * OWN].reshape(CH, half).astype(bf16)
        alongs.append(jnp.dot(weight[...], kernel_grad, preferred_element_type=f32))
        share = lax.dot_general(
            features[:, half * q : half * (q + 1)],
            kernel_grad,
            (((1,), (1,)), ((), ())),
            preferred_element_type=f32,
        )
        weight_sum = add(weight_sum, share)
    blank = jnp.zeros((8, 128), f32)
    for piece in range(16):
        r, c = piece // 4, piece % 4
        feature = alongs[c // 2][16 * r : 16 * (r + 1), 128 * (c % 2) : 128 * (c % 2 + 1)]
        r, c = piece // 2, piece % 2
        other = weight_sum[8 * r : 8 * (r + 1), 128 * c : 128 * (c + 1)]
        other = jnp.concatenate([other, blank], axis=0)
        sums[piece] = jnp.where(is_feature, feature, other).astype(bf16)


def parts(back, features, weight, **kw):
    return pl.pallas_call(
        parts_kernel,
        out_shape=jax.ShapeDtypeStruct((16, 16, 128), jnp.bfloat16),
        in_specs=[pl.BlockSpec(memory_space=pl.ANY)] + [pl.BlockSpec(memory_space=pltpu.VMEM)] * 2,
        out_specs=pl.BlockSpec(memory_space=pltpu.VMEM),
        scratch_shapes=[
            pltpu.VMEM((GROUP, 2 * OWN, TOK // 2), jnp.bfloat16),
            pltpu.SemaphoreType.DMA(()),
        ],
        compiler_params=pltpu.CompilerParams(vmem_limit_bytes=VMEM_LIMIT),
        name="parts",
        **kw,
    )(back, features, weight)


def assemble_kernel(own, other, feature_grad, weight_grad):
    f32 = jnp.float32
    is_feature = lax.axis_index("dp") == 0
    for piece in range(16):
        a = own[piece].astype(f32)
        b = other[piece].astype(f32)
        feature = jnp.where(is_feature, a, b)
        weight = jnp.where(is_feature, b, a)[:8]
        r, c = piece // 4, piece % 4
        feature_grad[16 * r : 16 * (r + 1), 128 * c : 128 * (c + 1)] = feature
        r, c = piece // 2, piece % 2
        weight_grad[8 * r : 8 * (r + 1), 128 * c : 128 * (c + 1)] = weight


def assemble(own, other, **kw):
    return pl.pallas_call(
        assemble_kernel,
        out_shape=(
            jax.ShapeDtypeStruct((ORDER, TOK), jnp.float32),
            jax.ShapeDtypeStruct((ORDER, CH), jnp.float32),
        ),
        in_specs=[pl.BlockSpec(memory_space=pltpu.VMEM)] * 2,
        out_specs=(pl.BlockSpec(memory_space=pltpu.VMEM),) * 2,
        name="assemble",
        **kw,
    )(own, other)


def final_kernel(
    back, values, gate_first, gate_second, grad, skip, output, values_grad, first_grad, second_grad
):
    f32, bf16 = jnp.float32, jnp.bfloat16
    both = back[:, :, :TOK].astype(f32)
    conv = both[:, :OWN].reshape(CH, TOK).T
    grad_conv = both[:, OWN:].reshape(CH, TOK).T
    x = values[...].astype(f32)
    g1 = gate_first[...].astype(f32)
    g2 = gate_second[...].astype(f32)
    dy = grad[...].astype(f32)
    bias = skip[...]
    total = conv + bias * (x * g1).astype(bf16).astype(f32)
    output[...] = (g2 * total).astype(bf16)
    second_grad[...] = (dy * total).astype(bf16)
    delta = grad_conv + bias * (dy * g2).astype(bf16).astype(f32)
    values_grad[...] = (delta * g1).astype(bf16)
    first_grad[...] = (delta * x).astype(bf16)


def final(back, values, gate_first, gate_second, grad, skip, **kw):
    shape = jax.ShapeDtypeStruct((TOK, CH), jnp.bfloat16)
    return pl.pallas_call(
        final_kernel,
        out_shape=(shape,) * 4,
        in_specs=[pl.BlockSpec(memory_space=pltpu.VMEM)] * 6,
        out_specs=(pl.BlockSpec(memory_space=pltpu.VMEM),) * 4,
        compiler_params=pltpu.CompilerParams(vmem_limit_bytes=VMEM_LIMIT),
        name="final",
        **kw,
    )(back, values, gate_first, gate_second, grad, skip)


def local(
    values,
    gate_first,
    gate_second,
    filter_features,
    filter_weight,
    decay_rate,
    skip_bias,
    output_grad,
):
    values, gate_first, gate_second, output_grad = (
        a[0] for a in (values, gate_first, gate_second, output_grad)
    )
    group = ("dp", "ctx")
    decay = decay_rate[None, :]
    sent = spread(values, gate_first, gate_second, output_grad, filter_features, filter_weight, decay)
    got = lax.all_to_all(sent, group, 0, 0, tiled=True)
    back = lax.all_to_all(spectral(got, decay), group, 0, 0, tiled=True)
    everywhere = ("dp", "chan", "ctx")
    groups = [[16 * z + j for z in range(16)] for j in range(16)]
    groups += [[256 + 16 * z + j for j in range(16)] for z in range(16)]

    def exchange(pieces):
        return lax.all_to_all(pieces, everywhere, 0, 0, axis_index_groups=groups, tiled=True)

    pieces = exchange(parts(back, filter_features, filter_weight))
    summed = jnp.sum(pieces.astype(jnp.float32), axis=0).astype(jnp.bfloat16)
    copies = exchange(jnp.broadcast_to(summed[None], (16, 16, 128)))
    back, copies = lax.optimization_barrier((back, copies))
    other = lax.ppermute(copies, "dp", [(0, 1), (1, 0)])
    outs = final(back, values, gate_first, gate_second, output_grad, skip_bias[None, :])
    feature_grad, weight_grad = assemble(copies, other)
    output, values_grad, first_grad, second_grad = (a[None] for a in outs)
    return (output, values_grad, first_grad, second_grad, weight_grad, feature_grad)


def solution(mesh):
    in_specs = (
        P("dp", "ctx", "chan"),
        P("dp", "ctx", "chan"),
        P("dp", "ctx", "chan"),
        P(None, "ctx"),
        P(None, "chan"),
        P("chan"),
        P("chan"),
        P("dp", "ctx", "chan"),
    )
    out_specs = (
        P("dp", "ctx", "chan"),
        P("dp", "ctx", "chan"),
        P("dp", "ctx", "chan"),
        P("dp", "ctx", "chan"),
        P(None, "chan"),
        P(None, "ctx"),
    )
    return jax.shard_map(local, mesh=mesh, in_specs=in_specs, out_specs=out_specs, check_vma=False)
```

```python
import functools
import math

import jax
import jax.numpy as jnp
import numpy as np
from jax import lax
from jax.experimental import pallas as pl
from jax.experimental.pallas import tpu as pltpu
from jax.sharding import PartitionSpec as P

LENGTH = 8192
PERIOD = 2 * LENGTH
TOK = 512
RADIX = 64
COLS = PERIOD // RADIX
BLOCKS = LENGTH // TOK
HALF = RADIX // 2 + 1
CH = 256
OWN = 8
GROUP = 32
ORDER = 64
TILE = 16
LANE = 128
CHUNKS = TOK // LANE
PAIRS = (HALF + 1) // 2
ROWS = 2 * HALF + PAIRS
VMEM_LIMIT = 24 * 1024 * 1024


def tables():
    grid = np.arange(COLS)
    angle = 2.0 * np.pi / COLS * (np.outer(grid, grid) % COLS)
    basis = np.concatenate([np.cos(angle), np.sin(angle)], axis=0).astype(jnp.bfloat16)
    turn = 2.0 * np.pi / PERIOD * np.outer(np.arange(HALF), grid)
    forward = np.stack([np.cos(turn), np.sin(turn)]).astype(np.float32)
    factor = 1.0 / (PERIOD * math.sqrt(LENGTH))
    inverse = (np.stack([np.cos(turn), np.sin(turn)]) * factor).astype(np.float32)
    return basis, forward, inverse


def add(a, b):
    if a is None:
        return b
    return a if b is None else a + b


def sub(a, b):
    if b is None:
        return a
    return -b if a is None else a - b


def neg(a):
    return None if a is None else -a


def rotate(value, index, period):
    real, imag = value
    if index == 0:
        return value
    if 4 * index == period:
        return imag, neg(real)
    c = math.cos(2 * math.pi * index / period)
    s = math.sin(2 * math.pi * index / period)
    if imag is None:
        return real * c, real * (-s)
    if 8 * index == period:
        return (real + imag) * c, (imag - real) * c
    return real * c + imag * s, imag * c - real * s


def rotate_back(value, index, period):
    real, imag = value
    if index == 0:
        return value
    if 4 * index == period:
        return neg(imag), real
    c = math.cos(2 * math.pi * index / period)
    s = math.sin(2 * math.pi * index / period)
    if 8 * index == period:
        return (real - imag) * c, (imag + real) * c
    return real * c - imag * s, imag * c + real * s


def real_dft(xs, n):
    if n == 2:
        return [(xs[0], None), (xs[0], None)]
    if n == 4:
        return [(xs[0] + xs[1], None), (xs[0], -xs[1]), (xs[0] - xs[1], None)]
    even = real_dft(xs[0::2], n // 2)
    odd = real_dft(xs[1::2], n // 2)
    out = [None] * (n // 2 + 1)
    for k in range(n // 4 + 1):
        t = rotate(odd[k], k, n)
        e = even[k]
        out[k] = (add(e[0], t[0]), add(e[1], t[1]))
        if 4 * k != n:
            out[n // 2 - k] = (sub(e[0], t[0]), sub(t[1], e[1]))
    return out


def real_inverse(spec, n):
    if n == 4:
        total = spec[0][0] + spec[2][0]
        diff = spec[0][0] - spec[2][0]
        return [total + 2.0 * spec[1][0], diff - 2.0 * spec[1][1]]
    even, odd = [], []
    for k in range(n // 4 + 1):
        a, b = spec[k], spec[n // 2 - k]
        if 4 * k == n:
            even.append((2.0 * a[0], None))
            odd.append((-2.0 * a[1], None))
            continue
        even.append((add(a[0], b[0]), sub(a[1], b[1])))
        odd.append(rotate_back((sub(a[0], b[0]), add(a[1], b[1])), k, n))
    first = real_inverse(even, n // 2)
    second = real_inverse(odd, n // 2)
    return [first[i // 2] if i % 2 == 0 else second[i // 2] for i in range(n // 2)]


def identity(size):
    row = lax.broadcasted_iota(jnp.int32, (size, size), 0)
    column = lax.broadcasted_iota(jnp.int32, (size, size), 1)
    return jnp.where(row == column, 1.0, 0.0).astype(jnp.bfloat16)


def turned_over(eye, block):
    return lax.dot_general(eye, block, (((1,), (1,)), ((), ())), preferred_element_type=jnp.float32)


def in_vmem(array):
    return pltpu.with_memory_space_constraint(array, pltpu.VMEM)


def in_hbm(array):
    return pltpu.with_memory_space_constraint(array, pltpu.HBM)


def spread_kernel(values, gate_first, gate_second, grad, features, weight, decay, ready):
    f32, bf16 = jnp.float32, jnp.bfloat16
    half = TOK // 2
    dp = lax.axis_index("dp")
    ctx = lax.axis_index("ctx")
    eye = identity(CH)
    mine = jnp.where(dp == 0, features[:, :half].astype(f32), features[:, half:].astype(f32))
    raw = lax.dot_general(
        mine.astype(bf16), weight[...], (((0,), (0,)), ((), ())), preferred_element_type=f32
    )
    first = ctx * TOK + dp * half
    positions = (first + lax.broadcasted_iota(jnp.int32, (half, 1), 0)).astype(f32) / LENGTH
    kernel = (raw * jnp.exp(-decay[...] * positions)).astype(bf16)
    kernel = turned_over(eye, kernel).reshape(GROUP, OWN, half)
    folded = jnp.concatenate([kernel[:, :, :LANE], kernel[:, :, LANE:]], axis=1)
    ready[:, CHUNKS * TILE :] = folded.astype(bf16)
    for part in range(2):
        rows = slice(part * half, (part + 1) * half)
        mixed = (values[rows].astype(f32) * gate_first[rows].astype(f32)).astype(bf16)
        scaled = (grad[rows].astype(f32) * gate_second[rows].astype(f32)).astype(bf16)
        mixed = turned_over(eye, mixed).reshape(GROUP, OWN, half)
        scaled = turned_over(eye, scaled).reshape(GROUP, OWN, half)
        both = jnp.concatenate([mixed, scaled], axis=1).astype(bf16)
        for c in range(2):
            row = (2 * part + c) * TILE
            ready[:, row : row + TILE] = both[:, :, c * LANE : (c + 1) * LANE]


def spread(values, gate_first, gate_second, grad, features, weight, decay, **kw):
    return pl.pallas_call(
        spread_kernel,
        out_shape=pltpu.VMEM((GROUP, (CHUNKS + 1) * TILE, LANE), jnp.bfloat16),
        in_specs=[pl.BlockSpec(memory_space=pltpu.VMEM)] * 7,
        out_specs=pl.BlockSpec(memory_space=pltpu.VMEM),
        compiler_params=pltpu.CompilerParams(vmem_limit_bytes=VMEM_LIMIT),
        name="spread",
        **kw,
    )(*(in_hbm(a) for a in (values, gate_first, gate_second, grad, features, weight, decay)))


def spectral_kernel(
    got, basis, forward, inverse, decay, out, lhs_re, lhs_im, res_re, res_im, rates
):
    f32, bf16 = jnp.float32, jnp.bfloat16
    rates[...] = jnp.broadcast_to(decay[...], (LANE, CH)).T
    first = (lax.axis_index("dp") * BLOCKS + lax.axis_index("ctx")) * OWN

    def lanes_of(chunk):
        return pl.ds(pl.multiple_of(chunk * LANE, LANE), LANE)

    def tile_of(chunk):
        return pl.ds(pl.multiple_of(chunk * TILE, TILE), TILE)

    def transformed(xs, lanes):
        turned = []
        for k, (real, imag) in enumerate(real_dft(xs, RADIX)):
            if k == 0:
                turned.append((real, jnp.zeros_like(real)))
                continue
            c = forward[0, k : k + 1, lanes]
            s = forward[1, k : k + 1, lanes]
            if imag is None:
                turned.append((real * c, -(real * s)))
            else:
                turned.append((real * c + imag * s, imag * c - real * s))
        return turned

    def joined(a, b):
        return jnp.concatenate([a, b], axis=0).astype(bf16)

    def signals_in(s, chunk):
        lanes = lanes_of(chunk)
        xs = [
            got[s * BLOCKS + j, tile_of(2 * h + chunk)].astype(f32)
            for j in range(BLOCKS)
            for h in range(2)
        ]
        low = transformed([x[:OWN] for x in xs], lanes)
        high = transformed([x[OWN:] for x in xs], lanes)
        for k in range(HALF):
            lhs_re[2 * k + s, :, lanes] = joined(low[k][0], high[k][0])
            lhs_im[2 * k + s, :, lanes] = joined(low[k][1], high[k][1])

    def sequence_in(s, carry):
        def chunk_in(chunk, inner):
            signals_in(s, chunk)
            return inner

        return lax.fori_loop(0, 2, chunk_in, carry)

    lax.fori_loop(0, 2, sequence_in, 0)

    blocks = [got[s * BLOCKS + j, CHUNKS * TILE :].astype(f32) for j in range(BLOCKS) for s in range(2)]
    for chunk in range(2):
        lanes = pl.ds(chunk * LANE, LANE)
        spec = transformed([x[chunk * OWN : (chunk + 1) * OWN] for x in blocks], lanes)
        spec.append((jnp.zeros_like(spec[0][0]),) * 2)
        for p in range(PAIRS):
            a, b = spec[2 * p], spec[2 * p + 1]
            lhs_re[2 * HALF + p, :, lanes] = joined(a[0], b[0])
            lhs_im[2 * HALF + p, :, lanes] = joined(a[1], b[1])

    def product(first, second):
        lhs = jnp.concatenate([first, second], axis=1)
        res = jnp.dot(lhs, basis[...], preferred_element_type=f32)
        return res.reshape(ROWS, TILE, COLS)

    real = lhs_re[...].reshape(ROWS * TILE, COLS)
    imag = lhs_im[...].reshape(ROWS * TILE, COLS)
    res_re[...] = product(real, imag)
    res_im[...] = product(imag, -real)

    def multiply(k, pair, rows):
        hr = res_re[2 * HALF + pair, rows, :]
        hi = res_im[2 * HALF + pair, rows, :]
        total_re, total_im = None, None
        for s in range(2):
            zr = res_re[2 * k + s, :OWN, :]
            zi = res_im[2 * k + s, :OWN, :]
            gr = res_re[2 * k + s, OWN:, :]
            gi = res_im[2 * k + s, OWN:, :]
            lhs_re[2 * k + s] = joined(zr * hr - zi * hi, gr * hr + gi * hi)
            lhs_im[2 * k + s] = joined(zr * hi + zi * hr, gi * hr - gr * hi)
            total_re = add(total_re, gr * zr + gi * zi)
            total_im = add(total_im, gi * zr - gr * zi)
        return total_re, total_im

    def multiply_pair(pair, carry):
        a = multiply(2 * pair, pair, slice(0, OWN))
        b = multiply(2 * pair + 1, pair, slice(OWN, TILE))
        lhs_re[2 * HALF + pair] = joined(a[0], b[0])
        lhs_im[2 * HALF + pair] = joined(a[1], b[1])
        return carry

    lax.fori_loop(0, PAIRS - 1, multiply_pair, 0, unroll=4)
    last = PAIRS - 1
    a = multiply(2 * last, last, slice(0, OWN))
    blank = jnp.zeros_like(a[0])
    lhs_re[2 * HALF + last] = joined(a[0], blank)
    lhs_im[2 * HALF + last] = joined(a[1], blank)

    real = lhs_re[...].reshape(ROWS * TILE, COLS)
    imag = lhs_im[...].reshape(ROWS * TILE, COLS)
    res_re[...] = product(real, -imag)
    res_im[...] = product(imag, real)

    def returned(spec, lanes):
        turned = []
        for k, (real, imag) in enumerate(spec):
            c = inverse[0, k : k + 1, lanes]
            s = inverse[1, k : k + 1, lanes]
            if k in (0, HALF - 1):
                turned.append((real * c - imag * s, None))
            else:
                turned.append((real * c - imag * s, imag * c + real * s))
        return real_inverse(turned, RADIX)

    rate = rates[pl.ds(pl.multiple_of(first, OWN), OWN), :]
    steps = [jnp.exp(-rate * (COLS * n / LENGTH)) for n in range(RADIX // 2)]
    ahead = lax.broadcasted_iota(jnp.int32, (OWN, LANE), 1).astype(f32)

    for chunk in range(2):
        lanes = pl.ds(chunk * LANE, LANE)
        spec = []
        for k in range(HALF):
            rows = slice(k % 2 * OWN, k % 2 * OWN + OWN)
            block = 2 * HALF + k // 2
            spec.append((res_re[block, rows, lanes], res_im[block, rows, lanes]))
        fine = jnp.exp(-rate * ((ahead + chunk * LANE) / LENGTH))
        pieces = [y * (fine * steps[n]) for n, y in enumerate(returned(spec, lanes))]
        row = (CHUNKS + chunk) * TILE
        for j in range(BLOCKS):
            both = joined(pieces[2 * j], pieces[2 * j + 1])
            out[j, row : row + TILE] = both
            out[BLOCKS + j, row : row + TILE] = both

    def sequence_out(s, carry):
        def chunk_out(chunk, inner):
            lanes = lanes_of(chunk)
            halves = []
            for rows in (slice(0, OWN), slice(OWN, TILE)):
                spec = [
                    (res_re[2 * k + s, rows, lanes], res_im[2 * k + s, rows, lanes]) for k in range(HALF)
                ]
                halves.append(returned(spec, lanes))
            for n in range(RADIX // 2):
                out[s * BLOCKS + n // 2, tile_of(n % 2 * 2 + chunk)] = joined(halves[0][n], halves[1][n])
            return inner

        lax.fori_loop(0, 2, chunk_out, 0)
        return carry

    lax.fori_loop(0, 2, sequence_out, 0)


def spectral(got, decay, **kw):
    basis, forward, inverse = (in_vmem(jnp.asarray(table)) for table in tables())
    wide = pltpu.VMEM((ROWS, TILE, COLS), jnp.bfloat16)
    result = pltpu.VMEM((ROWS, TILE, COLS), jnp.float32)
    return pl.pallas_call(
        spectral_kernel,
        out_shape=pltpu.VMEM((GROUP, (CHUNKS + 2) * TILE, LANE), jnp.bfloat16),
        in_specs=[pl.BlockSpec(memory_space=pltpu.VMEM)] * 5,
        out_specs=pl.BlockSpec(memory_space=pltpu.VMEM),
        scratch_shapes=[wide, wide, result, result, pltpu.VMEM((CH, LANE), jnp.float32)],
        compiler_params=pltpu.CompilerParams(vmem_limit_bytes=VMEM_LIMIT),
        name="spectral",
        **kw,
    )(in_vmem(got), basis, forward, inverse, in_vmem(decay))


def parts_kernel(back, features, weight, sums):
    f32, bf16 = jnp.float32, jnp.bfloat16
    half = TOK // 2
    first = CHUNKS * TILE
    is_feature = lax.axis_index("dp") == 0
    alongs, weight_sum = [], None
    for h in range(2):
        pieces = []
        for c in range(2):
            piece = back[:, first + c * TILE : first + (c + 1) * TILE].astype(f32)[:, h * OWN : (h + 1) * OWN]
            pieces.append(piece.reshape(CH, LANE))
        kernel_grad = jnp.concatenate(pieces, axis=1).astype(bf16)
        alongs.append(jnp.dot(weight[...], kernel_grad, preferred_element_type=f32))
        share = lax.dot_general(
            features[:, half * h : half * (h + 1)],
            kernel_grad,
            (((1,), (1,)), ((), ())),
            preferred_element_type=f32,
        )
        weight_sum = add(weight_sum, share)
    blank = jnp.zeros((8, LANE), f32)
    for piece in range(16):
        r, c = piece // 4, piece % 4
        feature = alongs[c // 2][16 * r : 16 * (r + 1), LANE * (c % 2) : LANE * (c % 2 + 1)]
        r, c = piece // 2, piece % 2
        other = weight_sum[8 * r : 8 * (r + 1), LANE * c : LANE * (c + 1)]
        other = jnp.concatenate([other, blank], axis=0)
        sums[piece] = jnp.where(is_feature, feature, other).astype(bf16)


def parts(back, features, weight, **kw):
    return pl.pallas_call(
        parts_kernel,
        out_shape=pltpu.VMEM((16, TILE, LANE), jnp.bfloat16),
        in_specs=[pl.BlockSpec(memory_space=pltpu.VMEM)] * 3,
        out_specs=pl.BlockSpec(memory_space=pltpu.VMEM),
        compiler_params=pltpu.CompilerParams(vmem_limit_bytes=VMEM_LIMIT),
        name="parts",
        **kw,
    )(in_vmem(back), in_vmem(features), in_vmem(weight))


def assemble_kernel(own, other, feature_grad, weight_grad):
    f32 = jnp.float32
    is_feature = lax.axis_index("dp") == 0
    for piece in range(16):
        a = own[piece].astype(f32)
        b = other[piece].astype(f32)
        feature = jnp.where(is_feature, a, b)
        weight = jnp.where(is_feature, b, a)[:8]
        r, c = piece // 4, piece % 4
        feature_grad[16 * r : 16 * (r + 1), 128 * c : 128 * (c + 1)] = feature
        r, c = piece // 2, piece % 2
        weight_grad[8 * r : 8 * (r + 1), 128 * c : 128 * (c + 1)] = weight


def assemble(own, other, **kw):
    return pl.pallas_call(
        assemble_kernel,
        out_shape=(
            jax.ShapeDtypeStruct((ORDER, TOK), jnp.float32),
            jax.ShapeDtypeStruct((ORDER, CH), jnp.float32),
        ),
        in_specs=[pl.BlockSpec(memory_space=pltpu.VMEM)] * 2,
        out_specs=(pl.BlockSpec(memory_space=pltpu.VMEM),) * 2,
        name="assemble",
        **kw,
    )(in_vmem(own), in_vmem(other))


def final_kernel(
    back, values, gate_first, gate_second, grad, skip, output, values_grad, first_grad, second_grad
):
    f32, bf16 = jnp.float32, jnp.bfloat16
    eye = identity(LANE)
    bias = skip[...]
    for chunk in range(CHUNKS):
        both = back[:, chunk * TILE : (chunk + 1) * TILE].astype(f32)
        conv = turned_over(eye, both[:, :OWN].reshape(CH, LANE).astype(bf16))
        grad_conv = turned_over(eye, both[:, OWN:].reshape(CH, LANE).astype(bf16))
        rows = slice(chunk * LANE, (chunk + 1) * LANE)
        x = values[rows].astype(f32)
        g1 = gate_first[rows].astype(f32)
        g2 = gate_second[rows].astype(f32)
        dy = grad[rows].astype(f32)
        total = conv + bias * (x * g1).astype(bf16).astype(f32)
        output[rows] = (g2 * total).astype(bf16)
        second_grad[rows] = (dy * total).astype(bf16)
        delta = grad_conv + bias * (dy * g2).astype(bf16).astype(f32)
        values_grad[rows] = (delta * g1).astype(bf16)
        first_grad[rows] = (delta * x).astype(bf16)


def final(back, values, gate_first, gate_second, grad, skip, **kw):
    shape = jax.ShapeDtypeStruct((TOK, CH), jnp.bfloat16)
    return pl.pallas_call(
        final_kernel,
        out_shape=(shape,) * 4,
        in_specs=[pl.BlockSpec(memory_space=pltpu.VMEM)] * 6,
        out_specs=(pl.BlockSpec(memory_space=pltpu.VMEM),) * 4,
        compiler_params=pltpu.CompilerParams(vmem_limit_bytes=VMEM_LIMIT),
        name="final",
        **kw,
    )(*(in_vmem(a) for a in (back, values, gate_first, gate_second, grad, skip)))


def local(
    values,
    gate_first,
    gate_second,
    filter_features,
    filter_weight,
    decay_rate,
    skip_bias,
    output_grad,
):
    values, gate_first, gate_second, output_grad = (
        a[0] for a in (values, gate_first, gate_second, output_grad)
    )
    group = ("dp", "ctx")
    decay = decay_rate[None, :]
    sent = spread(values, gate_first, gate_second, output_grad, filter_features, filter_weight, decay)
    got = lax.all_to_all(sent, group, 0, 0, tiled=True)
    back = lax.all_to_all(spectral(got, decay), group, 0, 0, tiled=True)
    everywhere = ("dp", "chan", "ctx")
    groups = [[16 * z + j for z in range(16)] for j in range(16)]
    groups += [[256 + 16 * z + j for j in range(16)] for z in range(16)]

    def exchange(pieces):
        return lax.all_to_all(pieces, everywhere, 0, 0, axis_index_groups=groups, tiled=True)

    pieces = exchange(parts(back, filter_features, filter_weight))
    summed = jnp.sum(pieces.astype(jnp.float32), axis=0).astype(jnp.bfloat16)
    copies = exchange(jnp.broadcast_to(summed[None], (16, 16, 128)))
    back, copies = lax.optimization_barrier((back, copies))
    other = lax.ppermute(copies, "dp", [(0, 1), (1, 0)])
    outs = final(back, values, gate_first, gate_second, output_grad, skip_bias[None, :])
    feature_grad, weight_grad = assemble(copies, other)
    output, values_grad, first_grad, second_grad = (a[None] for a in outs)
    return (output, values_grad, first_grad, second_grad, weight_grad, feature_grad)


def solution(mesh):
    in_specs = (
        P("dp", "ctx", "chan"),
        P("dp", "ctx", "chan"),
        P("dp", "ctx", "chan"),
        P(None, "ctx"),
        P(None, "chan"),
        P("chan"),
        P("chan"),
        P("dp", "ctx", "chan"),
    )
    out_specs = (
        P("dp", "ctx", "chan"),
        P("dp", "ctx", "chan"),
        P("dp", "ctx", "chan"),
        P("dp", "ctx", "chan"),
        P(None, "chan"),
        P(None, "ctx"),
    )
    return jax.shard_map(local, mesh=mesh, in_specs=in_specs, out_specs=out_specs, check_vma=False)
```

```python
import functools
import math

import jax
import jax.numpy as jnp
import numpy as np
from jax import lax
from jax.experimental import pallas as pl
from jax.experimental.pallas import tpu as pltpu
from jax.sharding import PartitionSpec as P

LENGTH = 8192
PERIOD = 2 * LENGTH
TOK = 512
RADIX = 64
COLS = PERIOD // RADIX
BLOCKS = LENGTH // TOK
HALF = RADIX // 2 + 1
CH = 256
OWN = 8
GROUP = 32
ORDER = 64
TILE = 16
LANE = 128
CHUNKS = TOK // LANE
PAIRS = (HALF + 1) // 2
ROWS = 2 * HALF + PAIRS
VMEM_LIMIT = 24 * 1024 * 1024


def tables():
    grid = np.arange(COLS)
    angle = 2.0 * np.pi / COLS * (np.outer(grid, grid) % COLS)
    basis = np.concatenate([np.cos(angle), np.sin(angle)], axis=0).astype(jnp.bfloat16)
    turn = 2.0 * np.pi / PERIOD * np.outer(np.arange(HALF), grid)
    forward = np.stack([np.cos(turn), np.sin(turn)]).astype(np.float32)
    factor = 1.0 / (PERIOD * math.sqrt(LENGTH))
    inverse = (np.stack([np.cos(turn), np.sin(turn)]) * factor).astype(np.float32)
    return basis, forward, inverse


def add(a, b):
    if a is None:
        return b
    return a if b is None else a + b


def sub(a, b):
    if b is None:
        return a
    return -b if a is None else a - b


def neg(a):
    return None if a is None else -a


def rotate(value, index, period):
    real, imag = value
    if index == 0:
        return value
    if 4 * index == period:
        return imag, neg(real)
    c = math.cos(2 * math.pi * index / period)
    s = math.sin(2 * math.pi * index / period)
    if imag is None:
        return real * c, real * (-s)
    if 8 * index == period:
        return (real + imag) * c, (imag - real) * c
    return real * c + imag * s, imag * c - real * s


def rotate_back(value, index, period):
    real, imag = value
    if index == 0:
        return value
    if 4 * index == period:
        return neg(imag), real
    c = math.cos(2 * math.pi * index / period)
    s = math.sin(2 * math.pi * index / period)
    if 8 * index == period:
        return (real - imag) * c, (imag + real) * c
    return real * c - imag * s, imag * c + real * s


def real_dft(xs, n):
    if n == 2:
        return [(xs[0], None), (xs[0], None)]
    if n == 4:
        return [(xs[0] + xs[1], None), (xs[0], -xs[1]), (xs[0] - xs[1], None)]
    even = real_dft(xs[0::2], n // 2)
    odd = real_dft(xs[1::2], n // 2)
    out = [None] * (n // 2 + 1)
    for k in range(n // 4 + 1):
        t = rotate(odd[k], k, n)
        e = even[k]
        out[k] = (add(e[0], t[0]), add(e[1], t[1]))
        if 4 * k != n:
            out[n // 2 - k] = (sub(e[0], t[0]), sub(t[1], e[1]))
    return out


def real_inverse(spec, n):
    if n == 4:
        total = spec[0][0] + spec[2][0]
        diff = spec[0][0] - spec[2][0]
        return [total + 2.0 * spec[1][0], diff - 2.0 * spec[1][1]]
    even, odd = [], []
    for k in range(n // 4 + 1):
        a, b = spec[k], spec[n // 2 - k]
        if 4 * k == n:
            even.append((2.0 * a[0], None))
            odd.append((-2.0 * a[1], None))
            continue
        even.append((add(a[0], b[0]), sub(a[1], b[1])))
        odd.append(rotate_back((sub(a[0], b[0]), add(a[1], b[1])), k, n))
    first = real_inverse(even, n // 2)
    second = real_inverse(odd, n // 2)
    return [first[i // 2] if i % 2 == 0 else second[i // 2] for i in range(n // 2)]


def identity(size):
    row = lax.broadcasted_iota(jnp.int32, (size, size), 0)
    column = lax.broadcasted_iota(jnp.int32, (size, size), 1)
    return jnp.where(row == column, 1.0, 0.0).astype(jnp.bfloat16)


def turned_over(eye, block):
    return lax.dot_general(eye, block, (((1,), (1,)), ((), ())), preferred_element_type=jnp.float32)


def in_vmem(array):
    return pltpu.with_memory_space_constraint(array, pltpu.VMEM)


def in_hbm(array):
    return pltpu.with_memory_space_constraint(array, pltpu.HBM)


def spread_kernel(values, gate_first, gate_second, grad, features, weight, decay, ready):
    f32, bf16 = jnp.float32, jnp.bfloat16
    half = TOK // 2
    dp = lax.axis_index("dp")
    ctx = lax.axis_index("ctx")
    eye = identity(CH)
    mine = jnp.where(dp == 0, features[:, :half].astype(f32), features[:, half:].astype(f32))
    raw = lax.dot_general(
        mine.astype(bf16), weight[...], (((0,), (0,)), ((), ())), preferred_element_type=f32
    )
    first = ctx * TOK + dp * half
    positions = (first + lax.broadcasted_iota(jnp.int32, (half, 1), 0)).astype(f32) / LENGTH
    kernel = (raw * jnp.exp(-decay[...] * positions)).astype(bf16)
    kernel = turned_over(eye, kernel).reshape(GROUP, OWN, half)
    folded = jnp.concatenate([kernel[:, :, :LANE], kernel[:, :, LANE:]], axis=1)
    ready[:, CHUNKS * TILE :] = folded.astype(bf16)
    for part in range(2):
        rows = slice(part * half, (part + 1) * half)
        mixed = (values[rows].astype(f32) * gate_first[rows].astype(f32)).astype(bf16)
        scaled = (grad[rows].astype(f32) * gate_second[rows].astype(f32)).astype(bf16)
        mixed = turned_over(eye, mixed).reshape(GROUP, OWN, half)
        scaled = turned_over(eye, scaled).reshape(GROUP, OWN, half)
        both = jnp.concatenate([mixed, scaled], axis=1).astype(bf16)
        for c in range(2):
            row = (2 * part + c) * TILE
            ready[:, row : row + TILE] = both[:, :, c * LANE : (c + 1) * LANE]


def spread(values, gate_first, gate_second, grad, features, weight, decay, **kw):
    return pl.pallas_call(
        spread_kernel,
        out_shape=pltpu.VMEM((GROUP, (CHUNKS + 1) * TILE, LANE), jnp.bfloat16),
        in_specs=[pl.BlockSpec(memory_space=pltpu.VMEM)] * 7,
        out_specs=pl.BlockSpec(memory_space=pltpu.VMEM),
        compiler_params=pltpu.CompilerParams(vmem_limit_bytes=VMEM_LIMIT),
        name="spread",
        **kw,
    )(*(in_hbm(a) for a in (values, gate_first, gate_second, grad, features, weight, decay)))


def spectral_kernel(
    got, basis, forward, inverse, decay, out, lhs_re, lhs_im, res_re, res_im, rates
):
    f32, bf16 = jnp.float32, jnp.bfloat16
    rates[...] = jnp.broadcast_to(decay[...], (LANE, CH)).T
    first = (lax.axis_index("dp") * BLOCKS + lax.axis_index("ctx")) * OWN

    def transformed(xs, lanes):
        turned = []
        for k, (real, imag) in enumerate(real_dft(xs, RADIX)):
            if k == 0:
                turned.append((real, jnp.zeros_like(real)))
                continue
            c = forward[0, k : k + 1, lanes]
            s = forward[1, k : k + 1, lanes]
            if imag is None:
                turned.append((real * c, -(real * s)))
            else:
                turned.append((real * c + imag * s, imag * c - real * s))
        return turned

    def joined(a, b):
        return jnp.concatenate([a, b], axis=0).astype(bf16)

    def place(s):
        return slice(s * HALF, (s + 1) * HALF)

    def signals_in(s, chunk):
        lanes = slice(chunk * LANE, (chunk + 1) * LANE)
        xs = [
            got[s * BLOCKS + j, (2 * h + chunk) * TILE : (2 * h + chunk + 1) * TILE].astype(f32)
            for j in range(BLOCKS)
            for h in range(2)
        ]
        low = transformed([x[:OWN] for x in xs], lanes)
        high = transformed([x[OWN:] for x in xs], lanes)
        for k in range(HALF):
            lhs_re[s * HALF + k, :, lanes] = joined(low[k][0], high[k][0])
            lhs_im[s * HALF + k, :, lanes] = joined(low[k][1], high[k][1])

    def kernel_in(chunk):
        xs = [
            got[s * BLOCKS + j, CHUNKS * TILE :].astype(f32)[chunk * OWN : (chunk + 1) * OWN]
            for j in range(BLOCKS)
            for s in range(2)
        ]
        lanes = slice(chunk * LANE, (chunk + 1) * LANE)
        spec = transformed(xs, lanes)
        spec.append((jnp.zeros_like(spec[0][0]),) * 2)
        for p in range(PAIRS):
            a, b = spec[2 * p], spec[2 * p + 1]
            lhs_re[2 * HALF + p, :, lanes] = joined(a[0], b[0])
            lhs_im[2 * HALF + p, :, lanes] = joined(a[1], b[1])

    def product(first, second):
        count = first.shape[0]
        lhs = jnp.concatenate([first, second], axis=2).reshape(count * TILE, 2 * COLS)
        res = jnp.dot(lhs, basis[...], preferred_element_type=f32)
        return res.reshape(count, TILE, COLS)

    def forth(tiles):
        real, imag = lhs_re[tiles], lhs_im[tiles]
        res_re[tiles] = product(real, imag)
        res_im[tiles] = product(imag, -real)

    def back(tiles):
        real, imag = lhs_re[tiles], lhs_im[tiles]
        res_re[tiles] = product(real, -imag)
        res_im[tiles] = product(imag, real)

    rest = slice(2 * HALF, ROWS)
    kernel_in(0)
    kernel_in(1)
    forth(rest)
    for s in range(2):
        signals_in(s, 0)
        signals_in(s, 1)
        forth(place(s))

    def multiply(k):
        pair, rows = k // 2, slice(k % 2 * OWN, k % 2 * OWN + OWN)
        hr = res_re[2 * HALF + pair, rows, :]
        hi = res_im[2 * HALF + pair, rows, :]
        total_re, total_im = None, None
        for s in range(2):
            tile = s * HALF + k
            zr = res_re[tile, :OWN, :]
            zi = res_im[tile, :OWN, :]
            gr = res_re[tile, OWN:, :]
            gi = res_im[tile, OWN:, :]
            lhs_re[tile] = joined(zr * hr - zi * hi, gr * hr + gi * hi)
            lhs_im[tile] = joined(zr * hi + zi * hr, gi * hr - gr * hi)
            total_re = add(total_re, gr * zr + gi * zi)
            total_im = add(total_im, gi * zr - gr * zi)
        return total_re, total_im

    for pair in range(PAIRS):
        a = multiply(2 * pair)
        if 2 * pair + 1 < HALF:
            b = multiply(2 * pair + 1)
        else:
            b = (jnp.zeros_like(a[0]),) * 2
        lhs_re[2 * HALF + pair] = joined(a[0], b[0])
        lhs_im[2 * HALF + pair] = joined(a[1], b[1])

    def returned(spec, lanes):
        turned = []
        for k, (real, imag) in enumerate(spec):
            c = inverse[0, k : k + 1, lanes]
            s = inverse[1, k : k + 1, lanes]
            if k in (0, HALF - 1):
                turned.append((real * c - imag * s, None))
            else:
                turned.append((real * c - imag * s, imag * c + real * s))
        return real_inverse(turned, RADIX)

    rate = rates[pl.ds(pl.multiple_of(first, OWN), OWN), :]
    steps = [jnp.exp(-rate * (COLS * n / LENGTH)) for n in range(RADIX // 2)]
    ahead = lax.broadcasted_iota(jnp.int32, (OWN, LANE), 1).astype(f32)

    def filter_out(chunk):
        lanes = slice(chunk * LANE, (chunk + 1) * LANE)
        spec = []
        for k in range(HALF):
            rows = slice(k % 2 * OWN, k % 2 * OWN + OWN)
            tile = 2 * HALF + k // 2
            spec.append((res_re[tile, rows, lanes], res_im[tile, rows, lanes]))
        fine = jnp.exp(-rate * ((ahead + chunk * LANE) / LENGTH))
        pieces = [y * (fine * steps[n]) for n, y in enumerate(returned(spec, lanes))]
        row = (CHUNKS + chunk) * TILE
        for j in range(BLOCKS):
            both = joined(pieces[2 * j], pieces[2 * j + 1])
            out[j, row : row + TILE] = both
            out[BLOCKS + j, row : row + TILE] = both

    def signals_out(s, chunk):
        lanes = slice(chunk * LANE, (chunk + 1) * LANE)
        halves = []
        for rows in (slice(0, OWN), slice(OWN, TILE)):
            spec = [
                (res_re[s * HALF + k, rows, lanes], res_im[s * HALF + k, rows, lanes])
                for k in range(HALF)
            ]
            halves.append(returned(spec, lanes))
        for n in range(RADIX // 2):
            row = (n % 2 * 2 + chunk) * TILE
            out[s * BLOCKS + n // 2, row : row + TILE] = joined(halves[0][n], halves[1][n])

    back(rest)
    back(place(0))
    filter_out(0)
    filter_out(1)
    back(place(1))
    for s in range(2):
        signals_out(s, 0)
        signals_out(s, 1)


def spectral(got, decay, **kw):
    basis, forward, inverse = (in_vmem(jnp.asarray(table)) for table in tables())
    wide = pltpu.VMEM((ROWS, TILE, COLS), jnp.bfloat16)
    result = pltpu.VMEM((ROWS, TILE, COLS), jnp.float32)
    return pl.pallas_call(
        spectral_kernel,
        out_shape=pltpu.VMEM((GROUP, (CHUNKS + 2) * TILE, LANE), jnp.bfloat16),
        in_specs=[pl.BlockSpec(memory_space=pltpu.VMEM)] * 5,
        out_specs=pl.BlockSpec(memory_space=pltpu.VMEM),
        scratch_shapes=[wide, wide, result, result, pltpu.VMEM((CH, LANE), jnp.float32)],
        compiler_params=pltpu.CompilerParams(vmem_limit_bytes=VMEM_LIMIT),
        name="spectral",
        **kw,
    )(in_vmem(got), basis, forward, inverse, in_vmem(decay))


def parts_kernel(back, features, weight, sums):
    f32, bf16 = jnp.float32, jnp.bfloat16
    half = TOK // 2
    first = CHUNKS * TILE
    is_feature = lax.axis_index("dp") == 0
    alongs, weight_sum = [], None
    for h in range(2):
        pieces = []
        for c in range(2):
            piece = back[:, first + c * TILE : first + (c + 1) * TILE].astype(f32)[:, h * OWN : (h + 1) * OWN]
            pieces.append(piece.reshape(CH, LANE))
        kernel_grad = jnp.concatenate(pieces, axis=1).astype(bf16)
        alongs.append(jnp.dot(weight[...], kernel_grad, preferred_element_type=f32))
        share = lax.dot_general(
            features[:, half * h : half * (h + 1)],
            kernel_grad,
            (((1,), (1,)), ((), ())),
            preferred_element_type=f32,
        )
        weight_sum = add(weight_sum, share)
    blank = jnp.zeros((8, LANE), f32)
    for piece in range(16):
        r, c = piece // 4, piece % 4
        feature = alongs[c // 2][16 * r : 16 * (r + 1), LANE * (c % 2) : LANE * (c % 2 + 1)]
        r, c = piece // 2, piece % 2
        other = weight_sum[8 * r : 8 * (r + 1), LANE * c : LANE * (c + 1)]
        other = jnp.concatenate([other, blank], axis=0)
        sums[piece] = jnp.where(is_feature, feature, other).astype(bf16)


def parts(back, features, weight, **kw):
    return pl.pallas_call(
        parts_kernel,
        out_shape=pltpu.VMEM((16, TILE, LANE), jnp.bfloat16),
        in_specs=[pl.BlockSpec(memory_space=pltpu.VMEM)] * 3,
        out_specs=pl.BlockSpec(memory_space=pltpu.VMEM),
        compiler_params=pltpu.CompilerParams(vmem_limit_bytes=VMEM_LIMIT),
        name="parts",
        **kw,
    )(in_vmem(back), in_vmem(features), in_vmem(weight))


def assemble_kernel(own, other, feature_grad, weight_grad):
    f32 = jnp.float32
    is_feature = lax.axis_index("dp") == 0
    for piece in range(16):
        a = own[piece].astype(f32)
        b = other[piece].astype(f32)
        feature = jnp.where(is_feature, a, b)
        weight = jnp.where(is_feature, b, a)[:8]
        r, c = piece // 4, piece % 4
        feature_grad[16 * r : 16 * (r + 1), 128 * c : 128 * (c + 1)] = feature
        r, c = piece // 2, piece % 2
        weight_grad[8 * r : 8 * (r + 1), 128 * c : 128 * (c + 1)] = weight


def assemble(own, other, **kw):
    return pl.pallas_call(
        assemble_kernel,
        out_shape=(
            jax.ShapeDtypeStruct((ORDER, TOK), jnp.float32),
            jax.ShapeDtypeStruct((ORDER, CH), jnp.float32),
        ),
        in_specs=[pl.BlockSpec(memory_space=pltpu.VMEM)] * 2,
        out_specs=(pl.BlockSpec(memory_space=pltpu.VMEM),) * 2,
        name="assemble",
        **kw,
    )(in_vmem(own), in_vmem(other))


def final_kernel(
    back, values, gate_first, gate_second, grad, skip, output, values_grad, first_grad, second_grad
):
    f32, bf16 = jnp.float32, jnp.bfloat16
    eye = identity(LANE)
    bias = skip[...]
    for chunk in range(CHUNKS):
        both = back[:, chunk * TILE : (chunk + 1) * TILE].astype(f32)
        conv = turned_over(eye, both[:, :OWN].reshape(CH, LANE).astype(bf16))
        grad_conv = turned_over(eye, both[:, OWN:].reshape(CH, LANE).astype(bf16))
        rows = slice(chunk * LANE, (chunk + 1) * LANE)
        x = values[rows].astype(f32)
        g1 = gate_first[rows].astype(f32)
        g2 = gate_second[rows].astype(f32)
        dy = grad[rows].astype(f32)
        total = conv + bias * (x * g1).astype(bf16).astype(f32)
        output[rows] = (g2 * total).astype(bf16)
        second_grad[rows] = (dy * total).astype(bf16)
        delta = grad_conv + bias * (dy * g2).astype(bf16).astype(f32)
        values_grad[rows] = (delta * g1).astype(bf16)
        first_grad[rows] = (delta * x).astype(bf16)


def final(back, values, gate_first, gate_second, grad, skip, **kw):
    shape = jax.ShapeDtypeStruct((TOK, CH), jnp.bfloat16)
    return pl.pallas_call(
        final_kernel,
        out_shape=(shape,) * 4,
        in_specs=[pl.BlockSpec(memory_space=pltpu.VMEM)] * 6,
        out_specs=(pl.BlockSpec(memory_space=pltpu.VMEM),) * 4,
        compiler_params=pltpu.CompilerParams(vmem_limit_bytes=VMEM_LIMIT),
        name="final",
        **kw,
    )(*(in_vmem(a) for a in (back, values, gate_first, gate_second, grad, skip)))


def local(
    values,
    gate_first,
    gate_second,
    filter_features,
    filter_weight,
    decay_rate,
    skip_bias,
    output_grad,
):
    values, gate_first, gate_second, output_grad = (
        a[0] for a in (values, gate_first, gate_second, output_grad)
    )
    group = ("dp", "ctx")
    decay = decay_rate[None, :]
    sent = spread(values, gate_first, gate_second, output_grad, filter_features, filter_weight, decay)
    got = lax.all_to_all(sent, group, 0, 0, tiled=True)
    back = lax.all_to_all(spectral(got, decay), group, 0, 0, tiled=True)
    everywhere = ("dp", "chan", "ctx")
    groups = [[16 * z + j for z in range(16)] for j in range(16)]
    groups += [[256 + 16 * z + j for j in range(16)] for z in range(16)]

    def exchange(pieces):
        return lax.all_to_all(pieces, everywhere, 0, 0, axis_index_groups=groups, tiled=True)

    pieces = exchange(parts(back, filter_features, filter_weight))
    summed = jnp.sum(pieces.astype(jnp.float32), axis=0).astype(jnp.bfloat16)
    copies = exchange(jnp.broadcast_to(summed[None], (16, 16, 128)))
    back, copies = lax.optimization_barrier((back, copies))
    other = lax.ppermute(copies, "dp", [(0, 1), (1, 0)])
    outs = final(back, values, gate_first, gate_second, output_grad, skip_bias[None, :])
    feature_grad, weight_grad = assemble(copies, other)
    output, values_grad, first_grad, second_grad = (a[None] for a in outs)
    return (output, values_grad, first_grad, second_grad, weight_grad, feature_grad)


def solution(mesh):
    in_specs = (
        P("dp", "ctx", "chan"),
        P("dp", "ctx", "chan"),
        P("dp", "ctx", "chan"),
        P(None, "ctx"),
        P(None, "chan"),
        P("chan"),
        P("chan"),
        P("dp", "ctx", "chan"),
    )
    out_specs = (
        P("dp", "ctx", "chan"),
        P("dp", "ctx", "chan"),
        P("dp", "ctx", "chan"),
        P("dp", "ctx", "chan"),
        P(None, "chan"),
        P(None, "ctx"),
    )
    return jax.shard_map(local, mesh=mesh, in_specs=in_specs, out_specs=out_specs, check_vma=False)
```

```python
import functools
import math

import jax
import jax.numpy as jnp
import numpy as np
from jax import lax
from jax.experimental import pallas as pl
from jax.experimental.pallas import tpu as pltpu
from jax.sharding import PartitionSpec as P

LENGTH = 8192
PERIOD = 2 * LENGTH
TOK = 512
RADIX = 64
COLS = PERIOD // RADIX
BLOCKS = LENGTH // TOK
HALF = RADIX // 2 + 1
CH = 256
OWN = 8
GROUP = 32
ORDER = 64
TILE = 16
LANE = 128
CHUNKS = TOK // LANE
QUAD = 4
PAIRS = (HALF + 1) // 2
ROWS = 2 * HALF + PAIRS
VMEM_LIMIT = 24 * 1024 * 1024


def tables():
    grid = np.arange(COLS)
    angle = 2.0 * np.pi / COLS * (np.outer(grid, grid) % COLS)
    basis = np.concatenate([np.cos(angle), np.sin(angle)], axis=0).astype(jnp.bfloat16)
    turn = 2.0 * np.pi / PERIOD * np.outer(np.arange(HALF), grid)
    forward = np.stack([np.cos(turn), np.sin(turn)]).astype(np.float32)
    factor = 1.0 / (PERIOD * math.sqrt(LENGTH))
    inverse = (np.stack([np.cos(turn), np.sin(turn)]) * factor).astype(np.float32)
    return basis, forward, inverse


def add(a, b):
    if a is None:
        return b
    return a if b is None else a + b


def sub(a, b):
    if b is None:
        return a
    return -b if a is None else a - b


def neg(a):
    return None if a is None else -a


def rotate(value, index, period):
    real, imag = value
    if index == 0:
        return value
    if 4 * index == period:
        return imag, neg(real)
    c = math.cos(2 * math.pi * index / period)
    s = math.sin(2 * math.pi * index / period)
    if imag is None:
        return real * c, real * (-s)
    if 8 * index == period:
        return (real + imag) * c, (imag - real) * c
    return real * c + imag * s, imag * c - real * s


def rotate_back(value, index, period):
    real, imag = value
    if index == 0:
        return value
    if 4 * index == period:
        return neg(imag), real
    c = math.cos(2 * math.pi * index / period)
    s = math.sin(2 * math.pi * index / period)
    if 8 * index == period:
        return (real - imag) * c, (imag + real) * c
    return real * c - imag * s, imag * c + real * s


def real_dft(xs, n):
    if n == 2:
        return [(xs[0], None), (xs[0], None)]
    if n == 4:
        return [(xs[0] + xs[1], None), (xs[0], -xs[1]), (xs[0] - xs[1], None)]
    even = real_dft(xs[0::2], n // 2)
    odd = real_dft(xs[1::2], n // 2)
    out = [None] * (n // 2 + 1)
    for k in range(n // 4 + 1):
        t = rotate(odd[k], k, n)
        e = even[k]
        out[k] = (add(e[0], t[0]), add(e[1], t[1]))
        if 4 * k != n:
            out[n // 2 - k] = (sub(e[0], t[0]), sub(t[1], e[1]))
    return out


def real_inverse(spec, n):
    if n == 4:
        total = spec[0][0] + spec[2][0]
        diff = spec[0][0] - spec[2][0]
        return [total + 2.0 * spec[1][0], diff - 2.0 * spec[1][1]]
    even, odd = [], []
    for k in range(n // 4 + 1):
        a, b = spec[k], spec[n // 2 - k]
        if 4 * k == n:
            even.append((2.0 * a[0], None))
            odd.append((-2.0 * a[1], None))
            continue
        even.append((add(a[0], b[0]), sub(a[1], b[1])))
        odd.append(rotate_back((sub(a[0], b[0]), add(a[1], b[1])), k, n))
    first = real_inverse(even, n // 2)
    second = real_inverse(odd, n // 2)
    return [first[i // 2] if i % 2 == 0 else second[i // 2] for i in range(n // 2)]


def identity(size):
    row = lax.broadcasted_iota(jnp.int32, (size, size), 0)
    column = lax.broadcasted_iota(jnp.int32, (size, size), 1)
    return jnp.where(row == column, 1.0, 0.0).astype(jnp.bfloat16)


def turned_over(eye, block):
    return lax.dot_general(eye, block, (((1,), (1,)), ((), ())), preferred_element_type=jnp.float32)


def in_vmem(array):
    return pltpu.with_memory_space_constraint(array, pltpu.VMEM)


def in_hbm(array):
    return pltpu.with_memory_space_constraint(array, pltpu.HBM)


def spread_kernel(values, gate_first, gate_second, grad, features, weight, decay, ready):
    f32, bf16 = jnp.float32, jnp.bfloat16
    half = TOK // 2
    dp = lax.axis_index("dp")
    ctx = lax.axis_index("ctx")
    eye = identity(CH)
    mine = jnp.where(dp == 0, features[:, :half].astype(f32), features[:, half:].astype(f32))
    raw = lax.dot_general(
        mine.astype(bf16), weight[...], (((0,), (0,)), ((), ())), preferred_element_type=f32
    )
    first = ctx * TOK + dp * half
    positions = (first + lax.broadcasted_iota(jnp.int32, (half, 1), 0)).astype(f32) / LENGTH
    kernel = (raw * jnp.exp(-decay[...] * positions)).astype(bf16)
    kernel = turned_over(eye, kernel).reshape(GROUP, OWN, half)
    folded = jnp.concatenate([kernel[:, :, :LANE], kernel[:, :, LANE:]], axis=1)
    ready[:, CHUNKS * TILE :] = folded.astype(bf16)
    for part in range(2):
        rows = slice(part * half, (part + 1) * half)
        mixed = (values[rows].astype(f32) * gate_first[rows].astype(f32)).astype(bf16)
        scaled = (grad[rows].astype(f32) * gate_second[rows].astype(f32)).astype(bf16)
        mixed = turned_over(eye, mixed).reshape(GROUP, OWN, half)
        scaled = turned_over(eye, scaled).reshape(GROUP, OWN, half)
        both = jnp.concatenate([mixed, scaled], axis=1).astype(bf16)
        for c in range(2):
            row = (2 * part + c) * TILE
            ready[:, row : row + TILE] = both[:, :, c * LANE : (c + 1) * LANE]


def spread(values, gate_first, gate_second, grad, features, weight, decay, **kw):
    return pl.pallas_call(
        spread_kernel,
        out_shape=pltpu.VMEM((GROUP, (CHUNKS + 1) * TILE, LANE), jnp.bfloat16),
        in_specs=[pl.BlockSpec(memory_space=pltpu.VMEM)] * 7,
        out_specs=pl.BlockSpec(memory_space=pltpu.VMEM),
        compiler_params=pltpu.CompilerParams(vmem_limit_bytes=VMEM_LIMIT),
        name="spread",
        **kw,
    )(*(in_hbm(a) for a in (values, gate_first, gate_second, grad, features, weight, decay)))


def spectral_kernel(
    got, basis, forward, inverse, decay, out, lhs_re, lhs_im, res_re, res_im, rates
):
    f32, bf16 = jnp.float32, jnp.bfloat16
    rates[...] = jnp.broadcast_to(decay[...], (LANE, CH)).T
    first = (lax.axis_index("dp") * BLOCKS + lax.axis_index("ctx")) * OWN

    def transformed(xs, lanes):
        turned = []
        for k, (real, imag) in enumerate(real_dft(xs, RADIX)):
            if k == 0:
                turned.append((real, jnp.zeros_like(real)))
                continue
            c = forward[0, k : k + 1, lanes]
            s = forward[1, k : k + 1, lanes]
            if imag is None:
                turned.append((real * c, -(real * s)))
            else:
                turned.append((real * c + imag * s, imag * c - real * s))
        return turned

    def joined(a, b):
        return jnp.concatenate([a, b], axis=0).astype(bf16)

    def place(s):
        return slice(s * HALF, (s + 1) * HALF)

    def signals_in(s, chunk):
        lanes = slice(chunk * LANE, (chunk + 1) * LANE)
        xs = [
            got[s * BLOCKS + j, (2 * h + chunk) * TILE : (2 * h + chunk + 1) * TILE].astype(f32)
            for j in range(BLOCKS)
            for h in range(2)
        ]
        low = transformed([x[:OWN] for x in xs], lanes)
        high = transformed([x[OWN:] for x in xs], lanes)
        for k in range(HALF):
            lhs_re[s * HALF + k, :, lanes] = joined(low[k][0], high[k][0])
            lhs_im[s * HALF + k, :, lanes] = joined(low[k][1], high[k][1])

    def kernel_in(chunk):
        xs = [
            got[s * BLOCKS + j, CHUNKS * TILE :].astype(f32)[chunk * OWN : (chunk + 1) * OWN]
            for j in range(BLOCKS)
            for s in range(2)
        ]
        lanes = slice(chunk * LANE, (chunk + 1) * LANE)
        spec = transformed(xs, lanes)
        spec.append((jnp.zeros_like(spec[0][0]),) * 2)
        for p in range(PAIRS):
            a, b = spec[2 * p], spec[2 * p + 1]
            lhs_re[2 * HALF + p, :, lanes] = joined(a[0], b[0])
            lhs_im[2 * HALF + p, :, lanes] = joined(a[1], b[1])

    def product(first, second):
        count = first.shape[0]
        lhs = jnp.concatenate([first, second], axis=2).reshape(count * TILE, 2 * COLS)
        res = jnp.dot(lhs, basis[...], preferred_element_type=f32)
        return res.reshape(count, TILE, COLS)

    def forth(tiles):
        real, imag = lhs_re[tiles], lhs_im[tiles]
        res_re[tiles] = product(real, imag)
        res_im[tiles] = product(imag, -real)

    def back(tiles):
        real, imag = lhs_re[tiles], lhs_im[tiles]
        res_re[tiles] = product(real, -imag)
        res_im[tiles] = product(imag, real)

    rest = slice(2 * HALF, ROWS)
    kernel_in(0)
    kernel_in(1)
    forth(rest)
    for s in range(2):
        signals_in(s, 0)
        signals_in(s, 1)
        forth(place(s))

    def multiply(k):
        pair, rows = k // 2, slice(k % 2 * OWN, k % 2 * OWN + OWN)
        hr = res_re[2 * HALF + pair, rows, :]
        hi = res_im[2 * HALF + pair, rows, :]
        total_re, total_im = None, None
        for s in range(2):
            tile = s * HALF + k
            zr = res_re[tile, :OWN, :]
            zi = res_im[tile, :OWN, :]
            gr = res_re[tile, OWN:, :]
            gi = res_im[tile, OWN:, :]
            lhs_re[tile] = joined(zr * hr - zi * hi, gr * hr + gi * hi)
            lhs_im[tile] = joined(zr * hi + zi * hr, gi * hr - gr * hi)
            total_re = add(total_re, gr * zr + gi * zi)
            total_im = add(total_im, gi * zr - gr * zi)
        return total_re, total_im

    for pair in range(PAIRS):
        a = multiply(2 * pair)
        if 2 * pair + 1 < HALF:
            b = multiply(2 * pair + 1)
        else:
            b = (jnp.zeros_like(a[0]),) * 2
        lhs_re[2 * HALF + pair] = joined(a[0], b[0])
        lhs_im[2 * HALF + pair] = joined(a[1], b[1])

    def returned(spec, lanes):
        turned = []
        for k, (real, imag) in enumerate(spec):
            c = inverse[0, k : k + 1, lanes]
            s = inverse[1, k : k + 1, lanes]
            if k in (0, HALF - 1):
                turned.append((real * c - imag * s, None))
            else:
                turned.append((real * c - imag * s, imag * c + real * s))
        return real_inverse(turned, RADIX)

    rate = rates[pl.ds(pl.multiple_of(first, OWN), OWN), :]
    steps = [jnp.exp(-rate * (COLS * n / LENGTH)) for n in range(RADIX // 2)]
    ahead = lax.broadcasted_iota(jnp.int32, (OWN, LANE), 1).astype(f32)

    def filter_out(chunk):
        lanes = slice(chunk * LANE, (chunk + 1) * LANE)
        spec = []
        for k in range(HALF):
            rows = slice(k % 2 * OWN, k % 2 * OWN + OWN)
            tile = 2 * HALF + k // 2
            spec.append((res_re[tile, rows, lanes], res_im[tile, rows, lanes]))
        fine = jnp.exp(-rate * ((ahead + chunk * LANE) / LENGTH))
        pieces = [y * (fine * steps[n]) for n, y in enumerate(returned(spec, lanes))]
        row = (CHUNKS + chunk) * TILE
        for j in range(BLOCKS):
            both = joined(pieces[2 * j], pieces[2 * j + 1])
            out[j, row : row + TILE] = both
            out[BLOCKS + j, row : row + TILE] = both

    def signals_out(s, chunk):
        lanes = slice(chunk * LANE, (chunk + 1) * LANE)
        halves = []
        for rows in (slice(0, OWN), slice(OWN, TILE)):
            spec = [
                (res_re[s * HALF + k, rows, lanes], res_im[s * HALF + k, rows, lanes])
                for k in range(HALF)
            ]
            halves.append(returned(spec, lanes))
        for n in range(RADIX // 2):
            row = (n % 2 * 2 + chunk) * TILE
            out[s * BLOCKS + n // 2, row : row + TILE] = joined(halves[0][n], halves[1][n])

    back(rest)
    back(place(0))
    filter_out(0)
    filter_out(1)
    back(place(1))
    for s in range(2):
        signals_out(s, 0)
        signals_out(s, 1)


def spectral(got, decay, **kw):
    basis, forward, inverse = (in_vmem(jnp.asarray(table)) for table in tables())
    wide = pltpu.VMEM((ROWS, TILE, COLS), jnp.bfloat16)
    result = pltpu.VMEM((ROWS, TILE, COLS), jnp.float32)
    return pl.pallas_call(
        spectral_kernel,
        out_shape=pltpu.VMEM((GROUP, (CHUNKS + 2) * TILE, LANE), jnp.bfloat16),
        in_specs=[pl.BlockSpec(memory_space=pltpu.VMEM)] * 5,
        out_specs=pl.BlockSpec(memory_space=pltpu.VMEM),
        scratch_shapes=[wide, wide, result, result, pltpu.VMEM((CH, LANE), jnp.float32)],
        compiler_params=pltpu.CompilerParams(vmem_limit_bytes=VMEM_LIMIT),
        name="spectral",
        **kw,
    )(in_vmem(got), basis, forward, inverse, in_vmem(decay))


def parts_kernel(back, features, weight, sums):
    f32, bf16 = jnp.float32, jnp.bfloat16
    half = TOK // 2
    first = CHUNKS * TILE
    is_feature = lax.axis_index("dp") == 0
    alongs, weight_sum = [], None
    for h in range(2):
        pieces = []
        for c in range(2):
            piece = back[:, first + c * TILE : first + (c + 1) * TILE].astype(f32)[:, h * OWN : (h + 1) * OWN]
            pieces.append(piece.reshape(CH, LANE))
        kernel_grad = jnp.concatenate(pieces, axis=1).astype(bf16)
        alongs.append(jnp.dot(weight[...], kernel_grad, preferred_element_type=f32))
        share = lax.dot_general(
            features[:, half * h : half * (h + 1)],
            kernel_grad,
            (((1,), (1,)), ((), ())),
            preferred_element_type=f32,
        )
        weight_sum = add(weight_sum, share)
    blank = jnp.zeros((ORDER - 2 * TILE, LANE), f32)
    for piece in range(QUAD):
        c = piece % 2
        feature = alongs[piece // 2][:, LANE * c : LANE * (c + 1)]
        rows = weight_sum[TILE * piece : TILE * (piece + 1)]
        other = jnp.concatenate([rows[:, :LANE], rows[:, LANE:], blank], axis=0)
        sums[piece] = jnp.where(is_feature, feature, other).astype(bf16)


def parts(back, features, weight, **kw):
    return pl.pallas_call(
        parts_kernel,
        out_shape=pltpu.VMEM((QUAD, ORDER, LANE), jnp.bfloat16),
        in_specs=[pl.BlockSpec(memory_space=pltpu.VMEM)] * 3,
        out_specs=pl.BlockSpec(memory_space=pltpu.VMEM),
        compiler_params=pltpu.CompilerParams(vmem_limit_bytes=VMEM_LIMIT),
        name="parts",
        **kw,
    )(in_vmem(back), in_vmem(features), in_vmem(weight))


def assemble_kernel(own, other, feature_grad, weight_grad):
    f32 = jnp.float32
    is_feature = lax.axis_index("dp") == 0
    for piece in range(QUAD):
        a = own[piece].astype(f32)
        b = other[piece].astype(f32)
        feature_grad[:, LANE * piece : LANE * (piece + 1)] = jnp.where(is_feature, a, b)
        rows = jnp.where(is_feature, b, a)
        weight = jnp.concatenate([rows[:TILE], rows[TILE : 2 * TILE]], axis=1)
        weight_grad[TILE * piece : TILE * (piece + 1)] = weight


def assemble(own, other, **kw):
    return pl.pallas_call(
        assemble_kernel,
        out_shape=(
            jax.ShapeDtypeStruct((ORDER, TOK), jnp.float32),
            jax.ShapeDtypeStruct((ORDER, CH), jnp.float32),
        ),
        in_specs=[pl.BlockSpec(memory_space=pltpu.VMEM)] * 2,
        out_specs=(pl.BlockSpec(memory_space=pltpu.VMEM),) * 2,
        name="assemble",
        **kw,
    )(in_vmem(own), in_vmem(other))


def final_kernel(
    back, values, gate_first, gate_second, grad, skip, output, values_grad, first_grad, second_grad
):
    f32, bf16 = jnp.float32, jnp.bfloat16
    eye = identity(LANE)
    bias = skip[...]
    for chunk in range(CHUNKS):
        both = back[:, chunk * TILE : (chunk + 1) * TILE].astype(f32)
        conv = turned_over(eye, both[:, :OWN].reshape(CH, LANE).astype(bf16))
        grad_conv = turned_over(eye, both[:, OWN:].reshape(CH, LANE).astype(bf16))
        rows = slice(chunk * LANE, (chunk + 1) * LANE)
        x = values[rows].astype(f32)
        g1 = gate_first[rows].astype(f32)
        g2 = gate_second[rows].astype(f32)
        dy = grad[rows].astype(f32)
        total = conv + bias * (x * g1).astype(bf16).astype(f32)
        output[rows] = (g2 * total).astype(bf16)
        second_grad[rows] = (dy * total).astype(bf16)
        delta = grad_conv + bias * (dy * g2).astype(bf16).astype(f32)
        values_grad[rows] = (delta * g1).astype(bf16)
        first_grad[rows] = (delta * x).astype(bf16)


def final(back, values, gate_first, gate_second, grad, skip, **kw):
    shape = jax.ShapeDtypeStruct((TOK, CH), jnp.bfloat16)
    return pl.pallas_call(
        final_kernel,
        out_shape=(shape,) * 4,
        in_specs=[pl.BlockSpec(memory_space=pltpu.VMEM)] * 6,
        out_specs=(pl.BlockSpec(memory_space=pltpu.VMEM),) * 4,
        compiler_params=pltpu.CompilerParams(vmem_limit_bytes=VMEM_LIMIT),
        name="final",
        **kw,
    )(*(in_vmem(a) for a in (back, values, gate_first, gate_second, grad, skip)))


EVERYWHERE = ("dp", "chan", "ctx")


def device(dp, chan, ctx):
    return dp * 256 + chan * 16 + ctx


def exchange(pieces):
    groups = []
    for other in range(16):
        for quad in range(4):
            groups.append([device(0, QUAD * quad + i, other) for i in range(QUAD)])
            groups.append([device(1, other, QUAD * quad + i) for i in range(QUAD)])
    return lax.all_to_all(pieces, EVERYWHERE, 0, 0, axis_index_groups=groups, tiled=True)


def rotate_quads(array, step):
    pairs = []
    for a in range(16):
        for b in range(16):
            after = (a + QUAD * step) % 16
            pairs.append((device(0, a, b), device(0, after, b)))
            pairs.append((device(1, b, a), device(1, b, after)))
    return lax.ppermute(array, EVERYWHERE, pairs)


def local(
    values,
    gate_first,
    gate_second,
    filter_features,
    filter_weight,
    decay_rate,
    skip_bias,
    output_grad,
):
    values, gate_first, gate_second, output_grad = (
        a[0] for a in (values, gate_first, gate_second, output_grad)
    )
    group = ("dp", "ctx")
    decay = decay_rate[None, :]
    sent = spread(values, gate_first, gate_second, output_grad, filter_features, filter_weight, decay)
    got = lax.all_to_all(sent, group, 0, 0, tiled=True)
    back = lax.all_to_all(spectral(got, decay), group, 0, 0, tiled=True)
    pieces = exchange(parts(back, filter_features, filter_weight))
    near = jnp.sum(pieces.astype(jnp.float32), axis=0)
    sent = near.astype(jnp.bfloat16)
    total = near
    for step in (1, 3, 2):
        total = total + rotate_quads(sent, step).astype(jnp.float32)
    copies = exchange(jnp.broadcast_to(total.astype(jnp.bfloat16)[None], (QUAD, ORDER, LANE)))
    back, copies = lax.optimization_barrier((back, copies))
    other = lax.ppermute(copies, "dp", [(0, 1), (1, 0)])
    outs = final(back, values, gate_first, gate_second, output_grad, skip_bias[None, :])
    feature_grad, weight_grad = assemble(copies, other)
    output, values_grad, first_grad, second_grad = (a[None] for a in outs)
    return (output, values_grad, first_grad, second_grad, weight_grad, feature_grad)


def solution(mesh):
    in_specs = (
        P("dp", "ctx", "chan"),
        P("dp", "ctx", "chan"),
        P("dp", "ctx", "chan"),
        P(None, "ctx"),
        P(None, "chan"),
        P("chan"),
        P("chan"),
        P("dp", "ctx", "chan"),
    )
    out_specs = (
        P("dp", "ctx", "chan"),
        P("dp", "ctx", "chan"),
        P("dp", "ctx", "chan"),
        P("dp", "ctx", "chan"),
        P(None, "chan"),
        P(None, "ctx"),
    )
    return jax.shard_map(local, mesh=mesh, in_specs=in_specs, out_specs=out_specs, check_vma=False)
```

```python
import functools
import math

import jax
import jax.numpy as jnp
import numpy as np
from jax import lax
from jax.experimental import pallas as pl
from jax.experimental.pallas import tpu as pltpu
from jax.sharding import PartitionSpec as P

LENGTH = 8192
PERIOD = 2 * LENGTH
TOK = 512
RADIX = 64
COLS = PERIOD // RADIX
BLOCKS = LENGTH // TOK
HALF = RADIX // 2 + 1
CH = 256
OWN = 8
GROUP = 32
ORDER = 64
TILE = 16
LANE = 128
CHUNKS = TOK // LANE
QUAD = 4
PAIRS = (HALF + 1) // 2
ROWS = 2 * HALF + PAIRS
VMEM_LIMIT = 24 * 1024 * 1024


def tables():
    grid = np.arange(COLS)
    angle = 2.0 * np.pi / COLS * (np.outer(grid, grid) % COLS)
    basis = np.concatenate([np.cos(angle), np.sin(angle)], axis=0).astype(jnp.bfloat16)
    turn = 2.0 * np.pi / PERIOD * np.outer(np.arange(HALF), grid)
    forward = np.stack([np.cos(turn), np.sin(turn)]).astype(np.float32)
    factor = 1.0 / (PERIOD * math.sqrt(LENGTH))
    inverse = (np.stack([np.cos(turn), np.sin(turn)]) * factor).astype(np.float32)
    return basis, forward, inverse


def add(a, b):
    if a is None:
        return b
    return a if b is None else a + b


def sub(a, b):
    if b is None:
        return a
    return -b if a is None else a - b


def neg(a):
    return None if a is None else -a


def rotate(value, index, period):
    real, imag = value
    if index == 0:
        return value
    if 4 * index == period:
        return imag, neg(real)
    c = math.cos(2 * math.pi * index / period)
    s = math.sin(2 * math.pi * index / period)
    if imag is None:
        return real * c, real * (-s)
    if 8 * index == period:
        return (real + imag) * c, (imag - real) * c
    return real * c + imag * s, imag * c - real * s


def rotate_back(value, index, period):
    real, imag = value
    if index == 0:
        return value
    if 4 * index == period:
        return neg(imag), real
    c = math.cos(2 * math.pi * index / period)
    s = math.sin(2 * math.pi * index / period)
    if 8 * index == period:
        return (real - imag) * c, (imag + real) * c
    return real * c - imag * s, imag * c + real * s


def real_dft(xs, n):
    if n == 2:
        return [(xs[0], None), (xs[0], None)]
    if n == 4:
        return [(xs[0] + xs[1], None), (xs[0], -xs[1]), (xs[0] - xs[1], None)]
    even = real_dft(xs[0::2], n // 2)
    odd = real_dft(xs[1::2], n // 2)
    out = [None] * (n // 2 + 1)
    for k in range(n // 4 + 1):
        t = rotate(odd[k], k, n)
        e = even[k]
        out[k] = (add(e[0], t[0]), add(e[1], t[1]))
        if 4 * k != n:
            out[n // 2 - k] = (sub(e[0], t[0]), sub(t[1], e[1]))
    return out


def real_inverse(spec, n):
    if n == 4:
        total = spec[0][0] + spec[2][0]
        diff = spec[0][0] - spec[2][0]
        return [total + 2.0 * spec[1][0], diff - 2.0 * spec[1][1]]
    even, odd = [], []
    for k in range(n // 4 + 1):
        a, b = spec[k], spec[n // 2 - k]
        if 4 * k == n:
            even.append((2.0 * a[0], None))
            odd.append((-2.0 * a[1], None))
            continue
        even.append((add(a[0], b[0]), sub(a[1], b[1])))
        odd.append(rotate_back((sub(a[0], b[0]), add(a[1], b[1])), k, n))
    first = real_inverse(even, n // 2)
    second = real_inverse(odd, n // 2)
    return [first[i // 2] if i % 2 == 0 else second[i // 2] for i in range(n // 2)]


def identity(size):
    row = lax.broadcasted_iota(jnp.int32, (size, size), 0)
    column = lax.broadcasted_iota(jnp.int32, (size, size), 1)
    return jnp.where(row == column, 1.0, 0.0).astype(jnp.bfloat16)


def turned_over(eye, block):
    return lax.dot_general(eye, block, (((1,), (1,)), ((), ())), preferred_element_type=jnp.float32)


def in_vmem(array):
    return pltpu.with_memory_space_constraint(array, pltpu.VMEM)


def in_hbm(array):
    return pltpu.with_memory_space_constraint(array, pltpu.HBM)


def spread_kernel(values, gate_first, gate_second, grad, features, weight, decay, ready):
    f32, bf16 = jnp.float32, jnp.bfloat16
    half = TOK // 2
    dp = lax.axis_index("dp")
    ctx = lax.axis_index("ctx")
    eye = identity(CH)
    mine = jnp.where(dp == 0, features[:, :half].astype(f32), features[:, half:].astype(f32))
    raw = lax.dot_general(
        mine.astype(bf16), weight[...], (((0,), (0,)), ((), ())), preferred_element_type=f32
    )
    first = ctx * TOK + dp * half
    positions = (first + lax.broadcasted_iota(jnp.int32, (half, 1), 0)).astype(f32) / LENGTH
    kernel = (raw * jnp.exp(-decay[...] * positions)).astype(bf16)
    kernel = turned_over(eye, kernel).reshape(GROUP, OWN, half)
    folded = jnp.concatenate([kernel[:, :, :LANE], kernel[:, :, LANE:]], axis=1)
    ready[:, CHUNKS * TILE :] = folded.astype(bf16)
    for part in range(2):
        rows = slice(part * half, (part + 1) * half)
        mixed = (values[rows].astype(f32) * gate_first[rows].astype(f32)).astype(bf16)
        scaled = (grad[rows].astype(f32) * gate_second[rows].astype(f32)).astype(bf16)
        mixed = turned_over(eye, mixed).reshape(GROUP, OWN, half)
        scaled = turned_over(eye, scaled).reshape(GROUP, OWN, half)
        both = jnp.concatenate([mixed, scaled], axis=1).astype(bf16)
        for c in range(2):
            row = (2 * part + c) * TILE
            ready[:, row : row + TILE] = both[:, :, c * LANE : (c + 1) * LANE]


def spread(values, gate_first, gate_second, grad, features, weight, decay, **kw):
    return pl.pallas_call(
        spread_kernel,
        out_shape=pltpu.VMEM((GROUP, (CHUNKS + 1) * TILE, LANE), jnp.bfloat16),
        in_specs=[pl.BlockSpec(memory_space=pltpu.VMEM)] * 7,
        out_specs=pl.BlockSpec(memory_space=pltpu.VMEM),
        compiler_params=pltpu.CompilerParams(vmem_limit_bytes=VMEM_LIMIT),
        name="spread",
        **kw,
    )(*(in_hbm(a) for a in (values, gate_first, gate_second, grad, features, weight, decay)))


def spectral_kernel(
    got, basis, forward, inverse, decay, out, lhs_re, lhs_im, res_re, res_im, rates
):
    f32, bf16 = jnp.float32, jnp.bfloat16
    rates[...] = jnp.broadcast_to(decay[...], (LANE, CH)).T
    first = (lax.axis_index("dp") * BLOCKS + lax.axis_index("ctx")) * OWN

    def transformed(xs, lanes):
        turned = []
        for k, (real, imag) in enumerate(real_dft(xs, RADIX)):
            if k == 0:
                turned.append((real, jnp.zeros_like(real)))
                continue
            c = forward[0, k : k + 1, lanes]
            s = forward[1, k : k + 1, lanes]
            if imag is None:
                turned.append((real * c, -(real * s)))
            else:
                turned.append((real * c + imag * s, imag * c - real * s))
        return turned

    def joined(a, b):
        return jnp.concatenate([a, b], axis=0).astype(bf16)

    def place(s):
        return slice(s * HALF, (s + 1) * HALF)

    def signals_in(s, chunk):
        lanes = slice(chunk * LANE, (chunk + 1) * LANE)
        xs = [
            got[s * BLOCKS + j, (2 * h + chunk) * TILE : (2 * h + chunk + 1) * TILE].astype(f32)
            for j in range(BLOCKS)
            for h in range(2)
        ]
        low = transformed([x[:OWN] for x in xs], lanes)
        high = transformed([x[OWN:] for x in xs], lanes)
        for k in range(HALF):
            lhs_re[s * HALF + k, :, lanes] = joined(low[k][0], high[k][0])
            lhs_im[s * HALF + k, :, lanes] = joined(low[k][1], high[k][1])

    def kernel_in(chunk):
        xs = [
            got[s * BLOCKS + j, CHUNKS * TILE :].astype(f32)[chunk * OWN : (chunk + 1) * OWN]
            for j in range(BLOCKS)
            for s in range(2)
        ]
        lanes = slice(chunk * LANE, (chunk + 1) * LANE)
        spec = transformed(xs, lanes)
        spec.append((jnp.zeros_like(spec[0][0]),) * 2)
        for p in range(PAIRS):
            a, b = spec[2 * p], spec[2 * p + 1]
            lhs_re[2 * HALF + p, :, lanes] = joined(a[0], b[0])
            lhs_im[2 * HALF + p, :, lanes] = joined(a[1], b[1])

    def product(first, second):
        count = first.shape[0]
        lhs = jnp.concatenate([first, second], axis=2).reshape(count * TILE, 2 * COLS)
        res = jnp.dot(lhs, basis[...], preferred_element_type=f32)
        return res.reshape(count, TILE, COLS)

    def forth(tiles):
        real, imag = lhs_re[tiles], lhs_im[tiles]
        res_re[tiles] = product(real, imag)
        res_im[tiles] = product(imag, -real)

    def back(tiles):
        real, imag = lhs_re[tiles], lhs_im[tiles]
        res_re[tiles] = product(real, -imag)
        res_im[tiles] = product(imag, real)

    rest = slice(2 * HALF, ROWS)
    kernel_in(0)
    kernel_in(1)
    forth(rest)
    for s in range(2):
        signals_in(s, 0)
        signals_in(s, 1)
        forth(place(s))

    def multiply(k):
        pair, rows = k // 2, slice(k % 2 * OWN, k % 2 * OWN + OWN)
        hr = res_re[2 * HALF + pair, rows, :]
        hi = res_im[2 * HALF + pair, rows, :]
        total_re, total_im = None, None
        for s in range(2):
            tile = s * HALF + k
            zr = res_re[tile, :OWN, :]
            zi = res_im[tile, :OWN, :]
            gr = res_re[tile, OWN:, :]
            gi = res_im[tile, OWN:, :]
            lhs_re[tile] = joined(zr * hr - zi * hi, gr * hr + gi * hi)
            lhs_im[tile] = joined(zr * hi + zi * hr, gi * hr - gr * hi)
            total_re = add(total_re, gr * zr + gi * zi)
            total_im = add(total_im, gi * zr - gr * zi)
        return total_re, total_im

    for pair in range(PAIRS):
        a = multiply(2 * pair)
        if 2 * pair + 1 < HALF:
            b = multiply(2 * pair + 1)
        else:
            b = (jnp.zeros_like(a[0]),) * 2
        lhs_re[2 * HALF + pair] = joined(a[0], b[0])
        lhs_im[2 * HALF + pair] = joined(a[1], b[1])

    def returned(spec, lanes):
        turned = []
        for k, (real, imag) in enumerate(spec):
            c = inverse[0, k : k + 1, lanes]
            s = inverse[1, k : k + 1, lanes]
            if k in (0, HALF - 1):
                turned.append((real * c - imag * s, None))
            else:
                turned.append((real * c - imag * s, imag * c + real * s))
        return real_inverse(turned, RADIX)

    rate = rates[pl.ds(pl.multiple_of(first, OWN), OWN), :]
    steps = [jnp.exp(-rate * (COLS * n / LENGTH)) for n in range(RADIX // 2)]
    ahead = lax.broadcasted_iota(jnp.int32, (OWN, LANE), 1).astype(f32)

    def filter_out(chunk):
        lanes = slice(chunk * LANE, (chunk + 1) * LANE)
        spec = []
        for k in range(HALF):
            rows = slice(k % 2 * OWN, k % 2 * OWN + OWN)
            tile = 2 * HALF + k // 2
            spec.append((res_re[tile, rows, lanes], res_im[tile, rows, lanes]))
        fine = jnp.exp(-rate * ((ahead + chunk * LANE) / LENGTH))
        pieces = [y * (fine * steps[n]) for n, y in enumerate(returned(spec, lanes))]
        row = (CHUNKS + chunk) * TILE
        for j in range(BLOCKS):
            both = joined(pieces[2 * j], pieces[2 * j + 1])
            out[j, row : row + TILE] = both
            out[BLOCKS + j, row : row + TILE] = both

    def signals_out(s, chunk):
        lanes = slice(chunk * LANE, (chunk + 1) * LANE)
        halves = []
        for rows in (slice(0, OWN), slice(OWN, TILE)):
            spec = [
                (res_re[s * HALF + k, rows, lanes], res_im[s * HALF + k, rows, lanes])
                for k in range(HALF)
            ]
            halves.append(returned(spec, lanes))
        for n in range(RADIX // 2):
            row = (n % 2 * 2 + chunk) * TILE
            out[s * BLOCKS + n // 2, row : row + TILE] = joined(halves[0][n], halves[1][n])

    back(rest)
    back(place(0))
    filter_out(0)
    filter_out(1)
    back(place(1))
    for s in range(2):
        signals_out(s, 0)
        signals_out(s, 1)


def spectral(got, decay, **kw):
    basis, forward, inverse = (in_vmem(jnp.asarray(table)) for table in tables())
    wide = pltpu.VMEM((ROWS, TILE, COLS), jnp.bfloat16)
    result = pltpu.VMEM((ROWS, TILE, COLS), jnp.float32)
    return pl.pallas_call(
        spectral_kernel,
        out_shape=pltpu.VMEM((GROUP, (CHUNKS + 2) * TILE, LANE), jnp.bfloat16),
        in_specs=[pl.BlockSpec(memory_space=pltpu.VMEM)] * 5,
        out_specs=pl.BlockSpec(memory_space=pltpu.VMEM),
        scratch_shapes=[wide, wide, result, result, pltpu.VMEM((CH, LANE), jnp.float32)],
        compiler_params=pltpu.CompilerParams(vmem_limit_bytes=VMEM_LIMIT),
        name="spectral",
        **kw,
    )(in_vmem(got), basis, forward, inverse, in_vmem(decay))


def parts_kernel(back, features, weight, sums):
    f32, bf16 = jnp.float32, jnp.bfloat16
    half = TOK // 2
    first = CHUNKS * TILE
    is_feature = lax.axis_index("dp") == 0
    alongs, weight_sum = [], None
    for h in range(2):
        pieces = []
        for c in range(2):
            piece = back[:, first + c * TILE : first + (c + 1) * TILE].astype(f32)[:, h * OWN : (h + 1) * OWN]
            pieces.append(piece.reshape(CH, LANE))
        kernel_grad = jnp.concatenate(pieces, axis=1).astype(bf16)
        alongs.append(jnp.dot(weight[...], kernel_grad, preferred_element_type=f32))
        share = lax.dot_general(
            features[:, half * h : half * (h + 1)],
            kernel_grad,
            (((1,), (1,)), ((), ())),
            preferred_element_type=f32,
        )
        weight_sum = add(weight_sum, share)
    blank = jnp.zeros((ORDER - 2 * TILE, LANE), f32)
    for piece in range(QUAD):
        c = piece % 2
        feature = alongs[piece // 2][:, LANE * c : LANE * (c + 1)]
        rows = weight_sum[TILE * piece : TILE * (piece + 1)]
        other = jnp.concatenate([rows[:, :LANE], rows[:, LANE:], blank], axis=0)
        sums[piece] = jnp.where(is_feature, feature, other).astype(bf16)


def parts(back, features, weight, **kw):
    return pl.pallas_call(
        parts_kernel,
        out_shape=pltpu.VMEM((QUAD, ORDER, LANE), jnp.bfloat16),
        in_specs=[pl.BlockSpec(memory_space=pltpu.VMEM)] * 3,
        out_specs=pl.BlockSpec(memory_space=pltpu.VMEM),
        compiler_params=pltpu.CompilerParams(vmem_limit_bytes=VMEM_LIMIT),
        name="parts",
        **kw,
    )(in_vmem(back), in_vmem(features), in_vmem(weight))


def assemble_kernel(own, other, feature_grad, weight_grad):
    f32 = jnp.float32
    is_feature = lax.axis_index("dp") == 0
    for piece in range(QUAD):
        a = own[piece].astype(f32)
        b = other[piece].astype(f32)
        feature_grad[:, LANE * piece : LANE * (piece + 1)] = jnp.where(is_feature, a, b)
        rows = jnp.where(is_feature, b, a)
        weight = jnp.concatenate([rows[:TILE], rows[TILE : 2 * TILE]], axis=1)
        weight_grad[TILE * piece : TILE * (piece + 1)] = weight


def assemble(own, other, **kw):
    return pl.pallas_call(
        assemble_kernel,
        out_shape=(
            jax.ShapeDtypeStruct((ORDER, TOK), jnp.float32),
            jax.ShapeDtypeStruct((ORDER, CH), jnp.float32),
        ),
        in_specs=[pl.BlockSpec(memory_space=pltpu.VMEM)] * 2,
        out_specs=(pl.BlockSpec(memory_space=pltpu.VMEM),) * 2,
        name="assemble",
        **kw,
    )(in_vmem(own), in_vmem(other))


def final_kernel(
    back, values, gate_first, gate_second, grad, skip, output, values_grad, first_grad, second_grad
):
    f32, bf16 = jnp.float32, jnp.bfloat16
    eye = identity(LANE)
    bias = skip[...]
    for chunk in range(CHUNKS):
        both = back[:, chunk * TILE : (chunk + 1) * TILE].astype(f32)
        conv = turned_over(eye, both[:, :OWN].reshape(CH, LANE).astype(bf16))
        grad_conv = turned_over(eye, both[:, OWN:].reshape(CH, LANE).astype(bf16))
        rows = slice(chunk * LANE, (chunk + 1) * LANE)
        x = values[rows].astype(f32)
        g1 = gate_first[rows].astype(f32)
        g2 = gate_second[rows].astype(f32)
        dy = grad[rows].astype(f32)
        total = conv + bias * (x * g1).astype(bf16).astype(f32)
        output[rows] = (g2 * total).astype(bf16)
        second_grad[rows] = (dy * total).astype(bf16)
        delta = grad_conv + bias * (dy * g2).astype(bf16).astype(f32)
        values_grad[rows] = (delta * g1).astype(bf16)
        first_grad[rows] = (delta * x).astype(bf16)


def final(back, values, gate_first, gate_second, grad, skip, **kw):
    shape = jax.ShapeDtypeStruct((TOK, CH), jnp.bfloat16)
    return pl.pallas_call(
        final_kernel,
        out_shape=(shape,) * 4,
        in_specs=[pl.BlockSpec(memory_space=pltpu.VMEM)] * 6,
        out_specs=(pl.BlockSpec(memory_space=pltpu.VMEM),) * 4,
        compiler_params=pltpu.CompilerParams(vmem_limit_bytes=VMEM_LIMIT),
        name="final",
        **kw,
    )(*(in_vmem(a) for a in (back, values, gate_first, gate_second, grad, skip)))


EVERYWHERE = ("dp", "chan", "ctx")


def device(dp, chan, ctx):
    return dp * 256 + chan * 16 + ctx


def exchange(pieces):
    groups = []
    for other in range(16):
        for quad in range(4):
            groups.append([device(0, QUAD * quad + i, other) for i in range(QUAD)])
            groups.append([device(1, other, QUAD * quad + i) for i in range(QUAD)])
    return lax.all_to_all(pieces, EVERYWHERE, 0, 0, axis_index_groups=groups, tiled=True)


def swap(array, distance):
    pairs = []
    for a in range(16):
        for b in range(16):
            pairs.append((device(0, a, b), device(0, a ^ distance, b)))
            pairs.append((device(1, b, a), device(1, b, a ^ distance)))
    return lax.ppermute(array, EVERYWHERE, pairs)


def local(
    values,
    gate_first,
    gate_second,
    filter_features,
    filter_weight,
    decay_rate,
    skip_bias,
    output_grad,
):
    values, gate_first, gate_second, output_grad = (
        a[0] for a in (values, gate_first, gate_second, output_grad)
    )
    group = ("dp", "ctx")
    decay = decay_rate[None, :]
    sent = spread(values, gate_first, gate_second, output_grad, filter_features, filter_weight, decay)
    got = lax.all_to_all(sent, group, 0, 0, tiled=True)
    back = lax.all_to_all(spectral(got, decay), group, 0, 0, tiled=True)
    pieces = exchange(parts(back, filter_features, filter_weight))
    total = jnp.sum(pieces.astype(jnp.float32), axis=0)
    for distance in (8, 4):
        sent = total.astype(jnp.bfloat16)
        total = sent.astype(jnp.float32) + swap(sent, distance).astype(jnp.float32)
    copies = exchange(jnp.broadcast_to(total.astype(jnp.bfloat16)[None], (QUAD, ORDER, LANE)))
    back, copies = lax.optimization_barrier((back, copies))
    other = lax.ppermute(copies, "dp", [(0, 1), (1, 0)])
    outs = final(back, values, gate_first, gate_second, output_grad, skip_bias[None, :])
    feature_grad, weight_grad = assemble(copies, other)
    output, values_grad, first_grad, second_grad = (a[None] for a in outs)
    return (output, values_grad, first_grad, second_grad, weight_grad, feature_grad)


def solution(mesh):
    in_specs = (
        P("dp", "ctx", "chan"),
        P("dp", "ctx", "chan"),
        P("dp", "ctx", "chan"),
        P(None, "ctx"),
        P(None, "chan"),
        P("chan"),
        P("chan"),
        P("dp", "ctx", "chan"),
    )
    out_specs = (
        P("dp", "ctx", "chan"),
        P("dp", "ctx", "chan"),
        P("dp", "ctx", "chan"),
        P("dp", "ctx", "chan"),
        P(None, "chan"),
        P(None, "ctx"),
    )
    return jax.shard_map(local, mesh=mesh, in_specs=in_specs, out_specs=out_specs, check_vma=False)
```

```python
import functools
import math

import jax
import jax.numpy as jnp
import numpy as np
from jax import lax
from jax.experimental import pallas as pl
from jax.experimental.pallas import tpu as pltpu
from jax.sharding import PartitionSpec as P

LENGTH = 8192
PERIOD = 2 * LENGTH
TOK = 512
RADIX = 64
COLS = PERIOD // RADIX
BLOCKS = LENGTH // TOK
HALF = RADIX // 2 + 1
CH = 256
OWN = 8
GROUP = 32
ORDER = 64
TILE = 16
LANE = 128
CHUNKS = TOK // LANE
PAIRS = (HALF + 1) // 2
ROWS = 2 * HALF + PAIRS
FIRST_CHAN = 9
LEADER = 25
VMEM_LIMIT = 24 * 1024 * 1024


def seat(member):
    return {0: LEADER, LEADER: 0}.get(member, member)


def tables():
    grid = np.arange(COLS)
    angle = 2.0 * np.pi / COLS * (np.outer(grid, grid) % COLS)
    basis = np.concatenate([np.cos(angle), np.sin(angle)], axis=0).astype(jnp.bfloat16)
    turn = 2.0 * np.pi / PERIOD * np.outer(np.arange(HALF), grid)
    forward = np.stack([np.cos(turn), np.sin(turn)]).astype(np.float32)
    factor = 1.0 / (PERIOD * math.sqrt(LENGTH))
    inverse = (np.stack([np.cos(turn), np.sin(turn)]) * factor).astype(np.float32)
    return basis, forward, inverse


def add(a, b):
    if a is None:
        return b
    return a if b is None else a + b


def sub(a, b):
    if b is None:
        return a
    return -b if a is None else a - b


def neg(a):
    return None if a is None else -a


def rotate(value, index, period):
    real, imag = value
    if index == 0:
        return value
    if 4 * index == period:
        return imag, neg(real)
    c = math.cos(2 * math.pi * index / period)
    s = math.sin(2 * math.pi * index / period)
    if imag is None:
        return real * c, real * (-s)
    if 8 * index == period:
        return (real + imag) * c, (imag - real) * c
    return real * c + imag * s, imag * c - real * s


def rotate_back(value, index, period):
    real, imag = value
    if index == 0:
        return value
    if 4 * index == period:
        return neg(imag), real
    c = math.cos(2 * math.pi * index / period)
    s = math.sin(2 * math.pi * index / period)
    if 8 * index == period:
        return (real - imag) * c, (imag + real) * c
    return real * c - imag * s, imag * c + real * s


def real_dft(xs, n):
    if n == 2:
        return [(xs[0], None), (xs[0], None)]
    if n == 4:
        return [(xs[0] + xs[1], None), (xs[0], -xs[1]), (xs[0] - xs[1], None)]
    even = real_dft(xs[0::2], n // 2)
    odd = real_dft(xs[1::2], n // 2)
    out = [None] * (n // 2 + 1)
    for k in range(n // 4 + 1):
        t = rotate(odd[k], k, n)
        e = even[k]
        out[k] = (add(e[0], t[0]), add(e[1], t[1]))
        if 4 * k != n:
            out[n // 2 - k] = (sub(e[0], t[0]), sub(t[1], e[1]))
    return out


def real_inverse(spec, n):
    if n == 4:
        total = spec[0][0] + spec[2][0]
        diff = spec[0][0] - spec[2][0]
        return [total + 2.0 * spec[1][0], diff - 2.0 * spec[1][1]]
    even, odd = [], []
    for k in range(n // 4 + 1):
        a, b = spec[k], spec[n // 2 - k]
        if 4 * k == n:
            even.append((2.0 * a[0], None))
            odd.append((-2.0 * a[1], None))
            continue
        even.append((add(a[0], b[0]), sub(a[1], b[1])))
        odd.append(rotate_back((sub(a[0], b[0]), add(a[1], b[1])), k, n))
    first = real_inverse(even, n // 2)
    second = real_inverse(odd, n // 2)
    return [first[i // 2] if i % 2 == 0 else second[i // 2] for i in range(n // 2)]


def identity(size):
    row = lax.broadcasted_iota(jnp.int32, (size, size), 0)
    column = lax.broadcasted_iota(jnp.int32, (size, size), 1)
    return jnp.where(row == column, 1.0, 0.0).astype(jnp.bfloat16)


def turned_over(eye, block):
    return lax.dot_general(eye, block, (((1,), (1,)), ((), ())), preferred_element_type=jnp.float32)


def in_vmem(array):
    return pltpu.with_memory_space_constraint(array, pltpu.VMEM)


def in_hbm(array):
    return pltpu.with_memory_space_constraint(array, pltpu.HBM)


def spread_kernel(values, gate_first, gate_second, grad, features, weight, decay, ready):
    f32, bf16 = jnp.float32, jnp.bfloat16
    half = TOK // 2
    dp = lax.axis_index("dp")
    ctx = lax.axis_index("ctx")
    eye = identity(CH)
    mine = jnp.where(dp == 0, features[:, :half].astype(f32), features[:, half:].astype(f32))
    raw = lax.dot_general(
        mine.astype(bf16), weight[...], (((0,), (0,)), ((), ())), preferred_element_type=f32
    )
    first = ctx * TOK + dp * half
    positions = (first + lax.broadcasted_iota(jnp.int32, (half, 1), 0)).astype(f32) / LENGTH
    kernel = (raw * jnp.exp(-decay[...] * positions)).astype(bf16)
    kernel = turned_over(eye, kernel).reshape(GROUP, OWN, half)
    folded = jnp.concatenate([kernel[:, :, :LANE], kernel[:, :, LANE:]], axis=1)
    ready[:, CHUNKS * TILE :] = folded.astype(bf16)
    for part in range(2):
        rows = slice(part * half, (part + 1) * half)
        mixed = (values[rows].astype(f32) * gate_first[rows].astype(f32)).astype(bf16)
        scaled = (grad[rows].astype(f32) * gate_second[rows].astype(f32)).astype(bf16)
        mixed = turned_over(eye, mixed).reshape(GROUP, OWN, half)
        scaled = turned_over(eye, scaled).reshape(GROUP, OWN, half)
        both = jnp.concatenate([mixed, scaled], axis=1).astype(bf16)
        for c in range(2):
            row = (2 * part + c) * TILE
            ready[:, row : row + TILE] = both[:, :, c * LANE : (c + 1) * LANE]


def spread(values, gate_first, gate_second, grad, features, weight, decay, **kw):
    return pl.pallas_call(
        spread_kernel,
        out_shape=pltpu.VMEM((GROUP, (CHUNKS + 1) * TILE, LANE), jnp.bfloat16),
        in_specs=[pl.BlockSpec(memory_space=pltpu.VMEM)] * 7,
        out_specs=pl.BlockSpec(memory_space=pltpu.VMEM),
        compiler_params=pltpu.CompilerParams(vmem_limit_bytes=VMEM_LIMIT),
        name="spread",
        **kw,
    )(*(in_hbm(a) for a in (values, gate_first, gate_second, grad, features, weight, decay)))


def spectral_kernel(
    got, basis, forward, inverse, decay, out, lhs_re, lhs_im, res_re, res_im, rates
):
    f32, bf16 = jnp.float32, jnp.bfloat16
    rates[...] = jnp.broadcast_to(decay[...], (LANE, CH)).T
    member = lax.axis_index("dp") * BLOCKS + lax.axis_index("ctx")
    place_of = jnp.where(member == 0, LEADER, jnp.where(member == LEADER, 0, member))
    first = place_of * OWN

    def transformed(xs, lanes):
        turned = []
        for k, (real, imag) in enumerate(real_dft(xs, RADIX)):
            if k == 0:
                turned.append((real, jnp.zeros_like(real)))
                continue
            c = forward[0, k : k + 1, lanes]
            s = forward[1, k : k + 1, lanes]
            if imag is None:
                turned.append((real * c, -(real * s)))
            else:
                turned.append((real * c + imag * s, imag * c - real * s))
        return turned

    def joined(a, b):
        return jnp.concatenate([a, b], axis=0).astype(bf16)

    def place(s):
        return slice(s * HALF, (s + 1) * HALF)

    def signals_in(s, chunk):
        lanes = slice(chunk * LANE, (chunk + 1) * LANE)
        xs = [
            got[seat(s * BLOCKS + j), (2 * h + chunk) * TILE : (2 * h + chunk + 1) * TILE].astype(f32)
            for j in range(BLOCKS)
            for h in range(2)
        ]
        low = transformed([x[:OWN] for x in xs], lanes)
        high = transformed([x[OWN:] for x in xs], lanes)
        for k in range(HALF):
            lhs_re[s * HALF + k, :, lanes] = joined(low[k][0], high[k][0])
            lhs_im[s * HALF + k, :, lanes] = joined(low[k][1], high[k][1])

    def kernel_in(chunk):
        xs = [
            got[seat(s * BLOCKS + j), CHUNKS * TILE :].astype(f32)[chunk * OWN : (chunk + 1) * OWN]
            for j in range(BLOCKS)
            for s in range(2)
        ]
        lanes = slice(chunk * LANE, (chunk + 1) * LANE)
        spec = transformed(xs, lanes)
        spec.append((jnp.zeros_like(spec[0][0]),) * 2)
        for p in range(PAIRS):
            a, b = spec[2 * p], spec[2 * p + 1]
            lhs_re[2 * HALF + p, :, lanes] = joined(a[0], b[0])
            lhs_im[2 * HALF + p, :, lanes] = joined(a[1], b[1])

    def product(first, second):
        count = first.shape[0]
        lhs = jnp.concatenate([first, second], axis=2).reshape(count * TILE, 2 * COLS)
        res = jnp.dot(lhs, basis[...], preferred_element_type=f32)
        return res.reshape(count, TILE, COLS)

    def forth(tiles):
        real, imag = lhs_re[tiles], lhs_im[tiles]
        res_re[tiles] = product(real, imag)
        res_im[tiles] = product(imag, -real)

    def back(tiles):
        real, imag = lhs_re[tiles], lhs_im[tiles]
        res_re[tiles] = product(real, -imag)
        res_im[tiles] = product(imag, real)

    rest = slice(2 * HALF, ROWS)
    kernel_in(0)
    kernel_in(1)
    forth(rest)
    for s in range(2):
        signals_in(s, 0)
        signals_in(s, 1)
        forth(place(s))

    def multiply(k):
        pair, rows = k // 2, slice(k % 2 * OWN, k % 2 * OWN + OWN)
        hr = res_re[2 * HALF + pair, rows, :]
        hi = res_im[2 * HALF + pair, rows, :]
        total_re, total_im = None, None
        for s in range(2):
            tile = s * HALF + k
            zr = res_re[tile, :OWN, :]
            zi = res_im[tile, :OWN, :]
            gr = res_re[tile, OWN:, :]
            gi = res_im[tile, OWN:, :]
            lhs_re[tile] = joined(zr * hr - zi * hi, gr * hr + gi * hi)
            lhs_im[tile] = joined(zr * hi + zi * hr, gi * hr - gr * hi)
            total_re = add(total_re, gr * zr + gi * zi)
            total_im = add(total_im, gi * zr - gr * zi)
        return total_re, total_im

    for pair in range(PAIRS):
        a = multiply(2 * pair)
        if 2 * pair + 1 < HALF:
            b = multiply(2 * pair + 1)
        else:
            b = (jnp.zeros_like(a[0]),) * 2
        lhs_re[2 * HALF + pair] = joined(a[0], b[0])
        lhs_im[2 * HALF + pair] = joined(a[1], b[1])

    def returned(spec, lanes):
        turned = []
        for k, (real, imag) in enumerate(spec):
            c = inverse[0, k : k + 1, lanes]
            s = inverse[1, k : k + 1, lanes]
            if k in (0, HALF - 1):
                turned.append((real * c - imag * s, None))
            else:
                turned.append((real * c - imag * s, imag * c + real * s))
        return real_inverse(turned, RADIX)

    rate = rates[pl.ds(pl.multiple_of(first, OWN), OWN), :]
    steps = [jnp.exp(-rate * (COLS * n / LENGTH)) for n in range(RADIX // 2)]
    ahead = lax.broadcasted_iota(jnp.int32, (OWN, LANE), 1).astype(f32)

    def filter_out(chunk):
        lanes = slice(chunk * LANE, (chunk + 1) * LANE)
        spec = []
        for k in range(HALF):
            rows = slice(k % 2 * OWN, k % 2 * OWN + OWN)
            tile = 2 * HALF + k // 2
            spec.append((res_re[tile, rows, lanes], res_im[tile, rows, lanes]))
        fine = jnp.exp(-rate * ((ahead + chunk * LANE) / LENGTH))
        pieces = [y * (fine * steps[n]) for n, y in enumerate(returned(spec, lanes))]
        row = (CHUNKS + chunk) * TILE
        for j in range(BLOCKS):
            both = joined(pieces[2 * j], pieces[2 * j + 1])
            out[seat(j), row : row + TILE] = both
            out[seat(BLOCKS + j), row : row + TILE] = both

    def signals_out(s, chunk):
        lanes = slice(chunk * LANE, (chunk + 1) * LANE)
        halves = []
        for rows in (slice(0, OWN), slice(OWN, TILE)):
            spec = [
                (res_re[s * HALF + k, rows, lanes], res_im[s * HALF + k, rows, lanes])
                for k in range(HALF)
            ]
            halves.append(returned(spec, lanes))
        for n in range(RADIX // 2):
            row = (n % 2 * 2 + chunk) * TILE
            out[seat(s * BLOCKS + n // 2), row : row + TILE] = joined(halves[0][n], halves[1][n])

    back(rest)
    back(place(0))
    filter_out(0)
    filter_out(1)
    back(place(1))
    for s in range(2):
        signals_out(s, 0)
        signals_out(s, 1)


def spectral(got, decay, **kw):
    basis, forward, inverse = (in_vmem(jnp.asarray(table)) for table in tables())
    wide = pltpu.VMEM((ROWS, TILE, COLS), jnp.bfloat16)
    result = pltpu.VMEM((ROWS, TILE, COLS), jnp.float32)
    return pl.pallas_call(
        spectral_kernel,
        out_shape=pltpu.VMEM((GROUP, (CHUNKS + 2) * TILE, LANE), jnp.bfloat16),
        in_specs=[pl.BlockSpec(memory_space=pltpu.VMEM)] * 5,
        out_specs=pl.BlockSpec(memory_space=pltpu.VMEM),
        scratch_shapes=[wide, wide, result, result, pltpu.VMEM((CH, LANE), jnp.float32)],
        compiler_params=pltpu.CompilerParams(vmem_limit_bytes=VMEM_LIMIT),
        name="spectral",
        **kw,
    )(in_vmem(got), basis, forward, inverse, in_vmem(decay))


def parts_kernel(back, features, weight, sums):
    f32, bf16 = jnp.float32, jnp.bfloat16
    half = TOK // 2
    first = CHUNKS * TILE
    is_feature = lax.axis_index("dp") == 0
    alongs, weight_sum = [], None
    for h in range(2):
        pieces = []
        for c in range(2):
            piece = back[:, first + c * TILE : first + (c + 1) * TILE].astype(f32)[:, h * OWN : (h + 1) * OWN]
            pieces.append(piece.reshape(CH, LANE))
        kernel_grad = jnp.concatenate(pieces, axis=1).astype(bf16)
        alongs.append(jnp.dot(weight[...], kernel_grad, preferred_element_type=f32))
        share = lax.dot_general(
            features[:, half * h : half * (h + 1)],
            kernel_grad,
            (((1,), (1,)), ((), ())),
            preferred_element_type=f32,
        )
        weight_sum = add(weight_sum, share)
    blank = jnp.zeros((8, LANE), f32)
    for piece in range(16):
        r, c = piece // 4, piece % 4
        feature = alongs[c // 2][16 * r : 16 * (r + 1), LANE * (c % 2) : LANE * (c % 2 + 1)]
        r, c = piece // 2, piece % 2
        other = weight_sum[8 * r : 8 * (r + 1), LANE * c : LANE * (c + 1)]
        other = jnp.concatenate([other, blank], axis=0)
        sums[piece] = jnp.where(is_feature, feature, other).astype(bf16)


def parts(back, features, weight, **kw):
    return pl.pallas_call(
        parts_kernel,
        out_shape=pltpu.VMEM((16, TILE, LANE), jnp.bfloat16),
        in_specs=[pl.BlockSpec(memory_space=pltpu.VMEM)] * 3,
        out_specs=pl.BlockSpec(memory_space=pltpu.VMEM),
        compiler_params=pltpu.CompilerParams(vmem_limit_bytes=VMEM_LIMIT),
        name="parts",
        **kw,
    )(in_vmem(back), in_vmem(features), in_vmem(weight))


def assemble_kernel(own, other, feature_grad, weight_grad):
    f32 = jnp.float32
    is_feature = lax.axis_index("dp") == 0
    for piece in range(16):
        a = own[piece].astype(f32)
        b = other[piece].astype(f32)
        feature = jnp.where(is_feature, a, b)
        weight = jnp.where(is_feature, b, a)[:8]
        r, c = piece // 4, piece % 4
        feature_grad[16 * r : 16 * (r + 1), 128 * c : 128 * (c + 1)] = feature
        r, c = piece // 2, piece % 2
        weight_grad[8 * r : 8 * (r + 1), 128 * c : 128 * (c + 1)] = weight


def assemble(own, other, **kw):
    return pl.pallas_call(
        assemble_kernel,
        out_shape=(
            jax.ShapeDtypeStruct((ORDER, TOK), jnp.float32),
            jax.ShapeDtypeStruct((ORDER, CH), jnp.float32),
        ),
        in_specs=[pl.BlockSpec(memory_space=pltpu.VMEM)] * 2,
        out_specs=(pl.BlockSpec(memory_space=pltpu.VMEM),) * 2,
        name="assemble",
        **kw,
    )(in_vmem(own), in_vmem(other))


def final_kernel(
    back, values, gate_first, gate_second, grad, skip, output, values_grad, first_grad, second_grad
):
    f32, bf16 = jnp.float32, jnp.bfloat16
    eye = identity(LANE)
    bias = skip[...]
    for chunk in range(CHUNKS):
        both = back[:, chunk * TILE : (chunk + 1) * TILE].astype(f32)
        conv = turned_over(eye, both[:, :OWN].reshape(CH, LANE).astype(bf16))
        grad_conv = turned_over(eye, both[:, OWN:].reshape(CH, LANE).astype(bf16))
        rows = slice(chunk * LANE, (chunk + 1) * LANE)
        x = values[rows].astype(f32)
        g1 = gate_first[rows].astype(f32)
        g2 = gate_second[rows].astype(f32)
        dy = grad[rows].astype(f32)
        total = conv + bias * (x * g1).astype(bf16).astype(f32)
        output[rows] = (g2 * total).astype(bf16)
        second_grad[rows] = (dy * total).astype(bf16)
        delta = grad_conv + bias * (dy * g2).astype(bf16).astype(f32)
        values_grad[rows] = (delta * g1).astype(bf16)
        first_grad[rows] = (delta * x).astype(bf16)


def final(back, values, gate_first, gate_second, grad, skip, **kw):
    shape = jax.ShapeDtypeStruct((TOK, CH), jnp.bfloat16)
    return pl.pallas_call(
        final_kernel,
        out_shape=(shape,) * 4,
        in_specs=[pl.BlockSpec(memory_space=pltpu.VMEM)] * 6,
        out_specs=(pl.BlockSpec(memory_space=pltpu.VMEM),) * 4,
        compiler_params=pltpu.CompilerParams(vmem_limit_bytes=VMEM_LIMIT),
        name="final",
        **kw,
    )(*(in_vmem(a) for a in (back, values, gate_first, gate_second, grad, skip)))


def local(
    values,
    gate_first,
    gate_second,
    filter_features,
    filter_weight,
    decay_rate,
    skip_bias,
    output_grad,
):
    values, gate_first, gate_second, output_grad = (
        a[0] for a in (values, gate_first, gate_second, output_grad)
    )
    planes = [[256 * (seat(i) // 16) + 16 * z + seat(i) % 16 for i in range(GROUP)] for z in range(16)]

    def trade(array):
        return lax.all_to_all(
            array, ("dp", "chan", "ctx"), 0, 0, axis_index_groups=planes, tiled=True
        )

    decay = decay_rate[None, :]
    sent = spread(values, gate_first, gate_second, output_grad, filter_features, filter_weight, decay)
    got = trade(sent)
    back = trade(spectral(got, decay))
    everywhere = ("dp", "chan", "ctx")
    around = [(z + FIRST_CHAN) % 16 for z in range(16)]
    groups = [[16 * z + j for z in around] for j in range(16)]
    groups += [[256 + 16 * z + j for j in range(16)] for z in range(16)]

    def exchange(pieces):
        return lax.all_to_all(pieces, everywhere, 0, 0, axis_index_groups=groups, tiled=True)

    pieces = exchange(parts(back, filter_features, filter_weight))
    summed = jnp.sum(pieces.astype(jnp.float32), axis=0).astype(jnp.bfloat16)
    copies = exchange(jnp.broadcast_to(summed[None], (16, 16, 128)))
    back, copies = lax.optimization_barrier((back, copies))
    other = lax.ppermute(copies, "dp", [(0, 1), (1, 0)])
    outs = final(back, values, gate_first, gate_second, output_grad, skip_bias[None, :])
    feature_grad, weight_grad = assemble(copies, other)
    output, values_grad, first_grad, second_grad = (a[None] for a in outs)
    return (output, values_grad, first_grad, second_grad, weight_grad, feature_grad)


def solution(mesh):
    in_specs = (
        P("dp", "ctx", "chan"),
        P("dp", "ctx", "chan"),
        P("dp", "ctx", "chan"),
        P(None, "ctx"),
        P(None, "chan"),
        P("chan"),
        P("chan"),
        P("dp", "ctx", "chan"),
    )
    out_specs = (
        P("dp", "ctx", "chan"),
        P("dp", "ctx", "chan"),
        P("dp", "ctx", "chan"),
        P("dp", "ctx", "chan"),
        P(None, "chan"),
        P(None, "ctx"),
    )
    return jax.shard_map(local, mesh=mesh, in_specs=in_specs, out_specs=out_specs, check_vma=False)
```

```python
import functools
import math

import jax
import jax.numpy as jnp
import numpy as np
from jax import lax
from jax.experimental import pallas as pl
from jax.experimental.pallas import tpu as pltpu
from jax.sharding import PartitionSpec as P

LENGTH = 8192
PERIOD = 2 * LENGTH
TOK = 512
RADIX = 64
COLS = PERIOD // RADIX
BLOCKS = LENGTH // TOK
HALF = RADIX // 2 + 1
CH = 256
OWN = 8
GROUP = 32
ORDER = 64
TILE = 16
LANE = 128
CHUNKS = TOK // LANE
PAIRS = (HALF + 1) // 2
ROWS = 2 * HALF + PAIRS
QUAD = 4
CHAN_QUADS = ((2, 1, 0, 3), (6, 5, 4, 7), (9, 8, 10, 11), (13, 12, 14, 15))
QUAD_ORDER = (2, 3, 1, 0)
LEADER = 25
VMEM_LIMIT = 24 * 1024 * 1024


def seat(member):
    return {0: LEADER, LEADER: 0}.get(member, member)


def tables():
    grid = np.arange(COLS)
    angle = 2.0 * np.pi / COLS * (np.outer(grid, grid) % COLS)
    basis = np.concatenate([np.cos(angle), np.sin(angle)], axis=0).astype(jnp.bfloat16)
    turn = 2.0 * np.pi / PERIOD * np.outer(np.arange(HALF), grid)
    forward = np.stack([np.cos(turn), np.sin(turn)]).astype(np.float32)
    factor = 1.0 / (PERIOD * math.sqrt(LENGTH))
    inverse = (np.stack([np.cos(turn), np.sin(turn)]) * factor).astype(np.float32)
    return basis, forward, inverse


def add(a, b):
    if a is None:
        return b
    return a if b is None else a + b


def sub(a, b):
    if b is None:
        return a
    return -b if a is None else a - b


def neg(a):
    return None if a is None else -a


def rotate(value, index, period):
    real, imag = value
    if index == 0:
        return value
    if 4 * index == period:
        return imag, neg(real)
    c = math.cos(2 * math.pi * index / period)
    s = math.sin(2 * math.pi * index / period)
    if imag is None:
        return real * c, real * (-s)
    if 8 * index == period:
        return (real + imag) * c, (imag - real) * c
    return real * c + imag * s, imag * c - real * s


def rotate_back(value, index, period):
    real, imag = value
    if index == 0:
        return value
    if 4 * index == period:
        return neg(imag), real
    c = math.cos(2 * math.pi * index / period)
    s = math.sin(2 * math.pi * index / period)
    if 8 * index == period:
        return (real - imag) * c, (imag + real) * c
    return real * c - imag * s, imag * c + real * s


def real_dft(xs, n):
    if n == 2:
        return [(xs[0], None), (xs[0], None)]
    if n == 4:
        return [(xs[0] + xs[1], None), (xs[0], -xs[1]), (xs[0] - xs[1], None)]
    even = real_dft(xs[0::2], n // 2)
    odd = real_dft(xs[1::2], n // 2)
    out = [None] * (n // 2 + 1)
    for k in range(n // 4 + 1):
        t = rotate(odd[k], k, n)
        e = even[k]
        out[k] = (add(e[0], t[0]), add(e[1], t[1]))
        if 4 * k != n:
            out[n // 2 - k] = (sub(e[0], t[0]), sub(t[1], e[1]))
    return out


def real_inverse(spec, n):
    if n == 4:
        total = spec[0][0] + spec[2][0]
        diff = spec[0][0] - spec[2][0]
        return [total + 2.0 * spec[1][0], diff - 2.0 * spec[1][1]]
    even, odd = [], []
    for k in range(n // 4 + 1):
        a, b = spec[k], spec[n // 2 - k]
        if 4 * k == n:
            even.append((2.0 * a[0], None))
            odd.append((-2.0 * a[1], None))
            continue
        even.append((add(a[0], b[0]), sub(a[1], b[1])))
        odd.append(rotate_back((sub(a[0], b[0]), add(a[1], b[1])), k, n))
    first = real_inverse(even, n // 2)
    second = real_inverse(odd, n // 2)
    return [first[i // 2] if i % 2 == 0 else second[i // 2] for i in range(n // 2)]


def identity(size):
    row = lax.broadcasted_iota(jnp.int32, (size, size), 0)
    column = lax.broadcasted_iota(jnp.int32, (size, size), 1)
    return jnp.where(row == column, 1.0, 0.0).astype(jnp.bfloat16)


def turned_over(eye, block):
    return lax.dot_general(eye, block, (((1,), (1,)), ((), ())), preferred_element_type=jnp.float32)


def in_vmem(array):
    return pltpu.with_memory_space_constraint(array, pltpu.VMEM)


def in_hbm(array):
    return pltpu.with_memory_space_constraint(array, pltpu.HBM)


def spread_kernel(values, gate_first, gate_second, grad, features, weight, decay, ready):
    f32, bf16 = jnp.float32, jnp.bfloat16
    half = TOK // 2
    dp = lax.axis_index("dp")
    ctx = lax.axis_index("ctx")
    eye = identity(CH)
    mine = jnp.where(dp == 0, features[:, :half].astype(f32), features[:, half:].astype(f32))
    raw = lax.dot_general(
        mine.astype(bf16), weight[...], (((0,), (0,)), ((), ())), preferred_element_type=f32
    )
    first = ctx * TOK + dp * half
    positions = (first + lax.broadcasted_iota(jnp.int32, (half, 1), 0)).astype(f32) / LENGTH
    kernel = (raw * jnp.exp(-decay[...] * positions)).astype(bf16)
    kernel = turned_over(eye, kernel).reshape(GROUP, OWN, half)
    folded = jnp.concatenate([kernel[:, :, :LANE], kernel[:, :, LANE:]], axis=1)
    ready[:, CHUNKS * TILE :] = folded.astype(bf16)
    for part in range(2):
        rows = slice(part * half, (part + 1) * half)
        mixed = (values[rows].astype(f32) * gate_first[rows].astype(f32)).astype(bf16)
        scaled = (grad[rows].astype(f32) * gate_second[rows].astype(f32)).astype(bf16)
        mixed = turned_over(eye, mixed).reshape(GROUP, OWN, half)
        scaled = turned_over(eye, scaled).reshape(GROUP, OWN, half)
        both = jnp.concatenate([mixed, scaled], axis=1).astype(bf16)
        for c in range(2):
            row = (2 * part + c) * TILE
            ready[:, row : row + TILE] = both[:, :, c * LANE : (c + 1) * LANE]


def spread(values, gate_first, gate_second, grad, features, weight, decay, **kw):
    return pl.pallas_call(
        spread_kernel,
        out_shape=pltpu.VMEM((GROUP, (CHUNKS + 1) * TILE, LANE), jnp.bfloat16),
        in_specs=[pl.BlockSpec(memory_space=pltpu.VMEM)] * 7,
        out_specs=pl.BlockSpec(memory_space=pltpu.VMEM),
        compiler_params=pltpu.CompilerParams(vmem_limit_bytes=VMEM_LIMIT),
        name="spread",
        **kw,
    )(*(in_hbm(a) for a in (values, gate_first, gate_second, grad, features, weight, decay)))


def spectral_kernel(
    got, basis, forward, inverse, decay, out, lhs_re, lhs_im, res_re, res_im, rates
):
    f32, bf16 = jnp.float32, jnp.bfloat16
    rates[...] = jnp.broadcast_to(decay[...], (LANE, CH)).T
    member = lax.axis_index("dp") * BLOCKS + lax.axis_index("ctx")
    place_of = jnp.where(member == 0, LEADER, jnp.where(member == LEADER, 0, member))
    first = place_of * OWN

    def transformed(xs, lanes):
        turned = []
        for k, (real, imag) in enumerate(real_dft(xs, RADIX)):
            if k == 0:
                turned.append((real, jnp.zeros_like(real)))
                continue
            c = forward[0, k : k + 1, lanes]
            s = forward[1, k : k + 1, lanes]
            if imag is None:
                turned.append((real * c, -(real * s)))
            else:
                turned.append((real * c + imag * s, imag * c - real * s))
        return turned

    def joined(a, b):
        return jnp.concatenate([a, b], axis=0).astype(bf16)

    def place(s):
        return slice(s * HALF, (s + 1) * HALF)

    def signals_in(s, chunk):
        lanes = slice(chunk * LANE, (chunk + 1) * LANE)
        xs = [
            got[seat(s * BLOCKS + j), (2 * h + chunk) * TILE : (2 * h + chunk + 1) * TILE].astype(f32)
            for j in range(BLOCKS)
            for h in range(2)
        ]
        low = transformed([x[:OWN] for x in xs], lanes)
        high = transformed([x[OWN:] for x in xs], lanes)
        for k in range(HALF):
            lhs_re[s * HALF + k, :, lanes] = joined(low[k][0], high[k][0])
            lhs_im[s * HALF + k, :, lanes] = joined(low[k][1], high[k][1])

    def kernel_in(chunk):
        xs = [
            got[seat(s * BLOCKS + j), CHUNKS * TILE :].astype(f32)[chunk * OWN : (chunk + 1) * OWN]
            for j in range(BLOCKS)
            for s in range(2)
        ]
        lanes = slice(chunk * LANE, (chunk + 1) * LANE)
        spec = transformed(xs, lanes)
        spec.append((jnp.zeros_like(spec[0][0]),) * 2)
        for p in range(PAIRS):
            a, b = spec[2 * p], spec[2 * p + 1]
            lhs_re[2 * HALF + p, :, lanes] = joined(a[0], b[0])
            lhs_im[2 * HALF + p, :, lanes] = joined(a[1], b[1])

    def product(first, second):
        count = first.shape[0]
        lhs = jnp.concatenate([first, second], axis=2).reshape(count * TILE, 2 * COLS)
        res = jnp.dot(lhs, basis[...], preferred_element_type=f32)
        return res.reshape(count, TILE, COLS)

    def forth(tiles):
        real, imag = lhs_re[tiles], lhs_im[tiles]
        res_re[tiles] = product(real, imag)
        res_im[tiles] = product(imag, -real)

    def back(tiles):
        real, imag = lhs_re[tiles], lhs_im[tiles]
        res_re[tiles] = product(real, -imag)
        res_im[tiles] = product(imag, real)

    rest = slice(2 * HALF, ROWS)
    kernel_in(0)
    kernel_in(1)
    forth(rest)
    for s in range(2):
        signals_in(s, 0)
        signals_in(s, 1)
        forth(place(s))

    def multiply(k):
        pair, rows = k // 2, slice(k % 2 * OWN, k % 2 * OWN + OWN)
        hr = res_re[2 * HALF + pair, rows, :]
        hi = res_im[2 * HALF + pair, rows, :]
        total_re, total_im = None, None
        for s in range(2):
            tile = s * HALF + k
            zr = res_re[tile, :OWN, :]
            zi = res_im[tile, :OWN, :]
            gr = res_re[tile, OWN:, :]
            gi = res_im[tile, OWN:, :]
            lhs_re[tile] = joined(zr * hr - zi * hi, gr * hr + gi * hi)
            lhs_im[tile] = joined(zr * hi + zi * hr, gi * hr - gr * hi)
            total_re = add(total_re, gr * zr + gi * zi)
            total_im = add(total_im, gi * zr - gr * zi)
        return total_re, total_im

    for pair in range(PAIRS):
        a = multiply(2 * pair)
        if 2 * pair + 1 < HALF:
            b = multiply(2 * pair + 1)
        else:
            b = (jnp.zeros_like(a[0]),) * 2
        lhs_re[2 * HALF + pair] = joined(a[0], b[0])
        lhs_im[2 * HALF + pair] = joined(a[1], b[1])

    def returned(spec, lanes):
        turned = []
        for k, (real, imag) in enumerate(spec):
            c = inverse[0, k : k + 1, lanes]
            s = inverse[1, k : k + 1, lanes]
            if k in (0, HALF - 1):
                turned.append((real * c - imag * s, None))
            else:
                turned.append((real * c - imag * s, imag * c + real * s))
        return real_inverse(turned, RADIX)

    rate = rates[pl.ds(pl.multiple_of(first, OWN), OWN), :]
    steps = [jnp.exp(-rate * (COLS * n / LENGTH)) for n in range(RADIX // 2)]
    ahead = lax.broadcasted_iota(jnp.int32, (OWN, LANE), 1).astype(f32)

    def filter_out(chunk):
        lanes = slice(chunk * LANE, (chunk + 1) * LANE)
        spec = []
        for k in range(HALF):
            rows = slice(k % 2 * OWN, k % 2 * OWN + OWN)
            tile = 2 * HALF + k // 2
            spec.append((res_re[tile, rows, lanes], res_im[tile, rows, lanes]))
        fine = jnp.exp(-rate * ((ahead + chunk * LANE) / LENGTH))
        pieces = [y * (fine * steps[n]) for n, y in enumerate(returned(spec, lanes))]
        row = (CHUNKS + chunk) * TILE
        for j in range(BLOCKS):
            both = joined(pieces[2 * j], pieces[2 * j + 1])
            out[seat(j), row : row + TILE] = both
            out[seat(BLOCKS + j), row : row + TILE] = both

    def signals_out(s, chunk):
        lanes = slice(chunk * LANE, (chunk + 1) * LANE)
        halves = []
        for rows in (slice(0, OWN), slice(OWN, TILE)):
            spec = [
                (res_re[s * HALF + k, rows, lanes], res_im[s * HALF + k, rows, lanes])
                for k in range(HALF)
            ]
            halves.append(returned(spec, lanes))
        for n in range(RADIX // 2):
            row = (n % 2 * 2 + chunk) * TILE
            out[seat(s * BLOCKS + n // 2), row : row + TILE] = joined(halves[0][n], halves[1][n])

    back(rest)
    back(place(0))
    filter_out(0)
    filter_out(1)
    back(place(1))
    for s in range(2):
        signals_out(s, 0)
        signals_out(s, 1)


def spectral(got, decay, **kw):
    basis, forward, inverse = (in_vmem(jnp.asarray(table)) for table in tables())
    wide = pltpu.VMEM((ROWS, TILE, COLS), jnp.bfloat16)
    result = pltpu.VMEM((ROWS, TILE, COLS), jnp.float32)
    return pl.pallas_call(
        spectral_kernel,
        out_shape=pltpu.VMEM((GROUP, (CHUNKS + 2) * TILE, LANE), jnp.bfloat16),
        in_specs=[pl.BlockSpec(memory_space=pltpu.VMEM)] * 5,
        out_specs=pl.BlockSpec(memory_space=pltpu.VMEM),
        scratch_shapes=[wide, wide, result, result, pltpu.VMEM((CH, LANE), jnp.float32)],
        compiler_params=pltpu.CompilerParams(vmem_limit_bytes=VMEM_LIMIT),
        name="spectral",
        **kw,
    )(in_vmem(got), basis, forward, inverse, in_vmem(decay))


def parts_kernel(back, features, weight, sums):
    f32, bf16 = jnp.float32, jnp.bfloat16
    half = TOK // 2
    first = CHUNKS * TILE
    is_feature = lax.axis_index("dp") == 0
    alongs, weight_sum = [], None
    for h in range(2):
        pieces = []
        for c in range(2):
            piece = back[:, first + c * TILE : first + (c + 1) * TILE].astype(f32)[:, h * OWN : (h + 1) * OWN]
            pieces.append(piece.reshape(CH, LANE))
        kernel_grad = jnp.concatenate(pieces, axis=1).astype(bf16)
        alongs.append(jnp.dot(weight[...], kernel_grad, preferred_element_type=f32))
        share = lax.dot_general(
            features[:, half * h : half * (h + 1)],
            kernel_grad,
            (((1,), (1,)), ((), ())),
            preferred_element_type=f32,
        )
        weight_sum = add(weight_sum, share)
    blank = jnp.zeros((ORDER - 2 * TILE, LANE), f32)
    for piece in range(QUAD):
        c = piece % 2
        feature = alongs[piece // 2][:, LANE * c : LANE * (c + 1)]
        rows = weight_sum[TILE * piece : TILE * (piece + 1)]
        other = jnp.concatenate([rows[:, :LANE], rows[:, LANE:], blank], axis=0)
        sums[piece] = jnp.where(is_feature, feature, other).astype(bf16)


def parts(back, features, weight, **kw):
    return pl.pallas_call(
        parts_kernel,
        out_shape=pltpu.VMEM((QUAD, ORDER, LANE), jnp.bfloat16),
        in_specs=[pl.BlockSpec(memory_space=pltpu.VMEM)] * 3,
        out_specs=pl.BlockSpec(memory_space=pltpu.VMEM),
        compiler_params=pltpu.CompilerParams(vmem_limit_bytes=VMEM_LIMIT),
        name="parts",
        **kw,
    )(in_vmem(back), in_vmem(features), in_vmem(weight))


def assemble_kernel(own, other, feature_grad, weight_grad):
    f32 = jnp.float32
    is_feature = lax.axis_index("dp") == 0
    for piece in range(QUAD):
        a = own[piece].astype(f32)
        b = other[piece].astype(f32)
        feature_grad[:, LANE * piece : LANE * (piece + 1)] = jnp.where(is_feature, a, b)
        rows = jnp.where(is_feature, b, a)
        weight = jnp.concatenate([rows[:TILE], rows[TILE : 2 * TILE]], axis=1)
        weight_grad[TILE * piece : TILE * (piece + 1)] = weight


def assemble(own, other, **kw):
    return pl.pallas_call(
        assemble_kernel,
        out_shape=(
            jax.ShapeDtypeStruct((ORDER, TOK), jnp.float32),
            jax.ShapeDtypeStruct((ORDER, CH), jnp.float32),
        ),
        in_specs=[pl.BlockSpec(memory_space=pltpu.VMEM)] * 2,
        out_specs=(pl.BlockSpec(memory_space=pltpu.VMEM),) * 2,
        name="assemble",
        **kw,
    )(in_vmem(own), in_vmem(other))


def final_kernel(
    back, values, gate_first, gate_second, grad, skip, output, values_grad, first_grad, second_grad
):
    f32, bf16 = jnp.float32, jnp.bfloat16
    eye = identity(LANE)
    bias = skip[...]
    for chunk in range(CHUNKS):
        both = back[:, chunk * TILE : (chunk + 1) * TILE].astype(f32)
        conv = turned_over(eye, both[:, :OWN].reshape(CH, LANE).astype(bf16))
        grad_conv = turned_over(eye, both[:, OWN:].reshape(CH, LANE).astype(bf16))
        rows = slice(chunk * LANE, (chunk + 1) * LANE)
        x = values[rows].astype(f32)
        g1 = gate_first[rows].astype(f32)
        g2 = gate_second[rows].astype(f32)
        dy = grad[rows].astype(f32)
        total = conv + bias * (x * g1).astype(bf16).astype(f32)
        output[rows] = (g2 * total).astype(bf16)
        second_grad[rows] = (dy * total).astype(bf16)
        delta = grad_conv + bias * (dy * g2).astype(bf16).astype(f32)
        values_grad[rows] = (delta * g1).astype(bf16)
        first_grad[rows] = (delta * x).astype(bf16)


def final(back, values, gate_first, gate_second, grad, skip, **kw):
    shape = jax.ShapeDtypeStruct((TOK, CH), jnp.bfloat16)
    return pl.pallas_call(
        final_kernel,
        out_shape=(shape,) * 4,
        in_specs=[pl.BlockSpec(memory_space=pltpu.VMEM)] * 6,
        out_specs=(pl.BlockSpec(memory_space=pltpu.VMEM),) * 4,
        compiler_params=pltpu.CompilerParams(vmem_limit_bytes=VMEM_LIMIT),
        name="final",
        **kw,
    )(*(in_vmem(a) for a in (back, values, gate_first, gate_second, grad, skip)))


def reduction_groups():
    near, far = [], []
    for other in range(16):
        for quad in CHAN_QUADS:
            near.append([z * 16 + other for z in quad])
        for seat_in in range(QUAD):
            far.append([CHAN_QUADS[quad][seat_in] * 16 + other for quad in QUAD_ORDER])
    for other in range(16):
        for i in range(QUAD):
            near.append([256 + other * 16 + QUAD * i + k for k in range(QUAD)])
            far.append([256 + other * 16 + QUAD * k + i for k in range(QUAD)])
    return near, far


def exchange(pieces, groups):
    return lax.all_to_all(
        pieces, ("dp", "chan", "ctx"), 0, 0, axis_index_groups=groups, tiled=True
    )


def local(
    values,
    gate_first,
    gate_second,
    filter_features,
    filter_weight,
    decay_rate,
    skip_bias,
    output_grad,
):
    values, gate_first, gate_second, output_grad = (
        a[0] for a in (values, gate_first, gate_second, output_grad)
    )
    planes = [[256 * (seat(i) // 16) + 16 * z + seat(i) % 16 for i in range(GROUP)] for z in range(16)]

    def trade(array):
        return lax.all_to_all(
            array, ("dp", "chan", "ctx"), 0, 0, axis_index_groups=planes, tiled=True
        )

    decay = decay_rate[None, :]
    sent = spread(values, gate_first, gate_second, output_grad, filter_features, filter_weight, decay)
    got = trade(sent)
    back = trade(spectral(got, decay))
    near, far = reduction_groups()
    quads = (QUAD, ORDER, LANE)
    pieces = exchange(parts(back, filter_features, filter_weight), near)
    summed = jnp.sum(pieces.astype(jnp.float32), axis=0).astype(jnp.bfloat16)
    pieces = exchange(jnp.broadcast_to(summed[None], quads), far)
    summed = jnp.sum(pieces.astype(jnp.float32), axis=0).astype(jnp.bfloat16)
    copies = exchange(jnp.broadcast_to(summed[None], quads), near)
    back, copies = lax.optimization_barrier((back, copies))
    other = lax.ppermute(copies, "dp", [(0, 1), (1, 0)])
    outs = final(back, values, gate_first, gate_second, output_grad, skip_bias[None, :])
    feature_grad, weight_grad = assemble(copies, other)
    output, values_grad, first_grad, second_grad = (a[None] for a in outs)
    return (output, values_grad, first_grad, second_grad, weight_grad, feature_grad)


def solution(mesh):
    in_specs = (
        P("dp", "ctx", "chan"),
        P("dp", "ctx", "chan"),
        P("dp", "ctx", "chan"),
        P(None, "ctx"),
        P(None, "chan"),
        P("chan"),
        P("chan"),
        P("dp", "ctx", "chan"),
    )
    out_specs = (
        P("dp", "ctx", "chan"),
        P("dp", "ctx", "chan"),
        P("dp", "ctx", "chan"),
        P("dp", "ctx", "chan"),
        P(None, "chan"),
        P(None, "ctx"),
    )
    return jax.shard_map(local, mesh=mesh, in_specs=in_specs, out_specs=out_specs, check_vma=False)
```

```python
import functools
import math

import jax
import jax.numpy as jnp
import numpy as np
from jax import lax
from jax.experimental import pallas as pl
from jax.experimental.pallas import tpu as pltpu
from jax.sharding import PartitionSpec as P

LENGTH = 8192
PERIOD = 2 * LENGTH
TOK = 512
RADIX = 64
COLS = PERIOD // RADIX
BLOCKS = LENGTH // TOK
HALF = RADIX // 2 + 1
CH = 256
OWN = 8
GROUP = 32
ORDER = 64
TILE = 16
LANE = 128
CHUNKS = TOK // LANE
PAIRS = (HALF + 1) // 2
ROWS = 2 * HALF + PAIRS
QUAD = 4
CHAN_QUADS = ((3, 1, 0, 2), (6, 5, 4, 7), (9, 8, 10, 11), (13, 12, 14, 15))
QUAD_ORDER = (2, 3, 1, 0)
LEADER = 25
VMEM_LIMIT = 24 * 1024 * 1024


def seat(member):
    return (member - LEADER) % GROUP


def tables():
    grid = np.arange(COLS)
    angle = 2.0 * np.pi / COLS * (np.outer(grid, grid) % COLS)
    basis = np.concatenate([np.cos(angle), np.sin(angle)], axis=0).astype(jnp.bfloat16)
    turn = 2.0 * np.pi / PERIOD * np.outer(np.arange(HALF), grid)
    forward = np.stack([np.cos(turn), np.sin(turn)]).astype(np.float32)
    factor = 1.0 / (PERIOD * math.sqrt(LENGTH))
    inverse = (np.stack([np.cos(turn), np.sin(turn)]) * factor).astype(np.float32)
    return basis, forward, inverse


def add(a, b):
    if a is None:
        return b
    return a if b is None else a + b


def sub(a, b):
    if b is None:
        return a
    return -b if a is None else a - b


def neg(a):
    return None if a is None else -a


def rotate(value, index, period):
    real, imag = value
    if index == 0:
        return value
    if 4 * index == period:
        return imag, neg(real)
    c = math.cos(2 * math.pi * index / period)
    s = math.sin(2 * math.pi * index / period)
    if imag is None:
        return real * c, real * (-s)
    if 8 * index == period:
        return (real + imag) * c, (imag - real) * c
    return real * c + imag * s, imag * c - real * s


def rotate_back(value, index, period):
    real, imag = value
    if index == 0:
        return value
    if 4 * index == period:
        return neg(imag), real
    c = math.cos(2 * math.pi * index / period)
    s = math.sin(2 * math.pi * index / period)
    if 8 * index == period:
        return (real - imag) * c, (imag + real) * c
    return real * c - imag * s, imag * c + real * s


def real_dft(xs, n):
    if n == 2:
        return [(xs[0], None), (xs[0], None)]
    if n == 4:
        return [(xs[0] + xs[1], None), (xs[0], -xs[1]), (xs[0] - xs[1], None)]
    even = real_dft(xs[0::2], n // 2)
    odd = real_dft(xs[1::2], n // 2)
    out = [None] * (n // 2 + 1)
    for k in range(n // 4 + 1):
        t = rotate(odd[k], k, n)
        e = even[k]
        out[k] = (add(e[0], t[0]), add(e[1], t[1]))
        if 4 * k != n:
            out[n // 2 - k] = (sub(e[0], t[0]), sub(t[1], e[1]))
    return out


def real_inverse(spec, n):
    if n == 4:
        total = spec[0][0] + spec[2][0]
        diff = spec[0][0] - spec[2][0]
        return [total + 2.0 * spec[1][0], diff - 2.0 * spec[1][1]]
    even, odd = [], []
    for k in range(n // 4 + 1):
        a, b = spec[k], spec[n // 2 - k]
        if 4 * k == n:
            even.append((2.0 * a[0], None))
            odd.append((-2.0 * a[1], None))
            continue
        even.append((add(a[0], b[0]), sub(a[1], b[1])))
        odd.append(rotate_back((sub(a[0], b[0]), add(a[1], b[1])), k, n))
    first = real_inverse(even, n // 2)
    second = real_inverse(odd, n // 2)
    return [first[i // 2] if i % 2 == 0 else second[i // 2] for i in range(n // 2)]


def identity(size):
    row = lax.broadcasted_iota(jnp.int32, (size, size), 0)
    column = lax.broadcasted_iota(jnp.int32, (size, size), 1)
    return jnp.where(row == column, 1.0, 0.0).astype(jnp.bfloat16)


def turned_over(eye, block):
    return lax.dot_general(eye, block, (((1,), (1,)), ((), ())), preferred_element_type=jnp.float32)


def in_vmem(array):
    return pltpu.with_memory_space_constraint(array, pltpu.VMEM)


def in_hbm(array):
    return pltpu.with_memory_space_constraint(array, pltpu.HBM)


def spread_kernel(values, gate_first, gate_second, grad, features, weight, decay, ready):
    f32, bf16 = jnp.float32, jnp.bfloat16
    half = TOK // 2
    dp = lax.axis_index("dp")
    ctx = lax.axis_index("ctx")
    eye = identity(CH)
    mine = jnp.where(dp == 0, features[:, :half].astype(f32), features[:, half:].astype(f32))
    raw = lax.dot_general(
        mine.astype(bf16), weight[...], (((0,), (0,)), ((), ())), preferred_element_type=f32
    )
    first = ctx * TOK + dp * half
    positions = (first + lax.broadcasted_iota(jnp.int32, (half, 1), 0)).astype(f32) / LENGTH
    kernel = (raw * jnp.exp(-decay[...] * positions)).astype(bf16)
    kernel = turned_over(eye, kernel).reshape(GROUP, OWN, half)
    folded = jnp.concatenate([kernel[:, :, :LANE], kernel[:, :, LANE:]], axis=1)
    ready[:, CHUNKS * TILE :] = folded.astype(bf16)
    for part in range(2):
        rows = slice(part * half, (part + 1) * half)
        mixed = (values[rows].astype(f32) * gate_first[rows].astype(f32)).astype(bf16)
        scaled = (grad[rows].astype(f32) * gate_second[rows].astype(f32)).astype(bf16)
        mixed = turned_over(eye, mixed).reshape(GROUP, OWN, half)
        scaled = turned_over(eye, scaled).reshape(GROUP, OWN, half)
        both = jnp.concatenate([mixed, scaled], axis=1).astype(bf16)
        for c in range(2):
            row = (2 * part + c) * TILE
            ready[:, row : row + TILE] = both[:, :, c * LANE : (c + 1) * LANE]


def spread(values, gate_first, gate_second, grad, features, weight, decay, **kw):
    return pl.pallas_call(
        spread_kernel,
        out_shape=pltpu.VMEM((GROUP, (CHUNKS + 1) * TILE, LANE), jnp.bfloat16),
        in_specs=[pl.BlockSpec(memory_space=pltpu.VMEM)] * 7,
        out_specs=pl.BlockSpec(memory_space=pltpu.VMEM),
        compiler_params=pltpu.CompilerParams(vmem_limit_bytes=VMEM_LIMIT),
        name="spread",
        **kw,
    )(*(in_hbm(a) for a in (values, gate_first, gate_second, grad, features, weight, decay)))


def spectral_kernel(
    got, basis, forward, inverse, decay, out, lhs_re, lhs_im, res_re, res_im, rates
):
    f32, bf16 = jnp.float32, jnp.bfloat16
    rates[...] = jnp.broadcast_to(decay[...], (LANE, CH)).T
    member = lax.axis_index("dp") * BLOCKS + lax.axis_index("ctx")
    place_of = (member + (GROUP - LEADER)) % GROUP
    first = place_of * OWN

    def transformed(xs, lanes):
        turned = []
        for k, (real, imag) in enumerate(real_dft(xs, RADIX)):
            if k == 0:
                turned.append((real, jnp.zeros_like(real)))
                continue
            c = forward[0, k : k + 1, lanes]
            s = forward[1, k : k + 1, lanes]
            if imag is None:
                turned.append((real * c, -(real * s)))
            else:
                turned.append((real * c + imag * s, imag * c - real * s))
        return turned

    def joined(a, b):
        return jnp.concatenate([a, b], axis=0).astype(bf16)

    def place(s):
        return slice(s * HALF, (s + 1) * HALF)

    def signals_in(s, chunk):
        lanes = slice(chunk * LANE, (chunk + 1) * LANE)
        xs = [
            got[seat(s * BLOCKS + j), (2 * h + chunk) * TILE : (2 * h + chunk + 1) * TILE].astype(f32)
            for j in range(BLOCKS)
            for h in range(2)
        ]
        low = transformed([x[:OWN] for x in xs], lanes)
        high = transformed([x[OWN:] for x in xs], lanes)
        for k in range(HALF):
            lhs_re[s * HALF + k, :, lanes] = joined(low[k][0], high[k][0])
            lhs_im[s * HALF + k, :, lanes] = joined(low[k][1], high[k][1])

    def kernel_in(chunk):
        xs = [
            got[seat(s * BLOCKS + j), CHUNKS * TILE :].astype(f32)[chunk * OWN : (chunk + 1) * OWN]
            for j in range(BLOCKS)
            for s in range(2)
        ]
        lanes = slice(chunk * LANE, (chunk + 1) * LANE)
        spec = transformed(xs, lanes)
        spec.append((jnp.zeros_like(spec[0][0]),) * 2)
        for p in range(PAIRS):
            a, b = spec[2 * p], spec[2 * p + 1]
            lhs_re[2 * HALF + p, :, lanes] = joined(a[0], b[0])
            lhs_im[2 * HALF + p, :, lanes] = joined(a[1], b[1])

    def product(first, second):
        count = first.shape[0]
        lhs = jnp.concatenate([first, second], axis=2).reshape(count * TILE, 2 * COLS)
        res = jnp.dot(lhs, basis[...], preferred_element_type=f32)
        return res.reshape(count, TILE, COLS)

    def forth(tiles):
        real, imag = lhs_re[tiles], lhs_im[tiles]
        res_re[tiles] = product(real, imag)
        res_im[tiles] = product(imag, -real)

    def back(tiles):
        real, imag = lhs_re[tiles], lhs_im[tiles]
        res_re[tiles] = product(real, -imag)
        res_im[tiles] = product(imag, real)

    rest = slice(2 * HALF, ROWS)
    kernel_in(0)
    kernel_in(1)
    forth(rest)
    for s in range(2):
        signals_in(s, 0)
        signals_in(s, 1)
        forth(place(s))

    def multiply(k):
        pair, rows = k // 2, slice(k % 2 * OWN, k % 2 * OWN + OWN)
        hr = res_re[2 * HALF + pair, rows, :]
        hi = res_im[2 * HALF + pair, rows, :]
        total_re, total_im = None, None
        for s in range(2):
            tile = s * HALF + k
            zr = res_re[tile, :OWN, :]
            zi = res_im[tile, :OWN, :]
            gr = res_re[tile, OWN:, :]
            gi = res_im[tile, OWN:, :]
            lhs_re[tile] = joined(zr * hr - zi * hi, gr * hr + gi * hi)
            lhs_im[tile] = joined(zr * hi + zi * hr, gi * hr - gr * hi)
            total_re = add(total_re, gr * zr + gi * zi)
            total_im = add(total_im, gi * zr - gr * zi)
        return total_re, total_im

    for pair in range(PAIRS):
        a = multiply(2 * pair)
        if 2 * pair + 1 < HALF:
            b = multiply(2 * pair + 1)
        else:
            b = (jnp.zeros_like(a[0]),) * 2
        lhs_re[2 * HALF + pair] = joined(a[0], b[0])
        lhs_im[2 * HALF + pair] = joined(a[1], b[1])

    def returned(spec, lanes):
        turned = []
        for k, (real, imag) in enumerate(spec):
            c = inverse[0, k : k + 1, lanes]
            s = inverse[1, k : k + 1, lanes]
            if k in (0, HALF - 1):
                turned.append((real * c - imag * s, None))
            else:
                turned.append((real * c - imag * s, imag * c + real * s))
        return real_inverse(turned, RADIX)

    rate = rates[pl.ds(pl.multiple_of(first, OWN), OWN), :]
    steps = [jnp.exp(-rate * (COLS * n / LENGTH)) for n in range(RADIX // 2)]
    ahead = lax.broadcasted_iota(jnp.int32, (OWN, LANE), 1).astype(f32)

    def filter_out(chunk):
        lanes = slice(chunk * LANE, (chunk + 1) * LANE)
        spec = []
        for k in range(HALF):
            rows = slice(k % 2 * OWN, k % 2 * OWN + OWN)
            tile = 2 * HALF + k // 2
            spec.append((res_re[tile, rows, lanes], res_im[tile, rows, lanes]))
        fine = jnp.exp(-rate * ((ahead + chunk * LANE) / LENGTH))
        pieces = [y * (fine * steps[n]) for n, y in enumerate(returned(spec, lanes))]
        row = (CHUNKS + chunk) * TILE
        for j in range(BLOCKS):
            both = joined(pieces[2 * j], pieces[2 * j + 1])
            out[seat(j), row : row + TILE] = both
            out[seat(BLOCKS + j), row : row + TILE] = both

    def signals_out(s, chunk):
        lanes = slice(chunk * LANE, (chunk + 1) * LANE)
        halves = []
        for rows in (slice(0, OWN), slice(OWN, TILE)):
            spec = [
                (res_re[s * HALF + k, rows, lanes], res_im[s * HALF + k, rows, lanes])
                for k in range(HALF)
            ]
            halves.append(returned(spec, lanes))
        for n in range(RADIX // 2):
            row = (n % 2 * 2 + chunk) * TILE
            out[seat(s * BLOCKS + n // 2), row : row + TILE] = joined(halves[0][n], halves[1][n])

    back(rest)
    back(place(0))
    filter_out(0)
    filter_out(1)
    back(place(1))
    for s in range(2):
        signals_out(s, 0)
        signals_out(s, 1)


def spectral(got, decay, **kw):
    basis, forward, inverse = (in_vmem(jnp.asarray(table)) for table in tables())
    wide = pltpu.VMEM((ROWS, TILE, COLS), jnp.bfloat16)
    result = pltpu.VMEM((ROWS, TILE, COLS), jnp.float32)
    return pl.pallas_call(
        spectral_kernel,
        out_shape=pltpu.VMEM((GROUP, (CHUNKS + 2) * TILE, LANE), jnp.bfloat16),
        in_specs=[pl.BlockSpec(memory_space=pltpu.VMEM)] * 5,
        out_specs=pl.BlockSpec(memory_space=pltpu.VMEM),
        scratch_shapes=[wide, wide, result, result, pltpu.VMEM((CH, LANE), jnp.float32)],
        compiler_params=pltpu.CompilerParams(vmem_limit_bytes=VMEM_LIMIT),
        name="spectral",
        **kw,
    )(in_vmem(got), basis, forward, inverse, in_vmem(decay))


def parts_kernel(back, features, weight, sums):
    f32, bf16 = jnp.float32, jnp.bfloat16
    half = TOK // 2
    first = CHUNKS * TILE
    is_feature = lax.axis_index("dp") == 0
    alongs, weight_sum = [], None
    for h in range(2):
        pieces = []
        for c in range(2):
            piece = back[:, first + c * TILE : first + (c + 1) * TILE].astype(f32)[:, h * OWN : (h + 1) * OWN]
            pieces.append(piece.reshape(CH, LANE))
        kernel_grad = jnp.concatenate(pieces, axis=1).astype(bf16)
        alongs.append(jnp.dot(weight[...], kernel_grad, preferred_element_type=f32))
        share = lax.dot_general(
            features[:, half * h : half * (h + 1)],
            kernel_grad,
            (((1,), (1,)), ((), ())),
            preferred_element_type=f32,
        )
        weight_sum = add(weight_sum, share)
    blank = jnp.zeros((ORDER - 2 * TILE, LANE), f32)
    for piece in range(QUAD):
        c = piece % 2
        feature = alongs[piece // 2][:, LANE * c : LANE * (c + 1)]
        rows = weight_sum[TILE * piece : TILE * (piece + 1)]
        other = jnp.concatenate([rows[:, :LANE], rows[:, LANE:], blank], axis=0)
        sums[piece] = jnp.where(is_feature, feature, other).astype(bf16)


def parts(back, features, weight, **kw):
    return pl.pallas_call(
        parts_kernel,
        out_shape=pltpu.VMEM((QUAD, ORDER, LANE), jnp.bfloat16),
        in_specs=[pl.BlockSpec(memory_space=pltpu.VMEM)] * 3,
        out_specs=pl.BlockSpec(memory_space=pltpu.VMEM),
        compiler_params=pltpu.CompilerParams(vmem_limit_bytes=VMEM_LIMIT),
        name="parts",
        **kw,
    )(in_vmem(back), in_vmem(features), in_vmem(weight))


def assemble_kernel(own, other, feature_grad, weight_grad):
    f32 = jnp.float32
    is_feature = lax.axis_index("dp") == 0
    for piece in range(QUAD):
        a = own[piece].astype(f32)
        b = other[piece].astype(f32)
        feature_grad[:, LANE * piece : LANE * (piece + 1)] = jnp.where(is_feature, a, b)
        rows = jnp.where(is_feature, b, a)
        weight = jnp.concatenate([rows[:TILE], rows[TILE : 2 * TILE]], axis=1)
        weight_grad[TILE * piece : TILE * (piece + 1)] = weight


def assemble(own, other, **kw):
    return pl.pallas_call(
        assemble_kernel,
        out_shape=(
            jax.ShapeDtypeStruct((ORDER, TOK), jnp.float32),
            jax.ShapeDtypeStruct((ORDER, CH), jnp.float32),
        ),
        in_specs=[pl.BlockSpec(memory_space=pltpu.VMEM)] * 2,
        out_specs=(pl.BlockSpec(memory_space=pltpu.VMEM),) * 2,
        name="assemble",
        **kw,
    )(in_vmem(own), in_vmem(other))


def final_kernel(
    back, values, gate_first, gate_second, grad, skip, output, values_grad, first_grad, second_grad
):
    f32, bf16 = jnp.float32, jnp.bfloat16
    eye = identity(LANE)
    bias = skip[...]
    for chunk in range(CHUNKS):
        both = back[:, chunk * TILE : (chunk + 1) * TILE].astype(f32)
        conv = turned_over(eye, both[:, :OWN].reshape(CH, LANE).astype(bf16))
        grad_conv = turned_over(eye, both[:, OWN:].reshape(CH, LANE).astype(bf16))
        rows = slice(chunk * LANE, (chunk + 1) * LANE)
        x = values[rows].astype(f32)
        g1 = gate_first[rows].astype(f32)
        g2 = gate_second[rows].astype(f32)
        dy = grad[rows].astype(f32)
        total = conv + bias * (x * g1).astype(bf16).astype(f32)
        output[rows] = (g2 * total).astype(bf16)
        second_grad[rows] = (dy * total).astype(bf16)
        delta = grad_conv + bias * (dy * g2).astype(bf16).astype(f32)
        values_grad[rows] = (delta * g1).astype(bf16)
        first_grad[rows] = (delta * x).astype(bf16)


def final(back, values, gate_first, gate_second, grad, skip, **kw):
    shape = jax.ShapeDtypeStruct((TOK, CH), jnp.bfloat16)
    return pl.pallas_call(
        final_kernel,
        out_shape=(shape,) * 4,
        in_specs=[pl.BlockSpec(memory_space=pltpu.VMEM)] * 6,
        out_specs=(pl.BlockSpec(memory_space=pltpu.VMEM),) * 4,
        compiler_params=pltpu.CompilerParams(vmem_limit_bytes=VMEM_LIMIT),
        name="final",
        **kw,
    )(*(in_vmem(a) for a in (back, values, gate_first, gate_second, grad, skip)))


def reduction_groups():
    near, far = [], []
    for other in range(16):
        for quad in CHAN_QUADS:
            near.append([z * 16 + other for z in quad])
        for seat_in in range(QUAD):
            far.append([CHAN_QUADS[quad][seat_in] * 16 + other for quad in QUAD_ORDER])
    for other in range(16):
        for i in range(QUAD):
            near.append([256 + other * 16 + QUAD * i + k for k in range(QUAD)])
            far.append([256 + other * 16 + QUAD * k + i for k in range(QUAD)])
    return near, far


def exchange(pieces, groups):
    return lax.all_to_all(
        pieces, ("dp", "chan", "ctx"), 0, 0, axis_index_groups=groups, tiled=True
    )


def local(
    values,
    gate_first,
    gate_second,
    filter_features,
    filter_weight,
    decay_rate,
    skip_bias,
    output_grad,
):
    values, gate_first, gate_second, output_grad = (
        a[0] for a in (values, gate_first, gate_second, output_grad)
    )
    members = [(LEADER + i) % GROUP for i in range(GROUP)]
    planes = [[256 * (i // 16) + 16 * z + i % 16 for i in members] for z in range(16)]

    def trade(array):
        return lax.all_to_all(
            array, ("dp", "chan", "ctx"), 0, 0, axis_index_groups=planes, tiled=True
        )

    decay = decay_rate[None, :]
    sent = spread(values, gate_first, gate_second, output_grad, filter_features, filter_weight, decay)
    got = trade(sent)
    back = trade(spectral(got, decay))
    near, far = reduction_groups()
    quads = (QUAD, ORDER, LANE)
    pieces = exchange(parts(back, filter_features, filter_weight), near)
    summed = jnp.sum(pieces.astype(jnp.float32), axis=0).astype(jnp.bfloat16)
    pieces = exchange(jnp.broadcast_to(summed[None], quads), far)
    summed = jnp.sum(pieces.astype(jnp.float32), axis=0).astype(jnp.bfloat16)
    copies = exchange(jnp.broadcast_to(summed[None], quads), near)
    back, copies = lax.optimization_barrier((back, copies))
    other = lax.ppermute(copies, "dp", [(0, 1), (1, 0)])
    outs = final(back, values, gate_first, gate_second, output_grad, skip_bias[None, :])
    feature_grad, weight_grad = assemble(copies, other)
    output, values_grad, first_grad, second_grad = (a[None] for a in outs)
    return (output, values_grad, first_grad, second_grad, weight_grad, feature_grad)


def solution(mesh):
    in_specs = (
        P("dp", "ctx", "chan"),
        P("dp", "ctx", "chan"),
        P("dp", "ctx", "chan"),
        P(None, "ctx"),
        P(None, "chan"),
        P("chan"),
        P("chan"),
        P("dp", "ctx", "chan"),
    )
    out_specs = (
        P("dp", "ctx", "chan"),
        P("dp", "ctx", "chan"),
        P("dp", "ctx", "chan"),
        P("dp", "ctx", "chan"),
        P(None, "chan"),
        P(None, "ctx"),
    )
    return jax.shard_map(local, mesh=mesh, in_specs=in_specs, out_specs=out_specs, check_vma=False)
```
